32 devices in a mesh: dp: 4 (over y, core), ctx: 4 (over z), tensor: 2 (over x).
Axes of the slice: x: 2, y: 2, z: 4, core: 2. Of those that a mesh axis runs over, the one named last changes fastest.
Arguments:
- tokens: bfloat16 [4, 4096, 512], P('dp', 'ctx'), may hold values from -6 to 6
- positions: int32 [4, 4096], P('dp', 'ctx'), may hold values from 0 to 4095, as said below
- norm_before: bfloat16 [512], replicated, may hold values from 0.099609375 to 1.8984375
- query_weight: bfloat16 [512, 512], P(None, 'tensor'), may hold values from -0.25 to 0.25
- key_weight: bfloat16 [512, 512], P(None, 'tensor'), may hold values from -0.25 to 0.25
- value_weight: bfloat16 [512, 512], P(None, 'tensor'), may hold values from -0.25 to 0.25
- output_weight: bfloat16 [512, 512], P('tensor'), may hold values from -6 to 6
- norm_middle: bfloat16 [512], replicated, may hold values from 0.099609375 to 1.8984375
- gate_weight: bfloat16 [512, 1376], P(None, 'tensor'), may hold values from -0.25 to 0.25
- up_weight: bfloat16 [512, 1376], P(None, 'tensor'), may hold values from -0.25 to 0.25
- down_weight: bfloat16 [1376, 512], P('tensor'), may hold values from -0.15625 to 0.15625
- cotangent: bfloat16 [4, 4096, 512], P('dp', 'ctx'), may hold values from -6 to 6
Outputs:
- block_output: bfloat16 [4, 4096, 512], P('dp', 'ctx')
- grad_tokens: float32 [4, 4096, 512], P('dp', 'ctx')
- grad_before: float32 [512], replicated
- grad_query: float32 [512, 512], P(None, 'tensor')
- grad_key: float32 [512, 512], P(None, 'tensor')
- grad_value: float32 [512, 512], P(None, 'tensor')
- grad_output: float32 [512, 512], P('tensor')
- grad_middle: float32 [512], replicated
- grad_gate: float32 [512, 1376], P(None, 'tensor')
- grad_up: float32 [512, 1376], P(None, 'tensor')
- grad_down: float32 [1376, 512], P('tensor')
The draws below stay inside these ranges and needn't reach their ends.
Inputs may be any that keep to these rules, and one draw needn't show every extreme that they name: Each row is a permutation of 0 to 4095. In each sequence either slot j holds position j, or for every k the 1024 slots from k * 1024 on hold, in increasing order, positions k * 512 to (k + 1) * 512 - 1 and then 4096 - (k + 1) * 512 to 4096 - k * 512 - 1; which of the two is drawn for each sequence.
All inputs are finite; a program needn't handle non-finite values.
Results may differ from the reference program's by a relative error of at most 0.02.
Values may be sent and summed in bfloat16 or wider, within the bound.
No kernel may reach another device: no remote copies, remote signals or barrier semaphores. Data moves between devices by JAX's collectives and lax.ppermute only.
A program may use at most 128 MiB of HBM per device.

```python
import math
import jax
import jax.numpy as jnp
from jax import lax

D = 512
HEADS = 8
HEAD = 64
FF = 1376
LENGTH = 4096
TOK_BLK = 1024
SEQS = 4


def draw_positions(key, part):
    key = jax.random.fold_in(key, 7)
    slot_index = jnp.arange(LENGTH, dtype=jnp.int32)
    half_block = TOK_BLK // 2
    owner_block = slot_index // TOK_BLK
    within = slot_index % TOK_BLK
    folded_order = jnp.where(within < half_block, owner_block * half_block + within, LENGTH - (owner_block + 1) * half_block + within - half_block)
    ordering = jax.random.randint(key, (SEQS, 1), 0, 2)
    return jnp.where(ordering == 1, folded_order[None, :], slot_index[None, :]).astype(jnp.int32)


def block_levels(rng, shape, cuts, low, largest):
    loudness, own = 1.0, jax.random.fold_in(rng, 6)
    for axis_at, blocks in cuts:
        draws = jnp.exp(jax.random.uniform(jax.random.fold_in(own, axis_at), (blocks,), jnp.float32, low / len(cuts), largest / len(cuts)))
        loudness = loudness * jnp.repeat(draws, shape[axis_at] // blocks).reshape([-1 if axis == axis_at else 1 for axis in range(len(shape))])
    return loudness


def noise(key, extent, spread, limit, shards=(), held_as=jnp.bfloat16):
    result = spread * jax.random.normal(key, extent, jnp.float32)
    if shards:
        result = result * block_levels(key, extent, shards, -0.22, 0.18)
    return jnp.clip(result, -limit, limit).astype(held_as)


def setup_inputs(seed: int = 0) -> dict:
    seeds = jax.random.split(jax.random.key(seed), 13)
    return {
        "tokens": noise(seeds[0], (SEQS, LENGTH, D), 1.0, 6.0, ((0, 4), (1, 4))),
        "positions": draw_positions(jax.random.fold_in(seeds[12], 71), 0),
        "norm_before": jnp.clip(1.0 + 0.18 * jax.random.normal(seeds[2], (D,), jnp.float32), 0.099609375, 1.8984375).astype(jnp.bfloat16),
        "query_weight": noise(seeds[3], (D, HEADS * HEAD), D ** -0.5, 0.25, ((1, 2),)),
        "key_weight": noise(seeds[4], (D, HEADS * HEAD), D ** -0.5, 0.25, ((1, 2),)),
        "value_weight": noise(seeds[5], (D, HEADS * HEAD), D ** -0.5, 0.25, ((1, 2),)),
        "output_weight": noise(seeds[6], (HEADS * HEAD, D), 1 ** -0.5, 6.0, ((0, 2),)),
        "norm_middle": jnp.clip(1.0 + 0.18 * jax.random.normal(seeds[7], (D,), jnp.float32), 0.099609375, 1.8984375).astype(jnp.bfloat16),
        "gate_weight": noise(seeds[8], (D, FF), D ** -0.5, 0.25, ((1, 2),)),
        "up_weight": noise(seeds[9], (D, FF), D ** -0.5, 0.25, ((1, 2),)),
        "down_weight": noise(seeds[10], (FF, D), FF ** -0.5, 0.15625, ((0, 2),)),
        "cotangent": noise(seeds[11], (SEQS, LENGTH, D), 1.0, 6.0, ((0, 4), (1, 4))),
    }


epsilon = 1e-05
rope_base = 10000.0
masked_score = -1e+30

@jax.custom_vjp
def low(v):
    return lax.optimization_barrier(v.astype(jnp.bfloat16)).astype(jnp.float32)

@jax.custom_vjp
def low_back(v):
    return v

def low_keep(v):
    return (low(v), None)

def low_pass(kept, grad):
    return (grad,)

def back_keep(v):
    return (v, None)

def back_low(kept, grad):
    return (low(grad),)
low.defvjp(low_keep, low_pass)
low_back.defvjp(back_keep, back_low)

def rope_tables(positions):
    frequency = rope_base ** (-jnp.arange(HEAD // 2).astype(jnp.float32) * 2.0 / HEAD)
    angles = positions.astype(jnp.float32)[..., None] * frequency
    return (jnp.cos(angles), jnp.sin(angles))

def rotate(matrix, cosine_table, sine_table):
    shaped = matrix.reshape(matrix.shape[:-1] + (-1, HEAD))
    front_half = shaped[..., :HEAD // 2]
    back_half = shaped[..., HEAD // 2:]
    cosine = cosine_table[..., None, :]
    sine_part = sine_table[..., None, :]
    turned = jnp.concatenate([front_half * cosine - back_half * sine_part, back_half * cosine + front_half * sine_part], axis=-1)
    return turned.reshape(matrix.shape)

def normalize(token_rows, gain_row):
    return token_rows * lax.rsqrt(lax.optimization_barrier(jnp.mean(token_rows * token_rows, axis=-1, keepdims=True)) + epsilon) * gain_row

def product(left, right):
    return jnp.dot(left, right, precision=lax.Precision.HIGHEST, preferred_element_type=jnp.float32)

def attend(queries, key_rows, value_rows, positions):
    block_width = math.gcd(LENGTH, 512)
    block_count = LENGTH // block_width
    query_blocks = queries.reshape(block_count, block_width, HEADS, HEAD)
    place_blocks = positions.reshape(block_count, block_width)
    key_heads = key_rows.reshape(LENGTH, HEADS, HEAD)
    value_heads = value_rows.reshape(LENGTH, HEADS, HEAD)

    def one_block(block_in):
        query_part, query_pos = block_in
        scores = jnp.einsum('qhe,khe->hqk', query_part, key_heads, precision=lax.Precision.HIGHEST) * HEAD ** (-0.5)
        scores = low_back(scores)
        allowed = positions[None, None, :] <= query_pos[None, :, None]
        scores = jnp.where(allowed, scores, masked_score)
        shifted = jnp.exp(scores - lax.optimization_barrier(jnp.max(scores, axis=-1, keepdims=True)))
        weights = shifted / lax.optimization_barrier(jnp.sum(shifted, axis=-1, keepdims=True))
        mixed = jnp.einsum('hqk,khe->qhe', low(weights), value_heads, precision=lax.Precision.HIGHEST)
        return mixed.reshape(block_width, HEADS * HEAD)
    return lax.map(jax.checkpoint(one_block), (query_blocks, place_blocks)).reshape(LENGTH, HEADS * HEAD)

def forward(token_rows, places, weights):
    gain_first, query_weight, key_weight, value_weight, output_weight, gain_second, gate_weight, up_weight, down_weight = weights
    cosine_table, sine_table = rope_tables(places)
    normed_first = low(normalize(token_rows, gain_first))
    queries = low(rotate(low_back(product(normed_first, query_weight)), cosine_table, sine_table))
    key_rows = low(rotate(low_back(product(normed_first, key_weight)), cosine_table, sine_table))
    value_rows = low(low_back(product(normed_first, value_weight)))
    mixed = low(low_back(attend(queries, key_rows, value_rows, places)))
    hidden = token_rows + low_back(product(mixed, output_weight))
    normed_second = low(normalize(hidden, gain_second))
    gate_rows = low_back(product(normed_second, gate_weight))
    upward = low_back(product(normed_second, up_weight))
    activated = low(gate_rows * jax.nn.sigmoid(gate_rows) * upward)
    return hidden + low_back(product(activated, down_weight))

def reference(tokens, positions, norm_before, query_weight, key_weight, value_weight, output_weight, norm_middle, gate_weight, up_weight, down_weight, cotangent):
    weights = tuple((member.astype(jnp.float32) for member in (norm_before, query_weight, key_weight, value_weight, output_weight, norm_middle, gate_weight, up_weight, down_weight)))

    def one_sequence(totals, sequence_in):
        token_rows, places, tangent = sequence_in

        def apply(rows_in, weights_in):
            return forward(rows_in, places, weights_in)
        outputs, pull_back = jax.vjp(apply, token_rows.astype(jnp.float32), weights)
        grad_rows, grad_weights = pull_back(tangent.astype(jnp.float32))
        totals = tuple((total_old + member for total_old, member in zip(totals, grad_weights)))
        return (totals, (outputs.astype(jnp.bfloat16), grad_rows))
    start_totals = tuple((jnp.zeros(member.shape, jnp.float32) for member in weights))
    totals, (block_output, grad_tokens) = lax.scan(one_sequence, start_totals, (tokens, positions, cotangent))
    return (block_output, grad_tokens, totals[0], totals[1], totals[2], totals[3], totals[4], totals[5], totals[6], totals[7], totals[8])
```

```python
import functools
import math

import jax
import jax.numpy as jnp
from jax import lax
from jax.experimental import pallas as pl
from jax.experimental.pallas import tpu as pltpu
from jax.sharding import PartitionSpec as P

HEAD = 64


epsilon = 1e-05
rope_base = 10000.0
masked_score = -1e30


def rope_tables(positions):
    frequency = rope_base ** (-jnp.arange(HEAD // 2).astype(jnp.float32) * 2.0 / HEAD)
    angles = positions.astype(jnp.float32)[..., None] * frequency
    return (jnp.cos(angles), jnp.sin(angles))


def rotate(matrix, cosine_table, sine_table):
    shaped = matrix.reshape(matrix.shape[:-1] + (-1, HEAD))
    front_half = shaped[..., : HEAD // 2]
    back_half = shaped[..., HEAD // 2 :]
    cosine = cosine_table[..., None, :]
    sine_part = sine_table[..., None, :]
    turned = jnp.concatenate(
        [front_half * cosine - back_half * sine_part, back_half * cosine + front_half * sine_part],
        axis=-1,
    )
    return turned.reshape(matrix.shape)


def normalize(token_rows, gain_row):
    inverse_rms = lax.rsqrt(jnp.mean(token_rows * token_rows, axis=-1, keepdims=True) + epsilon)
    return (token_rows * inverse_rms * gain_row, inverse_rms)


def norm_back(token_rows, inverse_rms, gain_row, grad_normed):
    weighted = grad_normed * gain_row
    inner_sum = jnp.mean(weighted * token_rows, axis=-1, keepdims=True)
    grad_rows = (
        inverse_rms * weighted - token_rows * (inverse_rms * inverse_rms * inverse_rms) * inner_sum
    )
    grad_gain = jnp.sum(grad_normed * token_rows * inverse_rms, axis=(0, 1))
    return (grad_rows, grad_gain)


def project(left, weight):
    return jnp.einsum("sbd,dh->sbh", left, weight, preferred_element_type=jnp.float32)


def project_back(grad_rows, weight):
    return jnp.einsum("sbh,dh->sbd", grad_rows, weight, preferred_element_type=jnp.float32)


def outer_sum(left, right):
    return jnp.einsum("sbd,sbh->dh", left, right, preferred_element_type=jnp.float32)


def as_heads(matrix):
    return matrix.reshape(matrix.shape[:2] + (-1, HEAD))


def split_blocks(matrix, block_width):
    block_count = matrix.shape[1] // block_width
    shaped = matrix.reshape(matrix.shape[:1] + (block_count, block_width) + matrix.shape[2:])
    return jnp.moveaxis(shaped, 1, 0)


def join_blocks(stacked):
    joined = jnp.moveaxis(stacked, 0, 1)
    return joined.reshape((joined.shape[0], joined.shape[1] * joined.shape[2]) + joined.shape[3:])


def forward_fold(query_heads, query_pos, scale_factor, fold_state, incoming):
    key_part, value_part, key_pos = incoming
    block_width = math.gcd(key_part.shape[1], 512)
    blocks = (
        split_blocks(as_heads(key_part), block_width),
        split_blocks(as_heads(value_part), block_width),
        split_blocks(key_pos, block_width),
    )

    def forward_step_block(block_state, block_in):
        key_heads, value_heads, block_pos = block_in
        allowed = block_pos[:, None, None, :] <= query_pos[:, None, :, None]
        old_max, old_total, old_accum = block_state
        scores = (
            jnp.einsum(
                "sqhe,skhe->shqk", query_heads, key_heads, preferred_element_type=jnp.float32
            )
            * scale_factor
        )
        scores = jnp.where(allowed, scores, masked_score)
        new_max = jnp.maximum(old_max, jnp.max(scores, axis=-1))
        weights = jnp.where(allowed, jnp.exp(scores - new_max[..., None]), 0.0)
        factor = jnp.exp(old_max - new_max)
        new_total = old_total * factor + jnp.sum(weights, axis=-1)
        new_accum = old_accum * factor[..., None] + jnp.einsum(
            "shqk,skhe->shqe",
            weights.astype(jnp.bfloat16),
            value_heads,
            preferred_element_type=jnp.float32,
        )
        return ((new_max, new_total, new_accum), None)

    final_state, unused = lax.scan(forward_step_block, fold_state, blocks)
    return final_state


def gradient_fold(
    query_heads, query_pos, grad_heads, log_total, delta_heads, scale_factor, fold_state, incoming
):
    key_part, value_part, key_pos = incoming
    row_count = key_part.shape[1]
    block_width = math.gcd(row_count, 512)
    blocks = (
        split_blocks(as_heads(key_part), block_width),
        split_blocks(as_heads(value_part), block_width),
        split_blocks(key_pos, block_width),
    )

    def gradient_step_block(query_state, block_in):
        key_heads, value_heads, block_pos = block_in
        allowed = block_pos[:, None, None, :] <= query_pos[:, None, :, None]
        scores = (
            jnp.einsum(
                "sqhe,skhe->shqk", query_heads, key_heads, preferred_element_type=jnp.float32
            )
            * scale_factor
        )
        weights = jnp.where(allowed, jnp.exp(scores - log_total[..., None]), 0.0)
        grad_weights = jnp.einsum(
            "sqhe,skhe->shqk", grad_heads, value_heads, preferred_element_type=jnp.float32
        )
        grad_scores = (weights * (grad_weights - delta_heads[..., None])).astype(jnp.bfloat16)
        new_query = query_state + jnp.einsum(
            "shqk,skhe->shqe", grad_scores, key_heads, preferred_element_type=jnp.float32
        )
        key_grad = jnp.einsum(
            "shqk,sqhe->skhe", grad_scores, query_heads, preferred_element_type=jnp.float32
        )
        value_grad = jnp.einsum(
            "shqk,sqhe->skhe",
            weights.astype(jnp.bfloat16),
            grad_heads,
            preferred_element_type=jnp.float32,
        )
        return (new_query, (key_grad, value_grad))

    query_state, key_total, value_total = fold_state
    query_state, outputs = lax.scan(gradient_step_block, query_state, blocks)
    key_rows = join_blocks(outputs[0])
    value_rows = join_blocks(outputs[1])
    key_total = key_rows
    value_total = value_rows
    return (query_state, key_total, value_total)


def shards(
    tokens,
    positions,
    norm_before,
    query_weight,
    key_weight,
    value_weight,
    output_weight,
    norm_middle,
    gate_weight,
    up_weight,
    down_weight,
    cotangent,
):
    sequences = tokens.shape[0]
    block_rows = tokens.shape[1]
    local_heads = query_weight.shape[1] // HEAD
    scale_factor = HEAD ** (-0.5)
    cosine_table, sine_table = rope_tables(positions)
    token_rows = tokens.astype(jnp.float32)
    gain_first = norm_before.astype(jnp.float32)
    gain_second = norm_middle.astype(jnp.float32)
    normed_first, inverse_first = normalize(token_rows, gain_first)
    normed_first = normed_first.astype(jnp.bfloat16)
    query_rot = rotate(project(normed_first, query_weight), cosine_table, sine_table).astype(
        jnp.bfloat16
    )
    key_rot = rotate(project(normed_first, key_weight), cosine_table, sine_table).astype(
        jnp.bfloat16
    )
    value_rows = project(normed_first, value_weight).astype(jnp.bfloat16)
    query_heads = as_heads(query_rot)
    head_shape = (sequences, local_heads, block_rows)
    start_state = (
        jnp.full(head_shape, masked_score, jnp.float32),
        jnp.zeros(head_shape, jnp.float32),
        jnp.zeros(head_shape + (HEAD,), jnp.float32),
    )
    row_max, row_total, accum_heads = forward_fold(
        query_heads,
        positions,
        scale_factor,
        start_state,
        (
            lax.all_gather(key_rot, "ctx", axis=1, tiled=True),
            lax.all_gather(value_rows, "ctx", axis=1, tiled=True),
            lax.all_gather(positions, "ctx", axis=1, tiled=True),
        ),
    )
    log_total = row_max + jnp.log(row_total)
    mixed_heads = jnp.swapaxes(accum_heads / row_total[..., None], 1, 2)
    mixed_rows = mixed_heads.reshape(sequences, block_rows, -1).astype(jnp.bfloat16)
    hidden = token_rows + lax.psum(
        project(mixed_rows, output_weight).astype(jnp.bfloat16), "tensor"
    ).astype(jnp.float32)
    normed_second, inverse_second = normalize(hidden, gain_second)
    normed_second = normed_second.astype(jnp.bfloat16)
    gate_rows = project(normed_second, gate_weight)
    upward = project(normed_second, up_weight)
    sigmoid_gate = jax.nn.sigmoid(gate_rows)
    silu_gate = gate_rows * sigmoid_gate
    activated = (silu_gate * upward).astype(jnp.bfloat16)
    block_output = (
        hidden
        + lax.psum(project(activated, down_weight).astype(jnp.bfloat16), "tensor").astype(
            jnp.float32
        )
    ).astype(jnp.bfloat16)
    grad_down = outer_sum(activated, cotangent)
    grad_act = project_back(cotangent, down_weight)
    grad_gate_rows = (
        grad_act * upward * sigmoid_gate * (1.0 + gate_rows * (1.0 - sigmoid_gate))
    ).astype(jnp.bfloat16)
    grad_up_rows = (grad_act * silu_gate).astype(jnp.bfloat16)
    grad_gate = outer_sum(normed_second, grad_gate_rows)
    grad_up = outer_sum(normed_second, grad_up_rows)
    second_part = project_back(grad_gate_rows, gate_weight) + project_back(grad_up_rows, up_weight)
    grad_second = lax.psum(second_part.astype(jnp.bfloat16), "tensor").astype(jnp.float32)
    hidden_back, grad_middle = norm_back(hidden, inverse_second, gain_second, grad_second)
    grad_hidden = cotangent.astype(jnp.float32) + hidden_back
    hidden_low = grad_hidden.astype(jnp.bfloat16)
    grad_output = outer_sum(mixed_rows, hidden_low)
    grad_mixed = project_back(hidden_low, output_weight).astype(jnp.bfloat16)
    grad_heads = as_heads(grad_mixed)
    delta_rows = jnp.sum(grad_heads.astype(jnp.float32) * mixed_heads, axis=-1)
    delta_heads = jnp.swapaxes(delta_rows, 1, 2)
    query_start = jnp.zeros(head_shape + (HEAD,), jnp.float32)
    whole_rows = block_rows * lax.axis_size("ctx")
    key_start = jnp.zeros((sequences, whole_rows, local_heads, HEAD), jnp.float32)
    query_sum, key_total, value_total = gradient_fold(
        query_heads,
        positions,
        grad_heads,
        log_total,
        delta_heads,
        scale_factor,
        (query_start, key_start, key_start),
        (
            lax.all_gather(key_rot, "ctx", axis=1, tiled=True),
            lax.all_gather(value_rows, "ctx", axis=1, tiled=True),
            lax.all_gather(positions, "ctx", axis=1, tiled=True),
        ),
    )
    key_sum, value_sum = (
        lax.psum_scatter(
            key_total.astype(jnp.bfloat16), "ctx", scatter_dimension=1, tiled=True
        ).astype(jnp.float32),
        lax.psum_scatter(
            value_total.astype(jnp.bfloat16), "ctx", scatter_dimension=1, tiled=True
        ).astype(jnp.float32),
    )
    query_back = rotate(
        jnp.swapaxes(query_sum, 1, 2).reshape(sequences, block_rows, -1) * scale_factor,
        cosine_table,
        -sine_table,
    ).astype(jnp.bfloat16)
    key_back = rotate(
        key_sum.reshape(sequences, block_rows, -1) * scale_factor, cosine_table, -sine_table
    ).astype(jnp.bfloat16)
    value_back = value_sum.reshape(sequences, block_rows, -1).astype(jnp.bfloat16)
    grad_query = outer_sum(normed_first, query_back)
    grad_key = outer_sum(normed_first, key_back)
    grad_value = outer_sum(normed_first, value_back)
    first_part = (
        project_back(query_back, query_weight)
        + project_back(key_back, key_weight)
        + project_back(value_back, value_weight)
    )
    grad_first = lax.psum(first_part.astype(jnp.bfloat16), "tensor").astype(jnp.float32)
    rows_back, grad_before = norm_back(token_rows, inverse_first, gain_first, grad_first)
    grad_tokens = grad_hidden + rows_back
    results = lax.psum(
        (
            grad_before,
            grad_query,
            grad_key,
            grad_value,
            grad_output,
            grad_middle,
            grad_gate,
            grad_up,
            grad_down,
        ),
        ("dp", "ctx"),
    )
    return (
        block_output,
        grad_tokens,
        results[0],
        results[1],
        results[2],
        results[3],
        results[4],
        results[5],
        results[6],
        results[7],
        results[8],
    )


f32, bf16 = jnp.float32, jnp.bfloat16


def dot(left, right, left_dim, right_dim):
    return lax.dot_general(
        left, right, (((left_dim,), (right_dim,)), ((), ())), preferred_element_type=f32
    )


def attend_kernel(block, place_ref, slot_ref, *refs):
    pieces = refs[:4]
    out_ref, attended_ref, log_ref, all_ref, key_ref, value_ref = refs[4:]
    half = pieces[0].shape[1] // 2
    length = all_ref.shape[1]
    for index, piece in enumerate(pieces):
        for side in range(2):
            columns = pl.ds(pl.multiple_of(place_ref[2 * index + side] * half, half), half)
            part = piece[:, side * half : (side + 1) * half]
            all_ref[:, columns] = part
            key_ref[columns, :] = part[HEAD : 2 * HEAD, :].astype(f32).T.astype(bf16)
            value_ref[0:HEAD, columns] = part[2 * HEAD :, :]
    value_ref[HEAD:, :] = jnp.ones((value_ref.shape[0] - HEAD, length), bf16)

    def query_step(query_index, unused):
        columns = pl.ds(pl.multiple_of(query_index * block, block), block)
        queries = all_ref[0:HEAD, columns]

        def key_step(key_index, state, diagonal=False):
            old_max, accum = state
            rows = pl.ds(pl.multiple_of(key_index * block, block), block)
            scores = dot(key_ref[rows, :], queries, 1, 0)
            if diagonal:
                key_at = lax.broadcasted_iota(jnp.int32, (block, block), 0)
                query_at = lax.broadcasted_iota(jnp.int32, (block, block), 1)
                scores = jnp.where(key_at <= query_at, scores, masked_score)
            new_max = jnp.maximum(old_max, jnp.max(scores, axis=0, keepdims=True))
            weights = jnp.exp(scores - new_max).astype(bf16)
            accum = accum * jnp.exp(old_max - new_max) + dot(value_ref[:, rows], weights, 1, 0)
            return new_max, accum

        state = (
            jnp.full((1, block), masked_score, f32),
            jnp.zeros((value_ref.shape[0], block), f32),
        )
        state = lax.fori_loop(0, query_index, key_step, state)
        row_max, accum = key_step(query_index, state, True)
        total = accum[HEAD : HEAD + 1, :]
        mixed = accum[0:HEAD, :] / total
        attended_ref[:, columns] = mixed
        log_ref[:, columns] = jnp.broadcast_to(row_max + jnp.log(total), (8, block))
        for side in range(block // half):
            slot = slot_ref[query_index * (block // half) + side]
            out_ref[slot] = mixed[:, side * half : (side + 1) * half].astype(bf16)
        return 0

    lax.fori_loop(0, length // block, query_step, 0)


def gradient_kernel(block, place_ref, send_ref, side_ref, *refs):
    pieces = refs[:8]
    all_ref, attended_ref, log_ref, cosine_ref, sine_ref, out_ref = refs[8:14]
    key_ref, value_ref, grad_ref, delta_ref, query_sum_ref, key_sum_ref = refs[14:]
    half = pieces[0].shape[1]
    length = all_ref.shape[1]
    for index, piece in enumerate(pieces):
        columns = pl.ds(pl.multiple_of(place_ref[index] * half, half), half)
        grad = piece[...]
        grad_ref[:, columns] = grad
        delta = jnp.sum(grad.astype(f32) * attended_ref[:, columns], axis=0, keepdims=True)
        delta_ref[:, columns] = jnp.broadcast_to(delta, (8, half))
    for index in range(length // half):
        columns = pl.ds(index * half, half)
        key_ref[columns, :] = all_ref[HEAD : 2 * HEAD, columns].astype(f32).T.astype(bf16)
        value_ref[columns, :] = all_ref[2 * HEAD :, columns].astype(f32).T.astype(bf16)
    query_sum_ref[...] = jnp.zeros_like(query_sum_ref)

    def key_step(key_index, unused):
        rows = pl.ds(pl.multiple_of(key_index * block, block), block)
        keys = key_ref[rows, :]
        values = value_ref[rows, :]
        keys_turned = all_ref[HEAD : 2 * HEAD, rows]

        def query_step(query_index, state, diagonal=False):
            key_sum, value_sum = state
            columns = pl.ds(pl.multiple_of(query_index * block, block), block)
            queries = all_ref[0:HEAD, columns]
            grads = grad_ref[:, columns]
            scores = dot(keys, queries, 1, 0) - log_ref[0:1, columns]
            if diagonal:
                key_at = lax.broadcasted_iota(jnp.int32, (block, block), 0)
                query_at = lax.broadcasted_iota(jnp.int32, (block, block), 1)
                scores = jnp.where(key_at <= query_at, scores, masked_score)
            weights = jnp.exp(scores)
            grad_weights = dot(values, grads, 1, 0) - delta_ref[0:1, columns]
            grad_scores = (weights * grad_weights).astype(bf16)
            value_sum = value_sum + dot(grads, weights.astype(bf16), 1, 1)
            key_sum = key_sum + dot(queries, grad_scores, 1, 1)
            query_sum_ref[:, columns] += dot(keys_turned, grad_scores, 1, 0)
            return key_sum, value_sum

        state = (jnp.zeros((HEAD, block), f32), jnp.zeros((HEAD, block), f32))
        state = query_step(key_index, state, True)
        key_sum, value_sum = lax.fori_loop(key_index + 1, length // block, query_step, state)
        key_sum_ref[0:HEAD, rows] = key_sum
        key_sum_ref[HEAD:, rows] = value_sum
        return 0

    lax.fori_loop(0, length // block, key_step, 0)

    def turn_back(rows, cosine, sine):
        front, back = rows[: HEAD // 2, :], rows[HEAD // 2 :, :]
        return jnp.concatenate([front * cosine + back * sine, back * cosine - front * sine], axis=0)

    def write_step(index, unused):
        columns = pl.ds(pl.multiple_of(index * half, half), half)
        cosine, sine = cosine_ref[:, columns], sine_ref[:, columns]
        to = send_ref[index]
        at = pl.ds(pl.multiple_of(side_ref[index] * half, half), half)
        query_rows = query_sum_ref[:, columns] * (HEAD**-0.5)
        out_ref[to, 0:HEAD, at] = turn_back(query_rows, cosine, sine).astype(bf16)
        out_ref[to, HEAD : 2 * HEAD, at] = turn_back(
            key_sum_ref[0:HEAD, columns], cosine, sine
        ).astype(bf16)
        out_ref[to, 2 * HEAD :, at] = key_sum_ref[HEAD:, columns].astype(bf16)
        return 0

    lax.fori_loop(0, length // half, write_step, 0)


def attend(place, slot, pieces):
    rows, width = pieces[0].shape
    half, length = width // 2, width * len(pieces)
    smem, vmem = pl.BlockSpec(memory_space=pltpu.SMEM), pl.BlockSpec(memory_space=pltpu.VMEM)
    return pl.pallas_call(
        functools.partial(attend_kernel, width),
        out_shape=(
            jax.ShapeDtypeStruct((2 * len(pieces), HEAD, half), bf16),
            jax.ShapeDtypeStruct((HEAD, length), f32),
            jax.ShapeDtypeStruct((8, length), f32),
            jax.ShapeDtypeStruct((rows, length), bf16),
        ),
        in_specs=[smem] * 2 + [vmem] * 4,
        out_specs=[vmem] * 4,
        scratch_shapes=[pltpu.VMEM((length, HEAD), bf16), pltpu.VMEM((HEAD + 16, length), bf16)],
        compiler_params=pltpu.CompilerParams(vmem_limit_bytes=48 << 20),
        cost_estimate=pl.CostEstimate(flops=20 * 10**9, bytes_accessed=10**7, transcendentals=0),
        name="attend",
    )(place, slot, *pieces)


def attend_back(place, send, side, pieces, everything, attended, log_total, cosine, sine):
    half = pieces[0].shape[1]
    rows, length = everything.shape
    smem, vmem = pl.BlockSpec(memory_space=pltpu.SMEM), pl.BlockSpec(memory_space=pltpu.VMEM)
    return pl.pallas_call(
        functools.partial(gradient_kernel, half),
        out_shape=jax.ShapeDtypeStruct((length // (2 * half), rows, 2 * half), bf16),
        in_specs=[smem] * 3 + [vmem] * 13,
        out_specs=vmem,
        scratch_shapes=[
            pltpu.VMEM((length, HEAD), bf16),
            pltpu.VMEM((length, HEAD), bf16),
            pltpu.VMEM((HEAD, length), bf16),
            pltpu.VMEM((8, length), f32),
            pltpu.VMEM((HEAD, length), f32),
            pltpu.VMEM((2 * HEAD, length), f32),
        ],
        compiler_params=pltpu.CompilerParams(vmem_limit_bytes=48 << 20),
        cost_estimate=pl.CostEstimate(flops=40 * 10**9, bytes_accessed=10**7, transcendentals=0),
        name="attend_back",
    )(place, send, side, *pieces, everything, attended, log_total, cosine, sine)


def pick(stacked, index):
    return lax.dynamic_index_in_dim(stacked, index, 0, keepdims=False)


def swap_tensor(array):
    return lax.ppermute(array, "tensor", [(0, 1), (1, 0)])


def swap_dp(array, bit):
    return lax.ppermute(array, "dp", [(index, index ^ bit) for index in range(4)])


def shift_ctx(array, step):
    size = lax.axis_size("ctx")
    return lax.ppermute(array, "ctx", [(index, (index + step) % size) for index in range(size)])


def shift_both(array, step, flip):
    size = lax.axis_size("ctx")
    pairs = [
        (2 * index + side, 2 * ((index + step) % size) + (side ^ flip))
        for index in range(size)
        for side in range(2)
    ]
    return lax.ppermute(array, ("ctx", "tensor"), pairs)


def in_order(relative, at, size):
    return jnp.take(jnp.stack(relative), (at - jnp.arange(size)) % size, axis=0)


def sum_scatter(rows):
    at, spot, size = lax.axis_index("dp"), lax.axis_index("ctx"), lax.axis_size("ctx")
    for bit, mine in ((1, at % 2), (2, at // 2)):
        rows = rows.reshape((2, rows.shape[0] // 2) + rows.shape[1:])
        arrived = swap_dp(pick(rows, 1 - mine), bit)
        rows = (pick(rows, mine).astype(f32) + arrived.astype(f32)).astype(bf16)
    rows = rows.reshape((size, rows.shape[0] // size) + rows.shape[1:])
    total = pick(rows, spot).astype(f32)
    for step in range(1, size):
        total = total + shift_ctx(pick(rows, (spot + step) % size), step).astype(f32)
    return total.astype(bf16)


def gather_pieces(piece):
    at, spot, size = lax.axis_index("dp"), lax.axis_index("ctx"), lax.axis_size("ctx")
    rows = in_order([piece] + [shift_ctx(piece, step) for step in range(1, size)], spot, size)
    rows = rows.reshape((-1,) + piece.shape[1:])
    for bit, mine in ((2, at // 2), (1, at % 2)):
        arrived = swap_dp(rows, bit)
        rows = jnp.where(
            mine == 0, jnp.concatenate([rows, arrived]), jnp.concatenate([arrived, rows])
        )
    return rows


def head_shards(
    tokens,
    positions,
    norm_before,
    query_weight,
    key_weight,
    value_weight,
    output_weight,
    norm_middle,
    gate_weight,
    up_weight,
    down_weight,
    cotangent,
):
    tokens, positions, cotangent = tokens[0], positions[0], cotangent[0]
    size, spot, side = lax.axis_size("ctx"), lax.axis_index("ctx"), lax.axis_index("tensor")
    count = tokens.shape[0]
    half = count // 2
    length = count * size
    gate_other, up_other = swap_tensor(gate_weight), swap_tensor(up_weight)
    down_other, output_other = swap_tensor(down_weight), swap_tensor(output_weight)

    straight = (positions[0] == spot * count) & (positions[half] == spot * count + half)

    def place_of(index, part):
        folded = jnp.where(part == 0, index, 2 * size - 1 - index)
        return jnp.where(straight, 2 * index + part, folded).astype(jnp.int32)

    places = jnp.arange(2 * size)
    owner = jnp.where(straight, places // 2, jnp.minimum(places, 2 * size - 1 - places))
    owner_half = jnp.where(straight, places % 2, (places >= size).astype(jnp.int32))
    owner_step = (owner - spot) % size
    steps = jnp.arange(size)
    place_in = place_of(((spot - steps) % size)[:, None], jnp.arange(2)[None, :]).reshape(-1)
    place_grad = place_of(
        ((spot - steps) % size)[:, None], (side ^ jnp.arange(2))[None, :]
    ).reshape(-1)
    slot = (2 * owner_step + (owner_half ^ side)).astype(jnp.int32)

    frequency = rope_base ** (-jnp.arange(HEAD // 2).astype(f32) * 2.0 / HEAD)
    angles = frequency[:, None] * positions.astype(f32)[None, :]
    cosine, sine = jnp.cos(angles), jnp.sin(angles)
    angles_all = frequency[:, None] * jnp.arange(length).astype(f32)[None, :]
    cosine_all, sine_all = jnp.cos(angles_all), jnp.sin(angles_all)

    token_rows = tokens.astype(f32)
    gain_first, gain_second = norm_before.astype(f32), norm_middle.astype(f32)
    normed_first, inverse_first = normalize(token_rows, gain_first)
    normed_first = normed_first.astype(bf16)

    def turn(rows):
        rows = rows.reshape(size, 2, HEAD // 2, count)
        front, back = rows[:, 0], rows[:, 1]
        turned = [front * cosine - back * sine, back * cosine + front * sine]
        return jnp.concatenate(turned, axis=1).astype(bf16)

    queries = turn(dot(query_weight, normed_first, 0, 1)) * bf16(HEAD**-0.5)
    keys = turn(dot(key_weight, normed_first, 0, 1))
    values = dot(value_weight, normed_first, 0, 1).astype(bf16).reshape(size, HEAD, count)
    per_head = jnp.concatenate([queries, keys, values], axis=1)
    pieces = [pick(per_head, spot)] + [
        shift_ctx(pick(per_head, (spot + step) % size), step) for step in range(1, size)
    ]
    mixed_out, attended, log_total, everything = attend(place_in, slot, pieces)

    def exchange(parts):
        return [
            parts[2 * step + flip] if step + flip == 0 else shift_both(parts[2 * step + flip], step, flip)
            for step in range(size)
            for flip in range(2)
        ]

    mixed = exchange([mixed_out[index] for index in range(2 * size)])
    mixed_own = in_order(mixed[0::2], spot, size).reshape(size * HEAD, half)
    mixed_other = in_order(mixed[1::2], spot, size).reshape(size * HEAD, half)

    my_tokens = lax.dynamic_slice_in_dim(token_rows, side * half, half, 0)
    my_cotangent = lax.dynamic_slice_in_dim(cotangent, side * half, half, 0)
    hidden = my_tokens + (dot(mixed_own, output_weight, 0, 0) + dot(mixed_other, output_other, 0, 0))
    normed_second, inverse_second = normalize(hidden, gain_second)
    normed_second = normed_second.astype(bf16)

    def feed(gate_part, up_part, down_part):
        gate_rows = dot(normed_second, gate_part, 1, 0)
        upward = dot(normed_second, up_part, 1, 0)
        sigmoid_gate = jax.nn.sigmoid(gate_rows)
        silu_gate = gate_rows * sigmoid_gate
        activated = (silu_gate * upward).astype(bf16)
        grad_act = dot(my_cotangent, down_part, 1, 1)
        grad_gate_rows = (
            grad_act * upward * sigmoid_gate * (1.0 + gate_rows * (1.0 - sigmoid_gate))
        ).astype(bf16)
        grad_up_rows = (grad_act * silu_gate).astype(bf16)
        forward = dot(activated, down_part, 1, 0)
        backward = dot(grad_gate_rows, gate_part, 1, 1) + dot(grad_up_rows, up_part, 1, 1)
        grads = jnp.concatenate(
            [
                dot(normed_second, grad_gate_rows, 0, 0).astype(bf16),
                dot(normed_second, grad_up_rows, 0, 0).astype(bf16),
                dot(my_cotangent, activated, 0, 0).astype(bf16),
            ],
            axis=1,
        )
        return forward, backward, grads

    forward_own, backward_own, grads_own = feed(gate_weight, up_weight, down_weight)
    forward_other, backward_other, grads_other = feed(gate_other, up_other, down_other)
    output_half = (hidden + (forward_own + forward_other)).astype(bf16)

    def both_halves(mine):
        other = swap_tensor(mine)
        return jnp.where(
            side == 0, jnp.concatenate([mine, other]), jnp.concatenate([other, mine])
        )

    block_output = both_halves(output_half)
    grad_second = backward_own + backward_other
    weighted = grad_second * gain_second
    inner = jnp.mean(weighted * hidden, axis=-1, keepdims=True)
    grad_hidden = my_cotangent.astype(f32) + (
        inverse_second * weighted - hidden * (inverse_second**3) * inner
    )
    grad_middle = jnp.sum(grad_second * hidden * inverse_second, axis=0)
    hidden_low = grad_hidden.astype(bf16)
    grad_mixed_own = dot(output_weight, hidden_low, 1, 1).astype(bf16).reshape(size, HEAD, half)
    grad_mixed_other = dot(output_other, hidden_low, 1, 1).astype(bf16).reshape(size, HEAD, half)
    grad_parts = []
    for step in range(size):
        grad_parts.append(pick(grad_mixed_own, (spot + step) % size))
        grad_parts.append(pick(grad_mixed_other, (spot + step) % size))
    grad_pieces = exchange(grad_parts)
    all_low = both_halves(hidden_low)

    def with_output(grads, mixed_part):
        return jnp.concatenate(
            [
                grads,
                dot(hidden_low, mixed_part, 0, 1).astype(bf16),
                jnp.broadcast_to(grad_middle.astype(bf16)[:, None], (grads.shape[0], 128)),
            ],
            axis=1,
        )

    feed_rows = with_output(grads_own, mixed_own).astype(f32) + swap_tensor(
        with_output(grads_other, mixed_other)
    ).astype(f32)
    feed_sum = gather_pieces(sum_scatter(feed_rows.astype(bf16))).astype(f32)
    units = gate_weight.shape[1]
    grad_gate = feed_sum[:, :units]
    grad_up = feed_sum[:, units : 2 * units]
    grad_down = feed_sum[:, 2 * units : 3 * units].T
    grad_output = feed_sum[:, 3 * units : 3 * units + size * HEAD].T
    grad_middle = feed_sum[:, 3 * units + size * HEAD]

    back_out = attend_back(
        place_grad,
        owner_step.astype(jnp.int32),
        owner_half.astype(jnp.int32),
        grad_pieces,
        everything,
        attended,
        log_total,
        cosine_all,
        sine_all,
    )
    back = [back_out[0]] + [shift_ctx(back_out[step], step) for step in range(1, size)]
    back = in_order(back, spot, size)
    query_back = back[:, 0:HEAD].reshape(size * HEAD, count)
    key_back = back[:, HEAD : 2 * HEAD].reshape(size * HEAD, count)
    value_back = back[:, 2 * HEAD :].reshape(size * HEAD, count)
    first_part = (
        dot(query_back, query_weight, 0, 1)
        + dot(key_back, key_weight, 0, 1)
        + dot(value_back, value_weight, 0, 1)
    )
    grad_before = jnp.sum(first_part * token_rows * inverse_first, axis=0)
    grad_before = grad_before + swap_tensor(grad_before)
    first_part = first_part.astype(bf16)
    grad_first = first_part.astype(f32) + swap_tensor(first_part).astype(f32)
    weighted = grad_first * gain_first
    inner = jnp.mean(weighted * token_rows, axis=-1, keepdims=True)
    grad_tokens = all_low.astype(f32) + (
        inverse_first * weighted - token_rows * (inverse_first**3) * inner
    )
    first_rows = jnp.concatenate(
        [
            dot(normed_first, query_back, 0, 1).astype(bf16),
            dot(normed_first, key_back, 0, 1).astype(bf16),
            dot(normed_first, value_back, 0, 1).astype(bf16),
            jnp.broadcast_to(grad_before.astype(bf16)[:, None], (normed_first.shape[1], 128)),
        ],
        axis=1,
    )
    first_sum = gather_pieces(sum_scatter(first_rows)).astype(f32)
    width = size * HEAD
    return (
        block_output[None],
        grad_tokens[None],
        first_sum[:, 3 * width],
        first_sum[:, :width],
        first_sum[:, width : 2 * width],
        first_sum[:, 2 * width : 3 * width],
        grad_output,
        grad_middle,
        grad_gate,
        grad_up,
        grad_down,
    )


def solution(mesh):
    sizes = dict(mesh.shape)

    def body(*arguments):
        local_heads = arguments[3].shape[1] // HEAD
        one_head = sizes["ctx"] == local_heads and sizes["tensor"] == 2 and sizes["dp"] == 4
        one_sequence = arguments[0].shape[0] == 1
        return (head_shards if one_head and one_sequence else shards)(*arguments)

    return jax.shard_map(
        body,
        mesh=mesh,
        in_specs=(
            P("dp", "ctx", None),
            P("dp", "ctx"),
            P(),
            P(None, "tensor"),
            P(None, "tensor"),
            P(None, "tensor"),
            P("tensor", None),
            P(),
            P(None, "tensor"),
            P(None, "tensor"),
            P("tensor", None),
            P("dp", "ctx", None),
        ),
        out_specs=(
            P("dp", "ctx", None),
            P("dp", "ctx", None),
            P(),
            P(None, "tensor"),
            P(None, "tensor"),
            P(None, "tensor"),
            P("tensor", None),
            P(),
            P(None, "tensor"),
            P(None, "tensor"),
            P("tensor", None),
        ),
        check_vma=False,
    )
```

```python
import functools
import math

import jax
import jax.numpy as jnp
from jax import lax
from jax.experimental import pallas as pl
from jax.experimental.pallas import tpu as pltpu
from jax.sharding import PartitionSpec as P

HEAD = 64


epsilon = 1e-05
rope_base = 10000.0
masked_score = -1e30


def rope_tables(positions):
    frequency = rope_base ** (-jnp.arange(HEAD // 2).astype(jnp.float32) * 2.0 / HEAD)
    angles = positions.astype(jnp.float32)[..., None] * frequency
    return (jnp.cos(angles), jnp.sin(angles))


def rotate(matrix, cosine_table, sine_table):
    shaped = matrix.reshape(matrix.shape[:-1] + (-1, HEAD))
    front_half = shaped[..., : HEAD // 2]
    back_half = shaped[..., HEAD // 2 :]
    cosine = cosine_table[..., None, :]
    sine_part = sine_table[..., None, :]
    turned = jnp.concatenate(
        [front_half * cosine - back_half * sine_part, back_half * cosine + front_half * sine_part],
        axis=-1,
    )
    return turned.reshape(matrix.shape)


def normalize(token_rows, gain_row):
    inverse_rms = lax.rsqrt(jnp.mean(token_rows * token_rows, axis=-1, keepdims=True) + epsilon)
    return (token_rows * inverse_rms * gain_row, inverse_rms)


def norm_back(token_rows, inverse_rms, gain_row, grad_normed):
    weighted = grad_normed * gain_row
    inner_sum = jnp.mean(weighted * token_rows, axis=-1, keepdims=True)
    grad_rows = (
        inverse_rms * weighted - token_rows * (inverse_rms * inverse_rms * inverse_rms) * inner_sum
    )
    grad_gain = jnp.sum(grad_normed * token_rows * inverse_rms, axis=(0, 1))
    return (grad_rows, grad_gain)


def project(left, weight):
    return jnp.einsum("sbd,dh->sbh", left, weight, preferred_element_type=jnp.float32)


def project_back(grad_rows, weight):
    return jnp.einsum("sbh,dh->sbd", grad_rows, weight, preferred_element_type=jnp.float32)


def outer_sum(left, right):
    return jnp.einsum("sbd,sbh->dh", left, right, preferred_element_type=jnp.float32)


def as_heads(matrix):
    return matrix.reshape(matrix.shape[:2] + (-1, HEAD))


def split_blocks(matrix, block_width):
    block_count = matrix.shape[1] // block_width
    shaped = matrix.reshape(matrix.shape[:1] + (block_count, block_width) + matrix.shape[2:])
    return jnp.moveaxis(shaped, 1, 0)


def join_blocks(stacked):
    joined = jnp.moveaxis(stacked, 0, 1)
    return joined.reshape((joined.shape[0], joined.shape[1] * joined.shape[2]) + joined.shape[3:])


def forward_fold(query_heads, query_pos, scale_factor, fold_state, incoming):
    key_part, value_part, key_pos = incoming
    block_width = math.gcd(key_part.shape[1], 512)
    blocks = (
        split_blocks(as_heads(key_part), block_width),
        split_blocks(as_heads(value_part), block_width),
        split_blocks(key_pos, block_width),
    )

    def forward_step_block(block_state, block_in):
        key_heads, value_heads, block_pos = block_in
        allowed = block_pos[:, None, None, :] <= query_pos[:, None, :, None]
        old_max, old_total, old_accum = block_state
        scores = (
            jnp.einsum(
                "sqhe,skhe->shqk", query_heads, key_heads, preferred_element_type=jnp.float32
            )
            * scale_factor
        )
        scores = jnp.where(allowed, scores, masked_score)
        new_max = jnp.maximum(old_max, jnp.max(scores, axis=-1))
        weights = jnp.where(allowed, jnp.exp(scores - new_max[..., None]), 0.0)
        factor = jnp.exp(old_max - new_max)
        new_total = old_total * factor + jnp.sum(weights, axis=-1)
        new_accum = old_accum * factor[..., None] + jnp.einsum(
            "shqk,skhe->shqe",
            weights.astype(jnp.bfloat16),
            value_heads,
            preferred_element_type=jnp.float32,
        )
        return ((new_max, new_total, new_accum), None)

    final_state, unused = lax.scan(forward_step_block, fold_state, blocks)
    return final_state


def gradient_fold(
    query_heads, query_pos, grad_heads, log_total, delta_heads, scale_factor, fold_state, incoming
):
    key_part, value_part, key_pos = incoming
    row_count = key_part.shape[1]
    block_width = math.gcd(row_count, 512)
    blocks = (
        split_blocks(as_heads(key_part), block_width),
        split_blocks(as_heads(value_part), block_width),
        split_blocks(key_pos, block_width),
    )

    def gradient_step_block(query_state, block_in):
        key_heads, value_heads, block_pos = block_in
        allowed = block_pos[:, None, None, :] <= query_pos[:, None, :, None]
        scores = (
            jnp.einsum(
                "sqhe,skhe->shqk", query_heads, key_heads, preferred_element_type=jnp.float32
            )
            * scale_factor
        )
        weights = jnp.where(allowed, jnp.exp(scores - log_total[..., None]), 0.0)
        grad_weights = jnp.einsum(
            "sqhe,skhe->shqk", grad_heads, value_heads, preferred_element_type=jnp.float32
        )
        grad_scores = (weights * (grad_weights - delta_heads[..., None])).astype(jnp.bfloat16)
        new_query = query_state + jnp.einsum(
            "shqk,skhe->shqe", grad_scores, key_heads, preferred_element_type=jnp.float32
        )
        key_grad = jnp.einsum(
            "shqk,sqhe->skhe", grad_scores, query_heads, preferred_element_type=jnp.float32
        )
        value_grad = jnp.einsum(
            "shqk,sqhe->skhe",
            weights.astype(jnp.bfloat16),
            grad_heads,
            preferred_element_type=jnp.float32,
        )
        return (new_query, (key_grad, value_grad))

    query_state, key_total, value_total = fold_state
    query_state, outputs = lax.scan(gradient_step_block, query_state, blocks)
    key_rows = join_blocks(outputs[0])
    value_rows = join_blocks(outputs[1])
    key_total = key_rows
    value_total = value_rows
    return (query_state, key_total, value_total)


def shards(
    tokens,
    positions,
    norm_before,
    query_weight,
    key_weight,
    value_weight,
    output_weight,
    norm_middle,
    gate_weight,
    up_weight,
    down_weight,
    cotangent,
):
    sequences = tokens.shape[0]
    block_rows = tokens.shape[1]
    local_heads = query_weight.shape[1] // HEAD
    scale_factor = HEAD ** (-0.5)
    cosine_table, sine_table = rope_tables(positions)
    token_rows = tokens.astype(jnp.float32)
    gain_first = norm_before.astype(jnp.float32)
    gain_second = norm_middle.astype(jnp.float32)
    normed_first, inverse_first = normalize(token_rows, gain_first)
    normed_first = normed_first.astype(jnp.bfloat16)
    query_rot = rotate(project(normed_first, query_weight), cosine_table, sine_table).astype(
        jnp.bfloat16
    )
    key_rot = rotate(project(normed_first, key_weight), cosine_table, sine_table).astype(
        jnp.bfloat16
    )
    value_rows = project(normed_first, value_weight).astype(jnp.bfloat16)
    query_heads = as_heads(query_rot)
    head_shape = (sequences, local_heads, block_rows)
    start_state = (
        jnp.full(head_shape, masked_score, jnp.float32),
        jnp.zeros(head_shape, jnp.float32),
        jnp.zeros(head_shape + (HEAD,), jnp.float32),
    )
    row_max, row_total, accum_heads = forward_fold(
        query_heads,
        positions,
        scale_factor,
        start_state,
        (
            lax.all_gather(key_rot, "ctx", axis=1, tiled=True),
            lax.all_gather(value_rows, "ctx", axis=1, tiled=True),
            lax.all_gather(positions, "ctx", axis=1, tiled=True),
        ),
    )
    log_total = row_max + jnp.log(row_total)
    mixed_heads = jnp.swapaxes(accum_heads / row_total[..., None], 1, 2)
    mixed_rows = mixed_heads.reshape(sequences, block_rows, -1).astype(jnp.bfloat16)
    hidden = token_rows + lax.psum(
        project(mixed_rows, output_weight).astype(jnp.bfloat16), "tensor"
    ).astype(jnp.float32)
    normed_second, inverse_second = normalize(hidden, gain_second)
    normed_second = normed_second.astype(jnp.bfloat16)
    gate_rows = project(normed_second, gate_weight)
    upward = project(normed_second, up_weight)
    sigmoid_gate = jax.nn.sigmoid(gate_rows)
    silu_gate = gate_rows * sigmoid_gate
    activated = (silu_gate * upward).astype(jnp.bfloat16)
    block_output = (
        hidden
        + lax.psum(project(activated, down_weight).astype(jnp.bfloat16), "tensor").astype(
            jnp.float32
        )
    ).astype(jnp.bfloat16)
    grad_down = outer_sum(activated, cotangent)
    grad_act = project_back(cotangent, down_weight)
    grad_gate_rows = (
        grad_act * upward * sigmoid_gate * (1.0 + gate_rows * (1.0 - sigmoid_gate))
    ).astype(jnp.bfloat16)
    grad_up_rows = (grad_act * silu_gate).astype(jnp.bfloat16)
    grad_gate = outer_sum(normed_second, grad_gate_rows)
    grad_up = outer_sum(normed_second, grad_up_rows)
    second_part = project_back(grad_gate_rows, gate_weight) + project_back(grad_up_rows, up_weight)
    grad_second = lax.psum(second_part.astype(jnp.bfloat16), "tensor").astype(jnp.float32)
    hidden_back, grad_middle = norm_back(hidden, inverse_second, gain_second, grad_second)
    grad_hidden = cotangent.astype(jnp.float32) + hidden_back
    hidden_low = grad_hidden.astype(jnp.bfloat16)
    grad_output = outer_sum(mixed_rows, hidden_low)
    grad_mixed = project_back(hidden_low, output_weight).astype(jnp.bfloat16)
    grad_heads = as_heads(grad_mixed)
    delta_rows = jnp.sum(grad_heads.astype(jnp.float32) * mixed_heads, axis=-1)
    delta_heads = jnp.swapaxes(delta_rows, 1, 2)
    query_start = jnp.zeros(head_shape + (HEAD,), jnp.float32)
    whole_rows = block_rows * lax.axis_size("ctx")
    key_start = jnp.zeros((sequences, whole_rows, local_heads, HEAD), jnp.float32)
    query_sum, key_total, value_total = gradient_fold(
        query_heads,
        positions,
        grad_heads,
        log_total,
        delta_heads,
        scale_factor,
        (query_start, key_start, key_start),
        (
            lax.all_gather(key_rot, "ctx", axis=1, tiled=True),
            lax.all_gather(value_rows, "ctx", axis=1, tiled=True),
            lax.all_gather(positions, "ctx", axis=1, tiled=True),
        ),
    )
    key_sum, value_sum = (
        lax.psum_scatter(
            key_total.astype(jnp.bfloat16), "ctx", scatter_dimension=1, tiled=True
        ).astype(jnp.float32),
        lax.psum_scatter(
            value_total.astype(jnp.bfloat16), "ctx", scatter_dimension=1, tiled=True
        ).astype(jnp.float32),
    )
    query_back = rotate(
        jnp.swapaxes(query_sum, 1, 2).reshape(sequences, block_rows, -1) * scale_factor,
        cosine_table,
        -sine_table,
    ).astype(jnp.bfloat16)
    key_back = rotate(
        key_sum.reshape(sequences, block_rows, -1) * scale_factor, cosine_table, -sine_table
    ).astype(jnp.bfloat16)
    value_back = value_sum.reshape(sequences, block_rows, -1).astype(jnp.bfloat16)
    grad_query = outer_sum(normed_first, query_back)
    grad_key = outer_sum(normed_first, key_back)
    grad_value = outer_sum(normed_first, value_back)
    first_part = (
        project_back(query_back, query_weight)
        + project_back(key_back, key_weight)
        + project_back(value_back, value_weight)
    )
    grad_first = lax.psum(first_part.astype(jnp.bfloat16), "tensor").astype(jnp.float32)
    rows_back, grad_before = norm_back(token_rows, inverse_first, gain_first, grad_first)
    grad_tokens = grad_hidden + rows_back
    results = lax.psum(
        (
            grad_before,
            grad_query,
            grad_key,
            grad_value,
            grad_output,
            grad_middle,
            grad_gate,
            grad_up,
            grad_down,
        ),
        ("dp", "ctx"),
    )
    return (
        block_output,
        grad_tokens,
        results[0],
        results[1],
        results[2],
        results[3],
        results[4],
        results[5],
        results[6],
        results[7],
        results[8],
    )


f32, bf16 = jnp.float32, jnp.bfloat16


def dot(left, right, left_dim, right_dim):
    return lax.dot_general(
        left, right, (((left_dim,), (right_dim,)), ((), ())), preferred_element_type=f32
    )


def attend_kernel(block, place_ref, slot_ref, *refs):
    pieces = refs[:4]
    out_ref, attended_ref, log_ref, all_ref, key_ref, value_ref = refs[4:]
    half = pieces[0].shape[1] // 2
    length = all_ref.shape[1]
    for index, piece in enumerate(pieces):
        for side in range(2):
            columns = pl.ds(pl.multiple_of(place_ref[2 * index + side] * half, half), half)
            part = piece[:, side * half : (side + 1) * half]
            all_ref[:, columns] = part
            key_ref[columns, :] = part[HEAD : 2 * HEAD, :].astype(f32).T.astype(bf16)
            value_ref[0:HEAD, columns] = part[2 * HEAD :, :]
    value_ref[HEAD:, :] = jnp.ones((value_ref.shape[0] - HEAD, length), bf16)

    def query_step(query_index, unused):
        columns = pl.ds(pl.multiple_of(query_index * block, block), block)
        queries = all_ref[0:HEAD, columns]

        def key_step(key_index, state, diagonal=False):
            old_max, accum = state
            rows = pl.ds(pl.multiple_of(key_index * block, block), block)
            scores = dot(key_ref[rows, :], queries, 1, 0)
            if diagonal:
                key_at = lax.broadcasted_iota(jnp.int32, (block, block), 0)
                query_at = lax.broadcasted_iota(jnp.int32, (block, block), 1)
                scores = jnp.where(key_at <= query_at, scores, masked_score)
            new_max = jnp.maximum(old_max, jnp.max(scores, axis=0, keepdims=True))
            weights = jnp.exp(scores - new_max).astype(bf16)
            accum = accum * jnp.exp(old_max - new_max) + dot(value_ref[:, rows], weights, 1, 0)
            return new_max, accum

        state = (
            jnp.full((1, block), masked_score, f32),
            jnp.zeros((value_ref.shape[0], block), f32),
        )
        state = lax.fori_loop(0, query_index, key_step, state)
        row_max, accum = key_step(query_index, state, True)
        total = accum[HEAD : HEAD + 1, :]
        mixed = accum[0:HEAD, :] / total
        attended_ref[:, columns] = mixed
        log_ref[:, columns] = jnp.broadcast_to(row_max + jnp.log(total), (8, block))
        for side in range(block // half):
            slot = slot_ref[query_index * (block // half) + side]
            out_ref[slot] = mixed[:, side * half : (side + 1) * half].astype(bf16)
        return 0

    lax.fori_loop(0, length // block, query_step, 0)


def gradient_kernel(block, first, last, place_ref, send_ref, side_ref, *refs):
    pieces_ref, all_ref, attended_ref, log_ref, *refs = refs
    half = pieces_ref.shape[2]
    length = all_ref.shape[1]
    ends = last == length // block
    if first:
        query_in_ref, key_in_ref, cosine_ref, sine_ref, *refs = refs
        out_ref, key_ref, value_ref, grad_ref, delta_ref, query_sum_ref, key_sum_ref = refs
        query_sum_ref[...] = query_in_ref[...]
        key_sum_ref[...] = key_in_ref[...]
    else:
        query_sum_ref, key_sum_ref, key_ref, value_ref, grad_ref, delta_ref = refs
        query_sum_ref[...] = jnp.zeros_like(query_sum_ref)
    for index in range(pieces_ref.shape[0]):
        columns = pl.ds(pl.multiple_of(place_ref[index] * half, half), half)
        grad = pieces_ref[index]
        grad_ref[:, columns] = grad
        delta = jnp.sum(grad.astype(f32) * attended_ref[:, columns], axis=0, keepdims=True)
        delta_ref[:, columns] = jnp.broadcast_to(delta, (8, half))
    for index in range(first, last):
        columns = pl.ds(index * block, block)
        key_ref[columns, :] = all_ref[HEAD : 2 * HEAD, columns].astype(f32).T.astype(bf16)
        value_ref[columns, :] = all_ref[2 * HEAD :, columns].astype(f32).T.astype(bf16)

    def key_step(key_index, unused):
        rows = pl.ds(pl.multiple_of(key_index * block, block), block)
        keys = key_ref[rows, :]
        values = value_ref[rows, :]
        keys_turned = all_ref[HEAD : 2 * HEAD, rows]

        def query_step(query_index, state, diagonal=False):
            key_sum, value_sum = state
            columns = pl.ds(pl.multiple_of(query_index * block, block), block)
            queries = all_ref[0:HEAD, columns]
            grads = grad_ref[:, columns]
            scores = dot(keys, queries, 1, 0) - log_ref[0:1, columns]
            if diagonal:
                key_at = lax.broadcasted_iota(jnp.int32, (block, block), 0)
                query_at = lax.broadcasted_iota(jnp.int32, (block, block), 1)
                scores = jnp.where(key_at <= query_at, scores, masked_score)
            weights = jnp.exp(scores)
            grad_weights = dot(values, grads, 1, 0) - delta_ref[0:1, columns]
            grad_scores = (weights * grad_weights).astype(bf16)
            value_sum = value_sum + dot(grads, weights.astype(bf16), 1, 1)
            key_sum = key_sum + dot(queries, grad_scores, 1, 1)
            query_sum_ref[:, columns] += dot(keys_turned, grad_scores, 1, 0)
            return key_sum, value_sum

        state = (jnp.zeros((HEAD, block), f32), jnp.zeros((HEAD, block), f32))
        state = query_step(key_index, state, True)
        key_sum, value_sum = lax.fori_loop(key_index + 1, length // block, query_step, state)
        key_sum_ref[0:HEAD, rows] = key_sum
        key_sum_ref[HEAD:, rows] = value_sum
        return 0

    lax.fori_loop(first, last, key_step, 0)
    if not ends:
        return

    def turn_back(rows, cosine, sine):
        front, back = rows[: HEAD // 2, :], rows[HEAD // 2 :, :]
        return jnp.concatenate([front * cosine + back * sine, back * cosine - front * sine], axis=0)

    def write_step(index, unused):
        columns = pl.ds(pl.multiple_of(index * half, half), half)
        cosine, sine = cosine_ref[:, columns], sine_ref[:, columns]
        to = send_ref[index]
        at = pl.ds(pl.multiple_of(side_ref[index] * half, half), half)
        query_rows = query_sum_ref[:, columns] * (HEAD**-0.5)
        out_ref[to, 0:HEAD, at] = turn_back(query_rows, cosine, sine).astype(bf16)
        out_ref[to, HEAD : 2 * HEAD, at] = turn_back(
            key_sum_ref[0:HEAD, columns], cosine, sine
        ).astype(bf16)
        out_ref[to, 2 * HEAD :, at] = key_sum_ref[HEAD:, columns].astype(bf16)
        return 0

    lax.fori_loop(0, length // half, write_step, 0)


def attend(place, slot, pieces):
    rows, width = pieces[0].shape
    half, length = width // 2, width * len(pieces)
    smem, vmem = pl.BlockSpec(memory_space=pltpu.SMEM), pl.BlockSpec(memory_space=pltpu.VMEM)
    return pl.pallas_call(
        functools.partial(attend_kernel, width),
        out_shape=(
            jax.ShapeDtypeStruct((2 * len(pieces), HEAD, half), bf16),
            jax.ShapeDtypeStruct((HEAD, length), f32),
            jax.ShapeDtypeStruct((8, length), f32),
            jax.ShapeDtypeStruct((rows, length), bf16),
        ),
        in_specs=[smem] * 2 + [vmem] * 4,
        out_specs=[vmem] * 4,
        scratch_shapes=[pltpu.VMEM((length, HEAD), bf16), pltpu.VMEM((HEAD + 16, length), bf16)],
        compiler_params=pltpu.CompilerParams(vmem_limit_bytes=48 << 20),
        cost_estimate=pl.CostEstimate(flops=10**6, bytes_accessed=10**4, transcendentals=0),
        name="attend",
    )(place, slot, *pieces)


def attend_back(first, last, scalars, pieces, everything, attended, log_total, *sums):
    half = pieces.shape[2]
    rows, length = everything.shape
    smem, vmem = pl.BlockSpec(memory_space=pltpu.SMEM), pl.BlockSpec(memory_space=pltpu.VMEM)
    totals = [(HEAD, length), (2 * HEAD, length)]
    scratch = [
        pltpu.VMEM((length, HEAD), bf16),
        pltpu.VMEM((length, HEAD), bf16),
        pltpu.VMEM((HEAD, length), bf16),
        pltpu.VMEM((8, length), f32),
    ]
    if first:
        out_shape = jax.ShapeDtypeStruct((length // (2 * half), rows, 2 * half), bf16)
        scratch = scratch + [pltpu.VMEM(shape, f32) for shape in totals]
    else:
        out_shape = tuple(jax.ShapeDtypeStruct(shape, f32) for shape in totals)
    return pl.pallas_call(
        functools.partial(gradient_kernel, half, first, last),
        out_shape=out_shape,
        in_specs=[smem] * 3 + [vmem] * (4 + len(sums)),
        out_specs=vmem if first else (vmem, vmem),
        scratch_shapes=scratch,
        compiler_params=pltpu.CompilerParams(vmem_limit_bytes=48 << 20),
        cost_estimate=pl.CostEstimate(flops=10**6, bytes_accessed=10**4, transcendentals=0),
        name="attend_back",
    )(*scalars, pieces, everything, attended, log_total, *sums)


SMEM, VMEM = pl.BlockSpec(memory_space=pltpu.SMEM), pl.BlockSpec(memory_space=pltpu.VMEM)
SMALL_COST = pl.CostEstimate(flops=10**6, bytes_accessed=10**4, transcendentals=0)


def kernel_call(kernel, name, out_shape, scalars, *arrays, scratch=()):
    return pl.pallas_call(
        kernel,
        out_shape=out_shape,
        in_specs=[SMEM] * len(scalars) + [VMEM] * len(arrays),
        out_specs=jax.tree.map(lambda unused: VMEM, out_shape),
        scratch_shapes=list(scratch),
        compiler_params=pltpu.CompilerParams(vmem_limit_bytes=48 << 20),
        cost_estimate=SMALL_COST,
        name=name,
    )(*scalars, *arrays)


def rows_at(index, count):
    return pl.ds(pl.multiple_of(index * count, count), count)


def token_kernel(side_ref, mine_ref, arrived_ref, tokens_ref, gain_ref, *refs):
    low_mine, low_arrived, out_mine, out_arrived, grad_ref, output_ref = refs
    side = side_ref[0]
    half = low_mine.shape[0]
    gain = gain_ref[...]
    for index, low, out in ((side, low_mine, out_mine), (1 - side, low_arrived, out_arrived)):
        rows = rows_at(index, half)
        grad = mine_ref[rows, :].astype(f32) + arrived_ref[rows, :].astype(f32)
        token = tokens_ref[rows, :].astype(f32)
        inverse = lax.rsqrt(jnp.mean(token * token, axis=1, keepdims=True) + epsilon)
        weighted = grad * gain
        inner = jnp.mean(weighted * token, axis=1, keepdims=True)
        grad_ref[rows, :] = low[...].astype(f32) + (
            inverse * weighted - token * (inverse * inverse * inverse) * inner
        )
        output_ref[rows, :] = out[...]


def feed_out_kernel(spot_ref, *refs):
    parts, outs, rows_ref = refs[:4], refs[4:9], refs[9]
    gate_ref, up_ref, down_ref, output_ref, middle_ref = outs
    core, row = spot_ref[0], spot_ref[1]
    piece = parts[0].shape[1]
    spots = ((core, row), (core, 1 - row), (1 - core, row), (1 - core, 1 - row))
    for part, (core_at, row_at) in zip(parts, spots):
        for split in range(2):
            rows_ref[rows_at(4 * core_at + 2 * split + row_at, piece), :] = part[split]
    units, width = down_ref.shape[0], output_ref.shape[0]
    padded = -(-units // 128) * 128
    gate_ref[...] = rows_ref[0:padded, :].astype(f32).T[:, :units]
    up_ref[...] = rows_ref[units : units + padded, :].astype(f32).T[:, :units]
    down_ref[...] = rows_ref[2 * units : 3 * units, :].astype(f32)
    output_ref[...] = rows_ref[3 * units : 3 * units + width, :].astype(f32)
    last = 3 * units + width
    middle_ref[...] = rows_ref[last : last + 16, :].astype(f32)


def first_out_kernel(spot_ref, *refs):
    size = len(refs) - 6
    parts, weight_ref, outs, rows_ref = refs[:size], refs[size], refs[size + 1 : -1], refs[-1]
    width = size * HEAD
    spot = spot_ref[0]
    total = None
    for which in range(3):
        for step, part in enumerate(parts):
            rows_ref[rows_at(lax.rem(spot - step + size, size), HEAD), :] = part[
                which * HEAD : (which + 1) * HEAD, :
            ].astype(f32)
        grad = rows_ref[...]
        outs[which][...] = grad.T
        term = jnp.sum(grad * weight_ref[which * width : (which + 1) * width, :].astype(f32), axis=0, keepdims=True)
        total = term if total is None else total + term
    outs[3][...] = jnp.broadcast_to(total, outs[3].shape)


def head_grad_kernel(side_ref, back_ref, *refs):
    normed, out_ref = refs[:-1], refs[-1]
    side, size = side_ref[0], back_ref.shape[0]
    half = back_ref.shape[2] // 2
    total = None
    for step in range(size):
        for place, rows in ((side, normed[2 * step]), (1 - side, normed[2 * step + 1])):
            term = dot(back_ref[(size - step) % size, :, rows_at(place, half)], rows[...], 1, 0)
            total = term if total is None else total + term
    out_ref[...] = total.astype(bf16)


def first_part_kernel(spot_ref, *refs):
    size = len(refs) - 3
    parts, weight_ref, out_ref, rows_ref = refs[:size], refs[size], refs[size + 1], refs[size + 2]
    spot = spot_ref[0]
    for step, part in enumerate(parts):
        for which in range(3):
            at = which * size + lax.rem(spot - step + size, size)
            rows_ref[rows_at(at, HEAD), :] = part[which * HEAD : (which + 1) * HEAD, :]
    block = out_ref.shape[0] // 4
    for index in range(4):
        rows = slice(index * block, (index + 1) * block)
        out_ref[rows, :] = dot(rows_ref[:, rows], weight_ref[...], 0, 0).astype(bf16)


def prepare_kernel(at_ref, tokens_ref, gain_ref, cosine_ref, sine_ref, *refs):
    weights, refs = refs[:3], refs[3:]
    pieces, (normed_ref, mine_ref, other_ref, turned_ref, heads_ref) = refs[:-5], refs[-5:]
    spot, side, size = at_ref[0], at_ref[1], len(pieces)
    half = mine_ref.shape[0]
    token = tokens_ref[...].astype(f32)
    inverse = lax.rsqrt(jnp.mean(token * token, axis=1, keepdims=True) + epsilon)
    normed_ref[...] = (token * inverse * gain_ref[...]).astype(bf16)
    cosine, sine = cosine_ref[...], sine_ref[...]
    width = size * HEAD
    for which, weight in enumerate(weights):
        turned = weight[...].astype(f32).T.astype(bf16)
        turned_ref[which * width : (which + 1) * width, :] = turned
        product = dot(turned, normed_ref[...], 1, 1)
        for head in range(size):
            rows = product[head * HEAD : (head + 1) * HEAD, :]
            if which < 2:
                front, back = rows[: HEAD // 2, :], rows[HEAD // 2 :, :]
                rows = jnp.concatenate(
                    [front * cosine - back * sine, back * cosine + front * sine], axis=0
                )
            rows = rows.astype(bf16)
            if which == 0:
                rows = rows * bf16(HEAD**-0.5)
            heads_ref[head, which * HEAD : (which + 1) * HEAD, :] = rows
    for step, piece in enumerate(pieces):
        piece[...] = heads_ref[lax.rem(spot + step, size)]
    mine_ref[...] = normed_ref[rows_at(side, half), :]
    other_ref[...] = normed_ref[rows_at(1 - side, half), :]


def feed_kernel(side_ref, mixed_ref, tokens_ref, cotangent_ref, gain_ref, *refs):
    output_mine, output_other, gate_mine, up_mine, down_mine, both_other, down_other, *refs = refs
    grad_ref, low_ref, out_ref, normed_ref, middle_ref, *kept, output_ref = refs
    side = side_ref[0]
    half, features = low_ref.shape
    block = 256
    size = output_mine.shape[0] // HEAD
    for index in range(size):
        rows = slice(index * HEAD, (index + 1) * HEAD)
        output_ref[rows_at(2 * index + side, HEAD), :] = output_mine[rows, :]
        output_ref[rows_at(2 * index + 1 - side, HEAD), :] = output_other[rows, :]
    middle_ref[...] = jnp.zeros_like(middle_ref)
    parts = (
        (gate_mine, slice(0, features), up_mine, slice(0, features), down_mine, kept[:3]),
        (both_other, slice(0, features), both_other, slice(features, 2 * features), down_other, kept[3:]),
    )

    def step(index, unused):
        rows = rows_at(index, block)
        far = pl.ds(pl.multiple_of(side * half + index * block, block), block)
        token, cotangent = tokens_ref[far, :].astype(f32), cotangent_ref[far, :]
        hidden = token + dot(mixed_ref[:, rows], output_ref[...], 0, 0)
        inverse = lax.rsqrt(jnp.mean(hidden * hidden, axis=1, keepdims=True) + epsilon)
        gain = gain_ref[...]
        normed = (hidden * inverse * gain).astype(bf16)
        normed_ref[rows, :] = normed
        output_rows, grad_second = hidden, None
        for gate, gate_at, up, up_at, down, (keep_gate, keep_up, keep_active) in parts:
            gate_rows = dot(normed, gate[gate_at, :], 1, 0)
            upward = dot(normed, up[up_at, :], 1, 0)
            sigmoid_gate = jax.nn.sigmoid(gate_rows)
            silu_gate = gate_rows * sigmoid_gate
            activated = (silu_gate * upward).astype(bf16)
            keep_active[rows, :] = activated
            grad_act = dot(cotangent, down[...], 1, 1)
            grad_gate = (
                grad_act * upward * sigmoid_gate * (1.0 + gate_rows * (1.0 - sigmoid_gate))
            ).astype(bf16)
            keep_gate[rows, :] = grad_gate
            grad_up = (grad_act * silu_gate).astype(bf16)
            keep_up[rows, :] = grad_up
            output_rows = output_rows + dot(activated, down[...], 1, 0)
            term = dot(grad_gate, gate[gate_at, :], 1, 1) + dot(grad_up, up[up_at, :], 1, 1)
            grad_second = term if grad_second is None else grad_second + term
        out_ref[rows, :] = output_rows.astype(bf16)
        weighted = grad_second * gain
        inner = jnp.mean(weighted * hidden, axis=1, keepdims=True)
        low = (
            cotangent.astype(f32)
            + (inverse * weighted - hidden * (inverse * inverse * inverse) * inner)
        ).astype(bf16)
        low_ref[rows, :] = low
        middle = jnp.sum(grad_second * hidden * inverse, axis=0, keepdims=True)
        middle_ref[...] += jnp.broadcast_to(middle, middle_ref.shape)
        grad_mixed = dot(output_ref[...], low, 1, 1).astype(bf16)
        for head in range(2 * size):
            grad_ref[head, :, rows] = grad_mixed[head * HEAD : (head + 1) * HEAD, :]
        return 0

    lax.fori_loop(0, half // block, step, 0)


def feed_grad_kernel(at_ref, mixed_ref, cotangent_ref, low_ref, normed_ref, middle_ref, *refs):
    kept, (keep_ref, send_ref, rows_ref, mixed_grad_ref) = refs[:6], refs[6:]
    core, side = at_ref[0], at_ref[1]
    half, units = low_ref.shape[0], kept[0].shape[1]
    width = mixed_ref.shape[0] // 2
    size = width // HEAD
    mixed_grad_ref[...] = dot(mixed_ref[...], low_ref[...], 1, 0).astype(bf16)
    cotangent = cotangent_ref[rows_at(side, half), :]
    last = 3 * units + width
    rows_ref[last : last + 16, :] = jnp.broadcast_to(
        middle_ref[0:1, :], (16, middle_ref.shape[1])
    ).astype(bf16)
    rows_ref[last + 16 :, :] = jnp.zeros_like(rows_ref[last + 16 :, :])
    piece = keep_ref.shape[1]
    for which, of_side in ((0, side), (1, 1 - side)):
        grad_gate, grad_up, activated = kept[3 * which : 3 * which + 3]
        rows_ref[0:units, :] = dot(grad_gate[...], normed_ref[...], 0, 0).astype(bf16)
        rows_ref[units : 2 * units, :] = dot(grad_up[...], normed_ref[...], 0, 0).astype(bf16)
        rows_ref[2 * units : 3 * units, :] = dot(activated[...], cotangent, 0, 0).astype(bf16)
        for index in range(size):
            at = 3 * units + index * HEAD
            rows_ref[at : at + HEAD, :] = mixed_grad_ref[rows_at(2 * index + of_side, HEAD), :]
        keep_ref[which] = rows_ref[rows_at(core, piece), :]
        send_ref[which] = rows_ref[rows_at(1 - core, piece), :]


def add_low(left, right):
    return (left.astype(f32) + right.astype(f32)).astype(bf16)


def split_kernel(row_ref, keep_ref, arrived_ref, mine_ref, other_ref, keep_out, send_out):
    row, half, piece = row_ref[0], mine_ref.shape[0], keep_out.shape[1]
    mine_ref[...] = add_low(keep_ref[0, 0:half, :], arrived_ref[0, 0:half, :])
    other_ref[...] = add_low(keep_ref[1, 0:half, :], arrived_ref[1, 0:half, :])
    for out, at in ((keep_out, row), (send_out, 1 - row)):
        rows = pl.ds(pl.multiple_of(half + at * piece, piece), piece)
        for which in range(2):
            out[which] = add_low(keep_ref[which, rows, :], arrived_ref[which, rows, :])


def cross_kernel(row_ref, first_ref, first_in, second_ref, second_in, keep, send, mine, other):
    row, piece = row_ref[0], keep.shape[0]
    for out, at in ((keep, row), (send, 1 - row)):
        rows = rows_at(at, piece)
        out[...] = add_low(first_ref[rows, :], first_in[rows, :])
    mine[...] = add_low(second_ref[0], second_in[0])
    other[...] = add_low(second_ref[1], second_in[1])


def quarter_kernel(spot_ref, first_ref, first_in, second_ref, second_in, *outs):
    spot, size = spot_ref[0], len(outs)
    for step, out in enumerate(outs):
        rows = rows_at(lax.rem(spot + step, size), out.shape[1])
        out[0] = add_low(first_ref[rows, :], first_in[rows, :])
        out[1] = add_low(second_ref[rows, :], second_in[rows, :])


def total_kernel(*refs):
    total = refs[0][...].astype(f32)
    for ref in refs[1:-1]:
        total = total + ref[...].astype(f32)
    refs[-1][...] = total.astype(bf16)


def join_kernel(spot_ref, *refs):
    parts, out, spot = refs[:-1], refs[-1], spot_ref[0]
    for step, part in enumerate(parts):
        for which in range(2):
            rows = rows_at(lax.rem(spot - step + len(parts), len(parts)), part.shape[1])
            out[which, rows, :] = part[which]


def swap_tensor(array):
    return lax.ppermute(array, "tensor", [(0, 1), (1, 0)])


def swap_dp(array, bit):
    return lax.ppermute(array, "dp", [(index, index ^ bit) for index in range(4)])


def shift_ctx(array, step):
    size = lax.axis_size("ctx")
    return lax.ppermute(array, "ctx", [(index, (index + step) % size) for index in range(size)])


def hold(*arrays):
    return lax.optimization_barrier(arrays)


def head_shards(
    tokens,
    positions,
    norm_before,
    query_weight,
    key_weight,
    value_weight,
    output_weight,
    norm_middle,
    gate_weight,
    up_weight,
    down_weight,
    cotangent,
):
    tokens, positions, cotangent = tokens[0], positions[0], cotangent[0]
    size, spot, side = lax.axis_size("ctx"), lax.axis_index("ctx"), lax.axis_index("tensor")
    core, row = lax.axis_index("dp") % 2, lax.axis_index("dp") // 2
    count, features = tokens.shape
    half = count // 2
    length = count * size
    width = size * HEAD
    piece = 64 * size * (-(-(3 * gate_weight.shape[1] + width + 16) // (64 * size))) // (2 * size * 4)

    def array(*shape, dtype=bf16):
        return jax.ShapeDtypeStruct(shape, dtype)

    def scalars_of(*members):
        return (jnp.stack([member.astype(jnp.int32) for member in members]),)

    gate_up_other = swap_tensor(jnp.concatenate([gate_weight, up_weight], axis=0))

    straight = (positions[0] == spot * count) & (positions[half] == spot * count + half)

    def place_of(index, part):
        folded = jnp.where(part == 0, index, 2 * size - 1 - index)
        return jnp.where(straight, 2 * index + part, folded).astype(jnp.int32).reshape(-1)

    places = jnp.arange(2 * size)
    owner = jnp.where(straight, places // 2, jnp.minimum(places, 2 * size - 1 - places))
    owner_half = jnp.where(straight, places % 2, (places >= size).astype(jnp.int32))
    steps = jnp.arange(size)
    place_in = place_of(((spot - steps) % size)[:, None], jnp.arange(2)[None, :])
    place_grad = place_of(steps[:, None], jnp.arange(2)[None, :])
    slot = (2 * owner + owner_half).astype(jnp.int32)

    frequency = rope_base ** (-jnp.arange(HEAD // 2).astype(f32) * 2.0 / HEAD)
    angles = frequency[:, None] * positions.astype(f32)[None, :]
    cosine, sine = jnp.cos(angles), jnp.sin(angles)
    angles_all = frequency[:, None] * jnp.arange(length).astype(f32)[None, :]
    cosine_all, sine_all = jnp.cos(angles_all), jnp.sin(angles_all)

    gain_first, gain_second = norm_before.astype(f32)[None], norm_middle.astype(f32)[None]
    *pieces, normed_first, my_normed, other_normed, weights_turned = kernel_call(
        prepare_kernel,
        "prepare",
        tuple(array(3 * HEAD, count) for unused in range(size))
        + (
            array(count, features),
            array(half, features),
            array(half, features),
            array(3 * width, features),
        ),
        scalars_of(spot, side),
        tokens,
        gain_first,
        cosine,
        sine,
        query_weight,
        key_weight,
        value_weight,
        scratch=[pltpu.VMEM((size, 3 * HEAD, count), bf16)],
    )
    pieces = [pieces[0]] + [shift_ctx(pieces[step], step) for step in range(1, size)]
    *pieces, gate_up_other, output_mine, down_mine, my_normed = hold(
        *pieces, gate_up_other, output_weight, down_weight, my_normed
    )
    mixed_out, attended, log_total, everything = attend(place_in, slot, pieces)
    mixed_out, normed_one = hold(mixed_out, shift_ctx(my_normed, 1))

    def exchange(parts):
        return lax.all_to_all(parts, ("ctx", "tensor"), 0, 0, tiled=True)

    mixed, normed_one, output_other, down_other, normed_three, second_normed = hold(
        exchange(mixed_out).reshape(2 * width, half),
        normed_one,
        swap_tensor(output_mine),
        swap_tensor(down_mine),
        shift_ctx(my_normed, size - 1),
        my_normed,
    )
    units = gate_weight.shape[1]
    grad_mixed, hidden_low, output_half, normed_second, grad_middle, *kept = kernel_call(
        feed_kernel,
        "feed",
        (
            array(2 * size, HEAD, half),
            array(half, features),
            array(half, features),
            array(half, features),
            array(8, features, dtype=f32),
        )
        + tuple(array(half, units) for unused in range(6)),
        scalars_of(side),
        mixed,
        tokens,
        cotangent,
        gain_second,
        output_weight,
        output_other,
        gate_weight,
        up_weight,
        down_weight,
        gate_up_other,
        down_other,
        scratch=[pltpu.VMEM((2 * width, features), bf16)],
    )
    grad_pieces = exchange(grad_mixed)
    rows_keep, rows_send = kernel_call(
        feed_grad_kernel,
        "feed_grad",
        (array(2, 4 * size * piece, features), array(2, 4 * size * piece, features)),
        scalars_of(core, side),
        mixed,
        cotangent,
        hidden_low,
        normed_second,
        grad_middle,
        *kept,
        scratch=[
            pltpu.VMEM((8 * size * piece, features), bf16),
            pltpu.VMEM((2 * width, features), bf16),
        ],
    )
    scalars = (
        place_grad,
        ((owner - spot) % size).astype(jnp.int32),
        owner_half.astype(jnp.int32),
    )
    grad_pieces, rows_arrived, normed_two, other_one, other_three = hold(
        grad_pieces,
        swap_dp(rows_send, 1),
        shift_ctx(second_normed, 2),
        swap_tensor(normed_one),
        swap_tensor(normed_three),
    )
    strip = size * piece
    first_mine, first_other, second_keep, second_send = kernel_call(
        split_kernel,
        "split",
        (
            array(2 * strip, features),
            array(2 * strip, features),
            array(2, strip, features),
            array(2, strip, features),
        ),
        scalars_of(row),
        rows_keep,
        rows_arrived,
    )
    grad_pieces, first_other, second_send = hold(grad_pieces, first_other, second_send)
    query_sum, key_sum = attend_back(
        0, 2, scalars, grad_pieces, everything, attended, log_total
    )
    query_sum, key_sum, first_in, second_in, hidden_low = hold(
        query_sum, key_sum, swap_tensor(first_other), swap_dp(second_send, 2), hidden_low
    )
    first_keep, first_send, second_mine, second_other = kernel_call(
        cross_kernel,
        "cross",
        tuple(array(strip, features) for unused in range(4)),
        scalars_of(row),
        first_mine,
        first_in,
        second_keep,
        second_in,
    )
    query_sum, key_sum, first_send, second_other = hold(query_sum, key_sum, first_send, second_other)
    back_out = attend_back(
        2,
        2 * size,
        scalars,
        grad_pieces,
        everything,
        attended,
        log_total,
        query_sum,
        key_sum,
        cosine_all,
        sine_all,
    )
    back_out, first_in, second_in, other_two, low_arrived, output_half = hold(
        back_out,
        swap_dp(first_send, 2),
        swap_tensor(second_other),
        swap_tensor(normed_two),
        swap_tensor(hidden_low),
        output_half,
    )
    back = [back_out[0]] + [shift_ctx(back_out[step], step) for step in range(1, size)]
    spot_now = (spot.astype(jnp.int32)[None],)
    normed_halves = [my_normed, other_normed]
    normed_halves += [normed_one, other_one, normed_two, other_two, normed_three, other_three]
    head_grad = kernel_call(
        head_grad_kernel,
        "head_grad",
        jax.ShapeDtypeStruct((3 * HEAD, features), bf16),
        (side.astype(jnp.int32)[None],),
        back_out,
        *normed_halves,
    )
    head_grad, first_in, second_in = hold(head_grad, first_in, second_in)
    quarters = kernel_call(
        quarter_kernel,
        "quarter",
        tuple(array(2, piece, features) for unused in range(size)),
        spot_now,
        first_keep,
        first_in,
        second_mine,
        second_in,
    )
    quarters = [quarters[0]] + [shift_ctx(quarters[step], step) for step in range(1, size)]
    total = kernel_call(total_kernel, "total", array(2, piece, features), (), *quarters)
    head_grad = add_low(head_grad, swap_dp(head_grad, 1))
    head_grad = add_low(head_grad, swap_dp(head_grad, 2))
    *back, head_grad, total, output_arrived = hold(
        *back, head_grad, total, swap_tensor(output_half)
    )
    first_part = kernel_call(
        first_part_kernel,
        "first_part",
        jax.ShapeDtypeStruct((count, features), bf16),
        spot_now,
        *back,
        weights_turned,
        scratch=[pltpu.VMEM((3 * width, count), bf16)],
    )
    first_arrived = swap_tensor(first_part)
    grad_tokens, block_output = kernel_call(
        token_kernel,
        "grad_tokens",
        (
            jax.ShapeDtypeStruct((count, features), f32),
            jax.ShapeDtypeStruct((count, features), bf16),
        ),
        (side.astype(jnp.int32)[None],),
        first_part,
        first_arrived,
        tokens,
        gain_first,
        hidden_low,
        low_arrived,
        output_half,
        output_arrived,
    )

    rows = kernel_call(
        join_kernel,
        "join",
        array(2, strip, features),
        spot_now,
        total,
        *[shift_ctx(total, step) for step in range(1, size)],
    )
    across = swap_dp(rows, 2)
    grad_gate, grad_up, grad_down, grad_output, grad_middle = kernel_call(
        feed_out_kernel,
        "feed_out",
        (
            jax.ShapeDtypeStruct((features, units), f32),
            jax.ShapeDtypeStruct((features, units), f32),
            jax.ShapeDtypeStruct((units, features), f32),
            jax.ShapeDtypeStruct((width, features), f32),
            jax.ShapeDtypeStruct((16, features), f32),
        ),
        (jnp.stack([core, row]).astype(jnp.int32),),
        rows,
        across,
        swap_dp(rows, 1),
        swap_dp(across, 1),
        scratch=[pltpu.VMEM((8 * strip, features), bf16)],
    )
    heads_grads = [head_grad] + [shift_ctx(head_grad, step) for step in range(1, size)]
    grad_query, grad_key, grad_value, grad_before = kernel_call(
        first_out_kernel,
        "first_out",
        tuple(jax.ShapeDtypeStruct((features, width), f32) for unused in range(3))
        + (jax.ShapeDtypeStruct((8, features), f32),),
        spot_now,
        *heads_grads,
        weights_turned,
        scratch=[pltpu.VMEM((width, features), f32)],
    )
    grad_before = (grad_before[0] + swap_tensor(grad_before)[0]) / gain_first[0]
    grad_middle = grad_middle[0]
    return (
        block_output[None],
        grad_tokens[None],
        grad_before,
        grad_query,
        grad_key,
        grad_value,
        grad_output,
        grad_middle,
        grad_gate,
        grad_up,
        grad_down,
    )


def solution(mesh):
    sizes = dict(mesh.shape)

    def body(*arguments):
        local_heads = arguments[3].shape[1] // HEAD
        one_head = sizes["ctx"] == local_heads and sizes["tensor"] == 2 and sizes["dp"] == 4
        one_sequence = arguments[0].shape[0] == 1
        return (head_shards if one_head and one_sequence else shards)(*arguments)

    return jax.shard_map(
        body,
        mesh=mesh,
        in_specs=(
            P("dp", "ctx", None),
            P("dp", "ctx"),
            P(),
            P(None, "tensor"),
            P(None, "tensor"),
            P(None, "tensor"),
            P("tensor", None),
            P(),
            P(None, "tensor"),
            P(None, "tensor"),
            P("tensor", None),
            P("dp", "ctx", None),
        ),
        out_specs=(
            P("dp", "ctx", None),
            P("dp", "ctx", None),
            P(),
            P(None, "tensor"),
            P(None, "tensor"),
            P(None, "tensor"),
            P("tensor", None),
            P(),
            P(None, "tensor"),
            P(None, "tensor"),
            P("tensor", None),
        ),
        check_vma=False,
    )
```

```python
import functools
import math

import jax
import jax.numpy as jnp
from jax import lax
from jax.experimental import pallas as pl
from jax.experimental.pallas import tpu as pltpu
from jax.sharding import PartitionSpec as P

HEAD = 64


epsilon = 1e-05
rope_base = 10000.0
masked_score = -1e30


def rope_tables(positions):
    frequency = rope_base ** (-jnp.arange(HEAD // 2).astype(jnp.float32) * 2.0 / HEAD)
    angles = positions.astype(jnp.float32)[..., None] * frequency
    return (jnp.cos(angles), jnp.sin(angles))


def rotate(matrix, cosine_table, sine_table):
    shaped = matrix.reshape(matrix.shape[:-1] + (-1, HEAD))
    front_half = shaped[..., : HEAD // 2]
    back_half = shaped[..., HEAD // 2 :]
    cosine = cosine_table[..., None, :]
    sine_part = sine_table[..., None, :]
    turned = jnp.concatenate(
        [front_half * cosine - back_half * sine_part, back_half * cosine + front_half * sine_part],
        axis=-1,
    )
    return turned.reshape(matrix.shape)


def normalize(token_rows, gain_row):
    inverse_rms = lax.rsqrt(jnp.mean(token_rows * token_rows, axis=-1, keepdims=True) + epsilon)
    return (token_rows * inverse_rms * gain_row, inverse_rms)


def norm_back(token_rows, inverse_rms, gain_row, grad_normed):
    weighted = grad_normed * gain_row
    inner_sum = jnp.mean(weighted * token_rows, axis=-1, keepdims=True)
    grad_rows = (
        inverse_rms * weighted - token_rows * (inverse_rms * inverse_rms * inverse_rms) * inner_sum
    )
    grad_gain = jnp.sum(grad_normed * token_rows * inverse_rms, axis=(0, 1))
    return (grad_rows, grad_gain)


def project(left, weight):
    return jnp.einsum("sbd,dh->sbh", left, weight, preferred_element_type=jnp.float32)


def project_back(grad_rows, weight):
    return jnp.einsum("sbh,dh->sbd", grad_rows, weight, preferred_element_type=jnp.float32)


def outer_sum(left, right):
    return jnp.einsum("sbd,sbh->dh", left, right, preferred_element_type=jnp.float32)


def as_heads(matrix):
    return matrix.reshape(matrix.shape[:2] + (-1, HEAD))


def split_blocks(matrix, block_width):
    block_count = matrix.shape[1] // block_width
    shaped = matrix.reshape(matrix.shape[:1] + (block_count, block_width) + matrix.shape[2:])
    return jnp.moveaxis(shaped, 1, 0)


def join_blocks(stacked):
    joined = jnp.moveaxis(stacked, 0, 1)
    return joined.reshape((joined.shape[0], joined.shape[1] * joined.shape[2]) + joined.shape[3:])


def forward_fold(query_heads, query_pos, scale_factor, fold_state, incoming):
    key_part, value_part, key_pos = incoming
    block_width = math.gcd(key_part.shape[1], 512)
    blocks = (
        split_blocks(as_heads(key_part), block_width),
        split_blocks(as_heads(value_part), block_width),
        split_blocks(key_pos, block_width),
    )

    def forward_step_block(block_state, block_in):
        key_heads, value_heads, block_pos = block_in
        allowed = block_pos[:, None, None, :] <= query_pos[:, None, :, None]
        old_max, old_total, old_accum = block_state
        scores = (
            jnp.einsum(
                "sqhe,skhe->shqk", query_heads, key_heads, preferred_element_type=jnp.float32
            )
            * scale_factor
        )
        scores = jnp.where(allowed, scores, masked_score)
        new_max = jnp.maximum(old_max, jnp.max(scores, axis=-1))
        weights = jnp.where(allowed, jnp.exp(scores - new_max[..., None]), 0.0)
        factor = jnp.exp(old_max - new_max)
        new_total = old_total * factor + jnp.sum(weights, axis=-1)
        new_accum = old_accum * factor[..., None] + jnp.einsum(
            "shqk,skhe->shqe",
            weights.astype(jnp.bfloat16),
            value_heads,
            preferred_element_type=jnp.float32,
        )
        return ((new_max, new_total, new_accum), None)

    final_state, unused = lax.scan(forward_step_block, fold_state, blocks)
    return final_state


def gradient_fold(
    query_heads, query_pos, grad_heads, log_total, delta_heads, scale_factor, fold_state, incoming
):
    key_part, value_part, key_pos = incoming
    row_count = key_part.shape[1]
    block_width = math.gcd(row_count, 512)
    blocks = (
        split_blocks(as_heads(key_part), block_width),
        split_blocks(as_heads(value_part), block_width),
        split_blocks(key_pos, block_width),
    )

    def gradient_step_block(query_state, block_in):
        key_heads, value_heads, block_pos = block_in
        allowed = block_pos[:, None, None, :] <= query_pos[:, None, :, None]
        scores = (
            jnp.einsum(
                "sqhe,skhe->shqk", query_heads, key_heads, preferred_element_type=jnp.float32
            )
            * scale_factor
        )
        weights = jnp.where(allowed, jnp.exp(scores - log_total[..., None]), 0.0)
        grad_weights = jnp.einsum(
            "sqhe,skhe->shqk", grad_heads, value_heads, preferred_element_type=jnp.float32
        )
        grad_scores = (weights * (grad_weights - delta_heads[..., None])).astype(jnp.bfloat16)
        new_query = query_state + jnp.einsum(
            "shqk,skhe->shqe", grad_scores, key_heads, preferred_element_type=jnp.float32
        )
        key_grad = jnp.einsum(
            "shqk,sqhe->skhe", grad_scores, query_heads, preferred_element_type=jnp.float32
        )
        value_grad = jnp.einsum(
            "shqk,sqhe->skhe",
            weights.astype(jnp.bfloat16),
            grad_heads,
            preferred_element_type=jnp.float32,
        )
        return (new_query, (key_grad, value_grad))

    query_state, key_total, value_total = fold_state
    query_state, outputs = lax.scan(gradient_step_block, query_state, blocks)
    key_rows = join_blocks(outputs[0])
    value_rows = join_blocks(outputs[1])
    key_total = key_rows
    value_total = value_rows
    return (query_state, key_total, value_total)


def shards(
    tokens,
    positions,
    norm_before,
    query_weight,
    key_weight,
    value_weight,
    output_weight,
    norm_middle,
    gate_weight,
    up_weight,
    down_weight,
    cotangent,
):
    sequences = tokens.shape[0]
    block_rows = tokens.shape[1]
    local_heads = query_weight.shape[1] // HEAD
    scale_factor = HEAD ** (-0.5)
    cosine_table, sine_table = rope_tables(positions)
    token_rows = tokens.astype(jnp.float32)
    gain_first = norm_before.astype(jnp.float32)
    gain_second = norm_middle.astype(jnp.float32)
    normed_first, inverse_first = normalize(token_rows, gain_first)
    normed_first = normed_first.astype(jnp.bfloat16)
    query_rot = rotate(project(normed_first, query_weight), cosine_table, sine_table).astype(
        jnp.bfloat16
    )
    key_rot = rotate(project(normed_first, key_weight), cosine_table, sine_table).astype(
        jnp.bfloat16
    )
    value_rows = project(normed_first, value_weight).astype(jnp.bfloat16)
    query_heads = as_heads(query_rot)
    head_shape = (sequences, local_heads, block_rows)
    start_state = (
        jnp.full(head_shape, masked_score, jnp.float32),
        jnp.zeros(head_shape, jnp.float32),
        jnp.zeros(head_shape + (HEAD,), jnp.float32),
    )
    row_max, row_total, accum_heads = forward_fold(
        query_heads,
        positions,
        scale_factor,
        start_state,
        (
            lax.all_gather(key_rot, "ctx", axis=1, tiled=True),
            lax.all_gather(value_rows, "ctx", axis=1, tiled=True),
            lax.all_gather(positions, "ctx", axis=1, tiled=True),
        ),
    )
    log_total = row_max + jnp.log(row_total)
    mixed_heads = jnp.swapaxes(accum_heads / row_total[..., None], 1, 2)
    mixed_rows = mixed_heads.reshape(sequences, block_rows, -1).astype(jnp.bfloat16)
    hidden = token_rows + lax.psum(
        project(mixed_rows, output_weight).astype(jnp.bfloat16), "tensor"
    ).astype(jnp.float32)
    normed_second, inverse_second = normalize(hidden, gain_second)
    normed_second = normed_second.astype(jnp.bfloat16)
    gate_rows = project(normed_second, gate_weight)
    upward = project(normed_second, up_weight)
    sigmoid_gate = jax.nn.sigmoid(gate_rows)
    silu_gate = gate_rows * sigmoid_gate
    activated = (silu_gate * upward).astype(jnp.bfloat16)
    block_output = (
        hidden
        + lax.psum(project(activated, down_weight).astype(jnp.bfloat16), "tensor").astype(
            jnp.float32
        )
    ).astype(jnp.bfloat16)
    grad_down = outer_sum(activated, cotangent)
    grad_act = project_back(cotangent, down_weight)
    grad_gate_rows = (
        grad_act * upward * sigmoid_gate * (1.0 + gate_rows * (1.0 - sigmoid_gate))
    ).astype(jnp.bfloat16)
    grad_up_rows = (grad_act * silu_gate).astype(jnp.bfloat16)
    grad_gate = outer_sum(normed_second, grad_gate_rows)
    grad_up = outer_sum(normed_second, grad_up_rows)
    second_part = project_back(grad_gate_rows, gate_weight) + project_back(grad_up_rows, up_weight)
    grad_second = lax.psum(second_part.astype(jnp.bfloat16), "tensor").astype(jnp.float32)
    hidden_back, grad_middle = norm_back(hidden, inverse_second, gain_second, grad_second)
    grad_hidden = cotangent.astype(jnp.float32) + hidden_back
    hidden_low = grad_hidden.astype(jnp.bfloat16)
    grad_output = outer_sum(mixed_rows, hidden_low)
    grad_mixed = project_back(hidden_low, output_weight).astype(jnp.bfloat16)
    grad_heads = as_heads(grad_mixed)
    delta_rows = jnp.sum(grad_heads.astype(jnp.float32) * mixed_heads, axis=-1)
    delta_heads = jnp.swapaxes(delta_rows, 1, 2)
    query_start = jnp.zeros(head_shape + (HEAD,), jnp.float32)
    whole_rows = block_rows * lax.axis_size("ctx")
    key_start = jnp.zeros((sequences, whole_rows, local_heads, HEAD), jnp.float32)
    query_sum, key_total, value_total = gradient_fold(
        query_heads,
        positions,
        grad_heads,
        log_total,
        delta_heads,
        scale_factor,
        (query_start, key_start, key_start),
        (
            lax.all_gather(key_rot, "ctx", axis=1, tiled=True),
            lax.all_gather(value_rows, "ctx", axis=1, tiled=True),
            lax.all_gather(positions, "ctx", axis=1, tiled=True),
        ),
    )
    key_sum, value_sum = (
        lax.psum_scatter(
            key_total.astype(jnp.bfloat16), "ctx", scatter_dimension=1, tiled=True
        ).astype(jnp.float32),
        lax.psum_scatter(
            value_total.astype(jnp.bfloat16), "ctx", scatter_dimension=1, tiled=True
        ).astype(jnp.float32),
    )
    query_back = rotate(
        jnp.swapaxes(query_sum, 1, 2).reshape(sequences, block_rows, -1) * scale_factor,
        cosine_table,
        -sine_table,
    ).astype(jnp.bfloat16)
    key_back = rotate(
        key_sum.reshape(sequences, block_rows, -1) * scale_factor, cosine_table, -sine_table
    ).astype(jnp.bfloat16)
    value_back = value_sum.reshape(sequences, block_rows, -1).astype(jnp.bfloat16)
    grad_query = outer_sum(normed_first, query_back)
    grad_key = outer_sum(normed_first, key_back)
    grad_value = outer_sum(normed_first, value_back)
    first_part = (
        project_back(query_back, query_weight)
        + project_back(key_back, key_weight)
        + project_back(value_back, value_weight)
    )
    grad_first = lax.psum(first_part.astype(jnp.bfloat16), "tensor").astype(jnp.float32)
    rows_back, grad_before = norm_back(token_rows, inverse_first, gain_first, grad_first)
    grad_tokens = grad_hidden + rows_back
    results = lax.psum(
        (
            grad_before,
            grad_query,
            grad_key,
            grad_value,
            grad_output,
            grad_middle,
            grad_gate,
            grad_up,
            grad_down,
        ),
        ("dp", "ctx"),
    )
    return (
        block_output,
        grad_tokens,
        results[0],
        results[1],
        results[2],
        results[3],
        results[4],
        results[5],
        results[6],
        results[7],
        results[8],
    )


f32, bf16 = jnp.float32, jnp.bfloat16


def dot(left, right, left_dim, right_dim):
    return lax.dot_general(
        left, right, (((left_dim,), (right_dim,)), ((), ())), preferred_element_type=f32
    )


def attend_kernel(block, place_ref, slot_ref, *refs):
    pieces = refs[:4]
    out_ref, attended_ref, log_ref, all_ref, key_ref, value_ref = refs[4:]
    half = pieces[0].shape[1] // 2
    length = all_ref.shape[1]
    for index, piece in enumerate(pieces):
        for side in range(2):
            columns = pl.ds(pl.multiple_of(place_ref[2 * index + side] * half, half), half)
            part = piece[:, side * half : (side + 1) * half]
            all_ref[:, columns] = part
            key_ref[columns, :] = part[HEAD : 2 * HEAD, :].astype(f32).T.astype(bf16)
            value_ref[0:HEAD, columns] = part[2 * HEAD :, :]
    value_ref[HEAD:, :] = jnp.ones((value_ref.shape[0] - HEAD, length), bf16)

    def query_step(query_index, unused):
        columns = pl.ds(pl.multiple_of(query_index * block, block), block)
        queries = all_ref[0:HEAD, columns]

        def key_step(key_index, state, diagonal=False):
            old_max, accum = state
            rows = pl.ds(pl.multiple_of(key_index * block, block), block)
            scores = dot(key_ref[rows, :], queries, 1, 0)
            if diagonal:
                key_at = lax.broadcasted_iota(jnp.int32, (block, block), 0)
                query_at = lax.broadcasted_iota(jnp.int32, (block, block), 1)
                scores = jnp.where(key_at <= query_at, scores, masked_score)
            new_max = jnp.maximum(old_max, jnp.max(scores, axis=0, keepdims=True))
            weights = jnp.exp(scores - new_max).astype(bf16)
            accum = accum * jnp.exp(old_max - new_max) + dot(value_ref[:, rows], weights, 1, 0)
            return new_max, accum

        state = (
            jnp.full((1, block), masked_score, f32),
            jnp.zeros((value_ref.shape[0], block), f32),
        )
        state = lax.fori_loop(0, query_index, key_step, state)
        row_max, accum = key_step(query_index, state, True)
        total = accum[HEAD : HEAD + 1, :]
        mixed = accum[0:HEAD, :] / total
        attended_ref[:, columns] = mixed
        log_ref[:, columns] = jnp.broadcast_to(row_max + jnp.log(total), (8, block))
        for side in range(block // half):
            slot = slot_ref[query_index * (block // half) + side]
            out_ref[slot] = mixed[:, side * half : (side + 1) * half].astype(bf16)
        return 0

    lax.fori_loop(0, length // block, query_step, 0)


def gradient_kernel(block, first, last, place_ref, send_ref, side_ref, *refs):
    pieces_ref, all_ref, attended_ref, log_ref, *refs = refs
    half = pieces_ref.shape[2]
    length = all_ref.shape[1]
    ends = last == length // block
    if first:
        query_in_ref, key_in_ref, *refs = refs
    if ends:
        cosine_ref, sine_ref, out_ref, *refs = refs
        key_ref, value_ref, grad_ref, delta_ref, query_sum_ref, key_sum_ref = refs
    else:
        query_sum_ref, key_sum_ref, key_ref, value_ref, grad_ref, delta_ref = refs
    if first:
        query_sum_ref[...] = query_in_ref[...]
        done = pl.ds(0, first * block)
        key_sum_ref[:, done] = key_in_ref[:, done]
    else:
        query_sum_ref[...] = jnp.zeros_like(query_sum_ref)
    for index in range(pieces_ref.shape[0]):
        columns = pl.ds(pl.multiple_of(place_ref[index] * half, half), half)
        grad = pieces_ref[index]
        grad_ref[:, columns] = grad
        delta = jnp.sum(grad.astype(f32) * attended_ref[:, columns], axis=0, keepdims=True)
        delta_ref[:, columns] = jnp.broadcast_to(delta, (8, half))
    for index in range(first, last):
        columns = pl.ds(index * block, block)
        key_ref[columns, :] = all_ref[HEAD : 2 * HEAD, columns].astype(f32).T.astype(bf16)
        value_ref[columns, :] = all_ref[2 * HEAD :, columns].astype(f32).T.astype(bf16)

    def key_step(key_index, unused):
        rows = pl.ds(pl.multiple_of(key_index * block, block), block)
        keys = key_ref[rows, :]
        values = value_ref[rows, :]
        keys_turned = all_ref[HEAD : 2 * HEAD, rows]

        def query_step(query_index, state, diagonal=False):
            key_sum, value_sum = state
            columns = pl.ds(pl.multiple_of(query_index * block, block), block)
            queries = all_ref[0:HEAD, columns]
            grads = grad_ref[:, columns]
            scores = dot(keys, queries, 1, 0) - log_ref[0:1, columns]
            if diagonal:
                key_at = lax.broadcasted_iota(jnp.int32, (block, block), 0)
                query_at = lax.broadcasted_iota(jnp.int32, (block, block), 1)
                scores = jnp.where(key_at <= query_at, scores, masked_score)
            weights = jnp.exp(scores)
            grad_weights = dot(values, grads, 1, 0) - delta_ref[0:1, columns]
            grad_scores = (weights * grad_weights).astype(bf16)
            value_sum = value_sum + dot(grads, weights.astype(bf16), 1, 1)
            key_sum = key_sum + dot(queries, grad_scores, 1, 1)
            query_sum_ref[:, columns] += dot(keys_turned, grad_scores, 1, 0)
            return key_sum, value_sum

        state = (jnp.zeros((HEAD, block), f32), jnp.zeros((HEAD, block), f32))
        state = query_step(key_index, state, True)
        key_sum, value_sum = lax.fori_loop(key_index + 1, length // block, query_step, state)
        key_sum_ref[0:HEAD, rows] = key_sum
        key_sum_ref[HEAD:, rows] = value_sum
        return 0

    lax.fori_loop(first, last, key_step, 0)
    if not ends:
        return

    def turn_back(rows, cosine, sine):
        front, back = rows[: HEAD // 2, :], rows[HEAD // 2 :, :]
        return jnp.concatenate([front * cosine + back * sine, back * cosine - front * sine], axis=0)

    def write_step(index, unused):
        columns = pl.ds(pl.multiple_of(index * half, half), half)
        cosine, sine = cosine_ref[:, columns], sine_ref[:, columns]
        to = send_ref[index]
        at = pl.ds(pl.multiple_of(side_ref[index] * half, half), half)
        query_rows = query_sum_ref[:, columns] * (HEAD**-0.5)
        out_ref[to, 0:HEAD, at] = turn_back(query_rows, cosine, sine).astype(bf16)
        out_ref[to, HEAD : 2 * HEAD, at] = turn_back(
            key_sum_ref[0:HEAD, columns], cosine, sine
        ).astype(bf16)
        out_ref[to, 2 * HEAD :, at] = key_sum_ref[HEAD:, columns].astype(bf16)
        return 0

    lax.fori_loop(0, length // half, write_step, 0)


def attend(place, slot, pieces):
    rows, width = pieces[0].shape
    half, length = width // 2, width * len(pieces)
    smem, vmem = pl.BlockSpec(memory_space=pltpu.SMEM), pl.BlockSpec(memory_space=pltpu.VMEM)
    return pl.pallas_call(
        functools.partial(attend_kernel, width),
        out_shape=(
            jax.ShapeDtypeStruct((2 * len(pieces), HEAD, half), bf16),
            jax.ShapeDtypeStruct((HEAD, length), f32),
            jax.ShapeDtypeStruct((8, length), f32),
            jax.ShapeDtypeStruct((rows, length), bf16),
        ),
        in_specs=[smem] * 2 + [vmem] * 4,
        out_specs=[vmem] * 4,
        scratch_shapes=[pltpu.VMEM((length, HEAD), bf16), pltpu.VMEM((HEAD + 16, length), bf16)],
        compiler_params=pltpu.CompilerParams(vmem_limit_bytes=60 << 20),
        cost_estimate=pl.CostEstimate(flops=10**6, bytes_accessed=10**4, transcendentals=0),
        name="attend",
    )(place, slot, *pieces)


def attend_back(first, last, scalars, pieces, everything, attended, log_total, *sums):
    half = pieces.shape[2]
    rows, length = everything.shape
    smem, vmem = pl.BlockSpec(memory_space=pltpu.SMEM), pl.BlockSpec(memory_space=pltpu.VMEM)
    totals = [(HEAD, length), (2 * HEAD, length)]
    scratch = [
        pltpu.VMEM((length, HEAD), bf16),
        pltpu.VMEM((length, HEAD), bf16),
        pltpu.VMEM((HEAD, length), bf16),
        pltpu.VMEM((8, length), f32),
    ]
    ends = last == length // half
    if ends:
        out_shape = jax.ShapeDtypeStruct((length // (2 * half), rows, 2 * half), bf16)
        scratch = scratch + [pltpu.VMEM(shape, f32) for shape in totals]
    else:
        out_shape = tuple(jax.ShapeDtypeStruct(shape, f32) for shape in totals)
    return pl.pallas_call(
        functools.partial(gradient_kernel, half, first, last),
        out_shape=out_shape,
        in_specs=[smem] * 3 + [vmem] * (4 + len(sums)),
        out_specs=vmem if ends else (vmem, vmem),
        scratch_shapes=scratch,
        compiler_params=pltpu.CompilerParams(vmem_limit_bytes=30 << 20),
        cost_estimate=pl.CostEstimate(flops=10**6, bytes_accessed=10**4, transcendentals=0),
        name="attend_back",
    )(*scalars, pieces, everything, attended, log_total, *sums)


SMEM, VMEM = pl.BlockSpec(memory_space=pltpu.SMEM), pl.BlockSpec(memory_space=pltpu.VMEM)


def kernel_call(kernel, name, out_shape, scalars, *arrays, scratch=(), vmem=16, micros=0):
    return pl.pallas_call(
        kernel,
        out_shape=out_shape,
        in_specs=[SMEM] * len(scalars) + [VMEM] * len(arrays),
        out_specs=jax.tree.map(lambda unused: VMEM, out_shape),
        scratch_shapes=list(scratch),
        compiler_params=pltpu.CompilerParams(vmem_limit_bytes=vmem << 20),
        cost_estimate=pl.CostEstimate(
            flops=10**6 + micros * 10**9, bytes_accessed=10**4, transcendentals=0
        ),
        name=name,
    )(*scalars, *arrays)


def rows_at(index, count):
    return pl.ds(pl.multiple_of(index * count, count), count)


def token_kernel(side_ref, mine_ref, arrived_ref, tokens_ref, gain_ref, *refs):
    pair_mine, pair_arrived, grad_ref, output_ref = refs
    side = side_ref[0]
    half = pair_mine.shape[1]
    gain = gain_ref[...]
    for index, pair in ((side, pair_mine), (1 - side, pair_arrived)):
        rows = rows_at(index, half)
        grad = mine_ref[rows, :].astype(f32) + arrived_ref[rows, :].astype(f32)
        token = tokens_ref[rows, :].astype(f32)
        inverse = lax.rsqrt(jnp.mean(token * token, axis=1, keepdims=True) + epsilon)
        weighted = grad * gain
        inner = jnp.mean(weighted * token, axis=1, keepdims=True)
        grad_ref[rows, :] = pair[0].astype(f32) + (
            inverse * weighted - token * (inverse * inverse * inverse) * inner
        )
        output_ref[rows, :] = pair[1]


def head_grad_kernel(at_ref, back_ref, weight_ref, *refs):
    *normed, keep_ref, send_ref, sum_ref = refs
    side, core, spot, size = at_ref[0], at_ref[1], at_ref[2], back_ref.shape[0]
    half = back_ref.shape[2] // 2
    total = None
    for step in range(size):
        for place, rows in ((side, normed[2 * step]), (1 - side, normed[2 * step + 1])):
            term = dot(back_ref[(size - step) % size, :, rows_at(place, half)], rows[...], 1, 0)
            total = term if total is None else total + term
    sum_ref[...] = total.astype(bf16)
    before = jnp.zeros((1, total.shape[1]), f32)
    for which in range(3):
        weight = weight_ref[rows_at(which * size + spot, HEAD), :].astype(f32)
        grad = total[which * HEAD : (which + 1) * HEAD, :]
        before = before + jnp.sum(weight * grad, axis=0, keepdims=True)
    rows = total.shape[0] // 2
    for out, at in ((keep_ref, core), (send_ref, 1 - core)):
        out[0:rows, :] = sum_ref[rows_at(at, rows), :]
        out[rows:, :] = jnp.broadcast_to(before, (16, total.shape[1])).astype(bf16)


def first_part_kernel(spot_ref, *refs):
    size = len(refs) - 3
    parts, weight_ref, out_ref, rows_ref = refs[:size], refs[size], refs[size + 1], refs[size + 2]
    spot = spot_ref[0]
    for step, part in enumerate(parts):
        for which in range(3):
            at = which * size + lax.rem(spot - step + size, size)
            rows_ref[rows_at(at, HEAD), :] = part[which * HEAD : (which + 1) * HEAD, :]
    block = out_ref.shape[0] // 4
    for index in range(4):
        rows = slice(index * block, (index + 1) * block)
        out_ref[rows, :] = dot(rows_ref[:, rows], weight_ref[...], 0, 0).astype(bf16)


def prepare_kernel(at_ref, tokens_ref, gain_ref, cosine_ref, sine_ref, *refs):
    weights, refs = refs[:3], refs[3:]
    pieces, (normed_ref, mine_ref, other_ref, turned_ref, heads_ref) = refs[:-5], refs[-5:]
    spot, side, size = at_ref[0], at_ref[1], len(pieces)
    half = mine_ref.shape[0]
    token = tokens_ref[...].astype(f32)
    inverse = lax.rsqrt(jnp.mean(token * token, axis=1, keepdims=True) + epsilon)
    normed_ref[...] = (token * inverse * gain_ref[...]).astype(bf16)
    cosine, sine = cosine_ref[...], sine_ref[...]
    width = size * HEAD
    for which, weight in enumerate(weights):
        turned = weight[...].astype(f32).T.astype(bf16)
        turned_ref[which * width : (which + 1) * width, :] = turned
        product = dot(turned, normed_ref[...], 1, 1)
        for head in range(size):
            rows = product[head * HEAD : (head + 1) * HEAD, :]
            if which < 2:
                front, back = rows[: HEAD // 2, :], rows[HEAD // 2 :, :]
                rows = jnp.concatenate(
                    [front * cosine - back * sine, back * cosine + front * sine], axis=0
                )
            rows = rows.astype(bf16)
            if which == 0:
                rows = rows * bf16(HEAD**-0.5)
            heads_ref[head, which * HEAD : (which + 1) * HEAD, :] = rows
    for step, piece in enumerate(pieces):
        piece[...] = heads_ref[lax.rem(spot + step, size)]
    mine_ref[...] = normed_ref[rows_at(side, half), :]
    other_ref[...] = normed_ref[rows_at(1 - side, half), :]


def feed_kernel(side_ref, mixed_ref, tokens_ref, cotangent_ref, gain_ref, *refs):
    output_mine, gate_mine, up_mine, down_mine, other, *refs = refs
    grad_ref, pair_ref, normed_ref, middle_ref, *kept, output_ref = refs
    side = side_ref[0]
    half, features = normed_ref.shape
    block = 256
    size, units = output_mine.shape[0] // HEAD, gate_mine.shape[0]
    for index in range(size):
        at = index * HEAD
        output_ref[rows_at(2 * index + side, HEAD), :] = output_mine[at : at + HEAD, :]
        at = 3 * units + index * HEAD
        output_ref[rows_at(2 * index + 1 - side, HEAD), :] = other[at : at + HEAD, :]
    middle_ref[...] = jnp.zeros_like(middle_ref)
    parts = (
        (gate_mine, up_mine, down_mine, kept[:3]),
        tuple(other.at[at * units : (at + 1) * units, :] for at in range(3)) + (kept[3:],),
    )

    def step(index, unused):
        rows = rows_at(index, block)
        far = pl.ds(pl.multiple_of(side * half + index * block, block), block)
        token, cotangent = tokens_ref[far, :].astype(f32), cotangent_ref[far, :]
        hidden = token + dot(mixed_ref[:, rows], output_ref[...], 0, 0)
        inverse = lax.rsqrt(jnp.mean(hidden * hidden, axis=1, keepdims=True) + epsilon)
        gain = gain_ref[...]
        normed = (hidden * inverse * gain).astype(bf16)
        normed_ref[rows, :] = normed
        output_rows, grad_second = hidden, None
        for gate, up, down, (keep_gate, keep_up, keep_active) in parts:
            gate_rows = dot(normed, gate[...], 1, 1)
            upward = dot(normed, up[...], 1, 1)
            sigmoid_gate = jax.nn.sigmoid(gate_rows)
            silu_gate = gate_rows * sigmoid_gate
            activated = (silu_gate * upward).astype(bf16)
            keep_active[rows, :] = activated
            grad_act = dot(cotangent, down[...], 1, 1)
            grad_gate = (
                grad_act * upward * sigmoid_gate * (1.0 + gate_rows * (1.0 - sigmoid_gate))
            ).astype(bf16)
            keep_gate[rows, :] = grad_gate
            grad_up = (grad_act * silu_gate).astype(bf16)
            keep_up[rows, :] = grad_up
            output_rows = output_rows + dot(activated, down[...], 1, 0)
            term = dot(grad_gate, gate[...], 1, 0) + dot(grad_up, up[...], 1, 0)
            grad_second = term if grad_second is None else grad_second + term
        pair_ref[1, rows, :] = output_rows.astype(bf16)
        weighted = grad_second * gain
        inner = jnp.mean(weighted * hidden, axis=1, keepdims=True)
        low = (
            cotangent.astype(f32)
            + (inverse * weighted - hidden * (inverse * inverse * inverse) * inner)
        ).astype(bf16)
        pair_ref[0, rows, :] = low
        middle = jnp.sum(grad_second * hidden * inverse, axis=0, keepdims=True)
        middle_ref[...] += jnp.broadcast_to(middle, middle_ref.shape)
        grad_mixed = dot(output_ref[...], low, 1, 1).astype(bf16)
        for head in range(2 * size):
            grad_ref[head, :, rows] = grad_mixed[head * HEAD : (head + 1) * HEAD, :]
        return 0

    lax.fori_loop(0, half // block, step, 0)


def feed_grad_kernel(at_ref, mixed_ref, cotangent_ref, pair_ref, normed_ref, middle_ref, *refs):
    kept, (keep_ref, send_ref, rows_ref, mixed_grad_ref) = refs[:6], refs[6:]
    core, side = at_ref[0], at_ref[1]
    half, units = kept[0].shape
    width = mixed_ref.shape[0] // 2
    size = width // HEAD
    mixed_grad_ref[...] = dot(mixed_ref[...], pair_ref[0], 1, 0).astype(bf16)
    cotangent = cotangent_ref[rows_at(side, half), :]
    last = 3 * units + width
    rows_ref[last : last + 16, :] = jnp.broadcast_to(
        middle_ref[0:1, :], (16, middle_ref.shape[1])
    ).astype(bf16)
    rows_ref[last + 16 :, :] = jnp.zeros_like(rows_ref[last + 16 :, :])
    piece = keep_ref.shape[1]
    for which, of_side in ((0, side), (1, 1 - side)):
        grad_gate, grad_up, activated = kept[3 * which : 3 * which + 3]
        rows_ref[0:units, :] = dot(grad_gate[...], normed_ref[...], 0, 0).astype(bf16)
        rows_ref[units : 2 * units, :] = dot(grad_up[...], normed_ref[...], 0, 0).astype(bf16)
        rows_ref[2 * units : 3 * units, :] = dot(activated[...], cotangent, 0, 0).astype(bf16)
        for index in range(size):
            at = 3 * units + index * HEAD
            rows_ref[at : at + HEAD, :] = mixed_grad_ref[rows_at(2 * index + of_side, HEAD), :]
        keep_ref[which] = rows_ref[rows_at(core, piece), :]
        send_ref[which] = rows_ref[rows_at(1 - core, piece), :]


def add_low(left, right):
    return (left.astype(f32) + right.astype(f32)).astype(bf16)


def split_kernel(row_ref, keep_ref, arrived_ref, mine_ref, other_ref, keep_out, send_out):
    row, half, piece = row_ref[0], mine_ref.shape[0], keep_out.shape[1]
    mine_ref[...] = add_low(keep_ref[0, 0:half, :], arrived_ref[0, 0:half, :])
    other_ref[...] = add_low(keep_ref[1, 0:half, :], arrived_ref[1, 0:half, :])
    for out, at in ((keep_out, row), (send_out, 1 - row)):
        rows = pl.ds(pl.multiple_of(half + at * piece, piece), piece)
        for which in range(2):
            out[which] = add_low(keep_ref[which, rows, :], arrived_ref[which, rows, :])


def cross_kernel(row_ref, first_ref, first_in, second_ref, second_in, keep, send, mine, other):
    row, piece = row_ref[0], keep.shape[0]
    for out, at in ((keep, row), (send, 1 - row)):
        rows = rows_at(at, piece)
        out[...] = add_low(first_ref[rows, :], first_in[rows, :])
    mine[...] = add_low(second_ref[0], second_in[0])
    other[...] = add_low(second_ref[1], second_in[1])


def quarter_kernel(spot_ref, first_ref, first_in, second_ref, second_in, *outs):
    spot, size = spot_ref[0], len(outs)
    for step, out in enumerate(outs):
        rows = rows_at(lax.rem(spot + step, size), out.shape[1])
        out[0] = add_low(first_ref[rows, :], first_in[rows, :])
        out[1] = add_low(second_ref[rows, :], second_in[rows, :])


def total_kernel(*refs):
    *parts, head_ref, head_in, out_ref = refs
    total = parts[0][...].astype(f32)
    for part in parts[1:]:
        total = total + part[...].astype(f32)
    piece = total.shape[1]
    out_ref[0:piece, :] = total[0].astype(bf16)
    out_ref[piece : 2 * piece, :] = total[1].astype(bf16)
    out_ref[2 * piece :, :] = add_low(head_ref[...], head_in[...])


def head_split_kernel(row_ref, keep_ref, arrived_ref, keep_out, send_out):
    row, piece = row_ref[0], keep_out.shape[0] - 16
    for out, at in ((keep_out, row), (send_out, 1 - row)):
        rows = rows_at(at, piece)
        out[0:piece, :] = add_low(keep_ref[rows, :], arrived_ref[rows, :])
        out[piece:, :] = add_low(keep_ref[2 * piece :, :], arrived_ref[2 * piece :, :])


def finish_kernel(at_ref, *refs):
    parts, outs, (rows_ref, heads_ref) = refs[:16], refs[16:-2], refs[-2:]
    gate_ref, up_ref, down_ref, output_ref, middle_ref, *first_refs = outs
    spot, core, row = at_ref[0], at_ref[1], at_ref[2]
    size, quarter = heads_ref.shape[0], heads_ref.shape[1] // 4
    piece = (parts[0].shape[0] - quarter - 16) // 2
    for step in range(size):
        at = lax.rem(spot - step + size, size)
        for row_flip in range(2):
            for core_flip in range(2):
                part = parts[4 * step + 2 * row_flip + core_flip]
                row_at = 1 - row if row_flip else row
                core_at = 1 - core if core_flip else core
                for split in range(2):
                    place = (4 * core_at + 2 * split + row_at) * size + at
                    rows_ref[rows_at(place, piece), :] = part[split * piece : (split + 1) * piece, :]
                rows = rows_at(2 * core_at + row_at, quarter)
                heads_ref[at, rows, :] = part[2 * piece : 2 * piece + quarter, :]
    units, width = down_ref.shape[0], output_ref.shape[0]
    gate_ref[...] = rows_ref[0:units, :].astype(f32)
    up_ref[...] = rows_ref[units : 2 * units, :].astype(f32)
    down_ref[...] = rows_ref[2 * units : 3 * units, :].astype(f32)
    output_ref[...] = rows_ref[3 * units : 3 * units + width, :].astype(f32)
    last = 3 * units + width
    middle_ref[...] = rows_ref[last : last + 16, :].astype(f32)
    for which in range(3):
        rows = slice(which * HEAD, (which + 1) * HEAD)
        grad = jnp.concatenate([heads_ref[head, rows, :].astype(f32) for head in range(size)], axis=0)
        first_refs[which][...] = grad.T


def swap_tensor(array):
    return lax.ppermute(array, "tensor", [(0, 1), (1, 0)])


def swap_dp(array, bit):
    return lax.ppermute(array, "dp", [(index, index ^ bit) for index in range(4)])


def shift_ctx(array, step):
    size = lax.axis_size("ctx")
    return lax.ppermute(array, "ctx", [(index, (index + step) % size) for index in range(size)])


def hold(*arrays):
    return lax.optimization_barrier(arrays)


def head_shards(
    tokens,
    positions,
    norm_before,
    query_weight,
    key_weight,
    value_weight,
    output_weight,
    norm_middle,
    gate_weight,
    up_weight,
    down_weight,
    cotangent,
):
    tokens, positions, cotangent = tokens[0], positions[0], cotangent[0]
    size, spot, side = lax.axis_size("ctx"), lax.axis_index("ctx"), lax.axis_index("tensor")
    core, row = lax.axis_index("dp") % 2, lax.axis_index("dp") // 2
    count, features = tokens.shape
    half = count // 2
    length = count * size
    width = size * HEAD
    piece = 64 * size * (-(-(3 * gate_weight.shape[1] + width + 16) // (64 * size))) // (2 * size * 4)

    def array(*shape, dtype=bf16):
        return jax.ShapeDtypeStruct(shape, dtype)

    def scalars_of(*members):
        return (jnp.stack([member.astype(jnp.int32) for member in members]),)

    gate_turned, up_turned = gate_weight.T, up_weight.T
    weights_other = swap_tensor(
        jnp.concatenate([gate_turned, up_turned, down_weight, output_weight], axis=0)
    )

    straight = (positions[0] == spot * count) & (positions[half] == spot * count + half)

    def place_of(index, part):
        folded = jnp.where(part == 0, index, 2 * size - 1 - index)
        return jnp.where(straight, 2 * index + part, folded).astype(jnp.int32).reshape(-1)

    places = jnp.arange(2 * size)
    owner = jnp.where(straight, places // 2, jnp.minimum(places, 2 * size - 1 - places))
    owner_half = jnp.where(straight, places % 2, (places >= size).astype(jnp.int32))
    steps = jnp.arange(size)
    place_in = place_of(((spot - steps) % size)[:, None], jnp.arange(2)[None, :])
    place_grad = place_of(steps[:, None], jnp.arange(2)[None, :])
    slot = (2 * owner + owner_half).astype(jnp.int32)

    frequency = rope_base ** (-jnp.arange(HEAD // 2).astype(f32) * 2.0 / HEAD)
    angles = frequency[:, None] * positions.astype(f32)[None, :]
    cosine, sine = jnp.cos(angles), jnp.sin(angles)
    angles_all = frequency[:, None] * jnp.arange(length).astype(f32)[None, :]
    cosine_all, sine_all = jnp.cos(angles_all), jnp.sin(angles_all)

    gain_first, gain_second = norm_before.astype(f32)[None], norm_middle.astype(f32)[None]
    *pieces, normed_first, my_normed, other_normed, weights_turned = kernel_call(
        prepare_kernel,
        "prepare",
        tuple(array(3 * HEAD, count) for unused in range(size))
        + (
            array(count, features),
            array(half, features),
            array(half, features),
            array(3 * width, features),
        ),
        scalars_of(spot, side),
        tokens,
        gain_first,
        cosine,
        sine,
        query_weight,
        key_weight,
        value_weight,
        scratch=[pltpu.VMEM((size, 3 * HEAD, count), bf16)],
        vmem=60,
    )
    pieces = [pieces[0]] + [shift_ctx(pieces[step], step) for step in range(1, size)]
    *pieces, my_normed, cosine_all, sine_all = hold(*pieces, my_normed, cosine_all, sine_all)
    mixed_out, attended, log_total, everything = attend(place_in, slot, pieces)
    mixed_out, normed_two, first_normed = hold(mixed_out, shift_ctx(my_normed, 2), my_normed)

    def exchange(parts):
        return lax.all_to_all(parts, ("ctx", "tensor"), 0, 0, tiled=True)

    mixed, other_two, weights_other = hold(
        exchange(mixed_out).reshape(2 * width, half), swap_tensor(normed_two), weights_other
    )
    units = gate_weight.shape[1]
    grad_mixed, pair, normed_second, grad_middle, *kept = kernel_call(
        feed_kernel,
        "feed",
        (
            array(2 * size, HEAD, half),
            array(2, half, features),
            array(half, features),
            array(8, features, dtype=f32),
        )
        + tuple(array(half, units) for unused in range(6)),
        scalars_of(side),
        mixed,
        tokens,
        cotangent,
        gain_second,
        output_weight,
        gate_turned,
        up_turned,
        down_weight,
        weights_other,
        scratch=[pltpu.VMEM((2 * width, features), bf16)],
        vmem=36,
    )
    grad_pieces = exchange(grad_mixed)
    rows_keep, rows_send = kernel_call(
        feed_grad_kernel,
        "feed_grad",
        (array(2, 4 * size * piece, features), array(2, 4 * size * piece, features)),
        scalars_of(core, side),
        mixed,
        cotangent,
        pair,
        normed_second,
        grad_middle,
        *kept,
        scratch=[
            pltpu.VMEM((8 * size * piece, features), bf16),
            pltpu.VMEM((2 * width, features), bf16),
        ],
        vmem=34,
        micros=8,
    )
    scalars = (
        place_grad,
        ((owner - spot) % size).astype(jnp.int32),
        owner_half.astype(jnp.int32),
    )
    rows_arrived = swap_dp(rows_send, 1)
    strip = size * piece
    first_mine, first_other, second_keep, second_send = kernel_call(
        split_kernel,
        "split",
        (
            array(2 * strip, features),
            array(2 * strip, features),
            array(2, strip, features),
            array(2, strip, features),
        ),
        scalars_of(row),
        rows_keep,
        rows_arrived,
        micros=3,
    )
    grad_pieces, first_other, second_send, first_normed = hold(
        grad_pieces, first_other, second_send, first_normed
    )
    shared = (scalars, grad_pieces, everything, attended, log_total)
    query_sum, key_sum = attend_back(0, 2, *shared)
    query_sum, key_sum, first_in, second_in, normed_one, third_normed = hold(
        query_sum,
        key_sum,
        swap_tensor(first_other),
        swap_dp(second_send, 2),
        shift_ctx(first_normed, 1),
        first_normed,
    )
    first_keep, first_send, second_mine, second_other = kernel_call(
        cross_kernel,
        "cross",
        tuple(array(strip, features) for unused in range(4)),
        scalars_of(row),
        first_mine,
        first_in,
        second_keep,
        second_in,
    )
    query_sum, key_sum, first_send, second_other, normed_one = hold(
        query_sum, key_sum, first_send, second_other, normed_one
    )
    query_sum, key_sum = attend_back(2, 4, *shared, query_sum, key_sum)
    query_sum, key_sum, first_in, second_in, normed_three, other_one = hold(
        query_sum,
        key_sum,
        swap_dp(first_send, 2),
        swap_tensor(second_other),
        shift_ctx(third_normed, size - 1),
        swap_tensor(normed_one),
    )
    spot_now = scalars_of(spot)
    quarters = kernel_call(
        quarter_kernel,
        "quarter",
        tuple(array(2, piece, features) for unused in range(size)),
        spot_now,
        first_keep,
        first_in,
        second_mine,
        second_in,
    )
    query_sum, key_sum, normed_three, *quarters = hold(query_sum, key_sum, normed_three, *quarters)
    back_out = attend_back(4, 2 * size, *shared, query_sum, key_sum, cosine_all, sine_all)
    quarters = [quarters[0]] + [shift_ctx(quarters[step], step) for step in range(1, size)]
    back_out, other_three, pair, *quarters = hold(
        back_out, swap_tensor(normed_three), pair, *quarters
    )
    pair_arrived = swap_tensor(pair)
    back = [back_out[0]] + [shift_ctx(back_out[step], step) for step in range(1, size)]
    normed_halves = [my_normed, other_normed]
    normed_halves += [normed_one, other_one, normed_two, other_two, normed_three, other_three]
    head_keep, head_send = kernel_call(
        head_grad_kernel,
        "head_grad",
        (array(3 * HEAD // 2 + 16, features), array(3 * HEAD // 2 + 16, features)),
        scalars_of(side, core, spot),
        back_out,
        weights_turned,
        *normed_halves,
        scratch=[pltpu.VMEM((3 * HEAD, features), bf16)],
    )
    head_keep, head_send = kernel_call(
        head_split_kernel,
        "head_split",
        (array(3 * HEAD // 4 + 16, features), array(3 * HEAD // 4 + 16, features)),
        scalars_of(row),
        head_keep,
        swap_dp(head_send, 1),
    )
    total = kernel_call(
        total_kernel,
        "total",
        array(2 * piece + 3 * HEAD // 4 + 16, features),
        (),
        *quarters,
        head_keep,
        swap_dp(head_send, 2),
    )
    *back, total, pair_arrived = hold(*back, total, pair_arrived)
    first_part = kernel_call(
        first_part_kernel,
        "first_part",
        jax.ShapeDtypeStruct((count, features), bf16),
        spot_now,
        *back,
        weights_turned,
        scratch=[pltpu.VMEM((3 * width, count), bf16)],
    )
    first_part, total = hold(first_part, total)
    arrivals = [total] + [shift_ctx(total, step) for step in range(1, size)]
    first_arrived, *across = hold(
        swap_tensor(first_part), *[swap_dp(arrived, 2) for arrived in arrivals]
    )
    grad_tokens, block_output = kernel_call(
        token_kernel,
        "grad_tokens",
        (
            jax.ShapeDtypeStruct((count, features), f32),
            jax.ShapeDtypeStruct((count, features), bf16),
        ),
        (side.astype(jnp.int32)[None],),
        first_part,
        first_arrived,
        tokens,
        gain_first,
        pair,
        pair_arrived,
    )

    parts = []
    for arrived, other_row in zip(arrivals, across):
        parts += [arrived, swap_dp(arrived, 1), other_row, swap_dp(other_row, 1)]
    last = 2 * piece + 3 * HEAD // 4
    before = sum(arrived[last : last + 8].astype(f32) for arrived in arrivals)
    grad_before = (before[0] + swap_tensor(before)[0]) / gain_first[0]
    (
        grad_gate,
        grad_up,
        grad_down,
        grad_output,
        grad_middle,
        grad_query,
        grad_key,
        grad_value,
    ) = kernel_call(
        finish_kernel,
        "finish",
        (
            array(units, features, dtype=f32),
            array(units, features, dtype=f32),
            array(units, features, dtype=f32),
            array(width, features, dtype=f32),
            array(16, features, dtype=f32),
        )
        + tuple(array(features, width, dtype=f32) for unused in range(3)),
        scalars_of(spot, core, row),
        *parts,
        scratch=[
            pltpu.VMEM((8 * strip, features), bf16),
            pltpu.VMEM((size, 3 * HEAD, features), bf16),
        ],
        vmem=30,
    )
    grad_middle = grad_middle[0]
    grad_gate, grad_up = grad_gate.T, grad_up.T
    return (
        block_output[None],
        grad_tokens[None],
        grad_before,
        grad_query,
        grad_key,
        grad_value,
        grad_output,
        grad_middle,
        grad_gate,
        grad_up,
        grad_down,
    )


def solution(mesh):
    sizes = dict(mesh.shape)

    def body(*arguments):
        local_heads = arguments[3].shape[1] // HEAD
        one_head = sizes["ctx"] == local_heads and sizes["tensor"] == 2 and sizes["dp"] == 4
        one_sequence = arguments[0].shape[0] == 1
        return (head_shards if one_head and one_sequence else shards)(*arguments)

    return jax.shard_map(
        body,
        mesh=mesh,
        in_specs=(
            P("dp", "ctx", None),
            P("dp", "ctx"),
            P(),
            P(None, "tensor"),
            P(None, "tensor"),
            P(None, "tensor"),
            P("tensor", None),
            P(),
            P(None, "tensor"),
            P(None, "tensor"),
            P("tensor", None),
            P("dp", "ctx", None),
        ),
        out_specs=(
            P("dp", "ctx", None),
            P("dp", "ctx", None),
            P(),
            P(None, "tensor"),
            P(None, "tensor"),
            P(None, "tensor"),
            P("tensor", None),
            P(),
            P(None, "tensor"),
            P(None, "tensor"),
            P("tensor", None),
        ),
        check_vma=False,
    )
```

```python
import functools
import math

import jax
import jax.numpy as jnp
from jax import lax
from jax.experimental import pallas as pl
from jax.experimental.pallas import tpu as pltpu
from jax.sharding import PartitionSpec as P

HEAD = 64


epsilon = 1e-05
rope_base = 10000.0
masked_score = -1e30


def rope_tables(positions):
    frequency = rope_base ** (-jnp.arange(HEAD // 2).astype(jnp.float32) * 2.0 / HEAD)
    angles = positions.astype(jnp.float32)[..., None] * frequency
    return (jnp.cos(angles), jnp.sin(angles))


def rotate(matrix, cosine_table, sine_table):
    shaped = matrix.reshape(matrix.shape[:-1] + (-1, HEAD))
    front_half = shaped[..., : HEAD // 2]
    back_half = shaped[..., HEAD // 2 :]
    cosine = cosine_table[..., None, :]
    sine_part = sine_table[..., None, :]
    turned = jnp.concatenate(
        [front_half * cosine - back_half * sine_part, back_half * cosine + front_half * sine_part],
        axis=-1,
    )
    return turned.reshape(matrix.shape)


def normalize(token_rows, gain_row):
    inverse_rms = lax.rsqrt(jnp.mean(token_rows * token_rows, axis=-1, keepdims=True) + epsilon)
    return (token_rows * inverse_rms * gain_row, inverse_rms)


def norm_back(token_rows, inverse_rms, gain_row, grad_normed):
    weighted = grad_normed * gain_row
    inner_sum = jnp.mean(weighted * token_rows, axis=-1, keepdims=True)
    grad_rows = (
        inverse_rms * weighted - token_rows * (inverse_rms * inverse_rms * inverse_rms) * inner_sum
    )
    grad_gain = jnp.sum(grad_normed * token_rows * inverse_rms, axis=(0, 1))
    return (grad_rows, grad_gain)


def project(left, weight):
    return jnp.einsum("sbd,dh->sbh", left, weight, preferred_element_type=jnp.float32)


def project_back(grad_rows, weight):
    return jnp.einsum("sbh,dh->sbd", grad_rows, weight, preferred_element_type=jnp.float32)


def outer_sum(left, right):
    return jnp.einsum("sbd,sbh->dh", left, right, preferred_element_type=jnp.float32)


def as_heads(matrix):
    return matrix.reshape(matrix.shape[:2] + (-1, HEAD))


def split_blocks(matrix, block_width):
    block_count = matrix.shape[1] // block_width
    shaped = matrix.reshape(matrix.shape[:1] + (block_count, block_width) + matrix.shape[2:])
    return jnp.moveaxis(shaped, 1, 0)


def join_blocks(stacked):
    joined = jnp.moveaxis(stacked, 0, 1)
    return joined.reshape((joined.shape[0], joined.shape[1] * joined.shape[2]) + joined.shape[3:])


def forward_fold(query_heads, query_pos, scale_factor, fold_state, incoming):
    key_part, value_part, key_pos = incoming
    block_width = math.gcd(key_part.shape[1], 512)
    blocks = (
        split_blocks(as_heads(key_part), block_width),
        split_blocks(as_heads(value_part), block_width),
        split_blocks(key_pos, block_width),
    )

    def forward_step_block(block_state, block_in):
        key_heads, value_heads, block_pos = block_in
        allowed = block_pos[:, None, None, :] <= query_pos[:, None, :, None]
        old_max, old_total, old_accum = block_state
        scores = (
            jnp.einsum(
                "sqhe,skhe->shqk", query_heads, key_heads, preferred_element_type=jnp.float32
            )
            * scale_factor
        )
        scores = jnp.where(allowed, scores, masked_score)
        new_max = jnp.maximum(old_max, jnp.max(scores, axis=-1))
        weights = jnp.where(allowed, jnp.exp(scores - new_max[..., None]), 0.0)
        factor = jnp.exp(old_max - new_max)
        new_total = old_total * factor + jnp.sum(weights, axis=-1)
        new_accum = old_accum * factor[..., None] + jnp.einsum(
            "shqk,skhe->shqe",
            weights.astype(jnp.bfloat16),
            value_heads,
            preferred_element_type=jnp.float32,
        )
        return ((new_max, new_total, new_accum), None)

    final_state, unused = lax.scan(forward_step_block, fold_state, blocks)
    return final_state


def gradient_fold(
    query_heads, query_pos, grad_heads, log_total, delta_heads, scale_factor, fold_state, incoming
):
    key_part, value_part, key_pos = incoming
    row_count = key_part.shape[1]
    block_width = math.gcd(row_count, 512)
    blocks = (
        split_blocks(as_heads(key_part), block_width),
        split_blocks(as_heads(value_part), block_width),
        split_blocks(key_pos, block_width),
    )

    def gradient_step_block(query_state, block_in):
        key_heads, value_heads, block_pos = block_in
        allowed = block_pos[:, None, None, :] <= query_pos[:, None, :, None]
        scores = (
            jnp.einsum(
                "sqhe,skhe->shqk", query_heads, key_heads, preferred_element_type=jnp.float32
            )
            * scale_factor
        )
        weights = jnp.where(allowed, jnp.exp(scores - log_total[..., None]), 0.0)
        grad_weights = jnp.einsum(
            "sqhe,skhe->shqk", grad_heads, value_heads, preferred_element_type=jnp.float32
        )
        grad_scores = (weights * (grad_weights - delta_heads[..., None])).astype(jnp.bfloat16)
        new_query = query_state + jnp.einsum(
            "shqk,skhe->shqe", grad_scores, key_heads, preferred_element_type=jnp.float32
        )
        key_grad = jnp.einsum(
            "shqk,sqhe->skhe", grad_scores, query_heads, preferred_element_type=jnp.float32
        )
        value_grad = jnp.einsum(
            "shqk,sqhe->skhe",
            weights.astype(jnp.bfloat16),
            grad_heads,
            preferred_element_type=jnp.float32,
        )
        return (new_query, (key_grad, value_grad))

    query_state, key_total, value_total = fold_state
    query_state, outputs = lax.scan(gradient_step_block, query_state, blocks)
    key_rows = join_blocks(outputs[0])
    value_rows = join_blocks(outputs[1])
    key_total = key_rows
    value_total = value_rows
    return (query_state, key_total, value_total)


def shards(
    tokens,
    positions,
    norm_before,
    query_weight,
    key_weight,
    value_weight,
    output_weight,
    norm_middle,
    gate_weight,
    up_weight,
    down_weight,
    cotangent,
):
    sequences = tokens.shape[0]
    block_rows = tokens.shape[1]
    local_heads = query_weight.shape[1] // HEAD
    scale_factor = HEAD ** (-0.5)
    cosine_table, sine_table = rope_tables(positions)
    token_rows = tokens.astype(jnp.float32)
    gain_first = norm_before.astype(jnp.float32)
    gain_second = norm_middle.astype(jnp.float32)
    normed_first, inverse_first = normalize(token_rows, gain_first)
    normed_first = normed_first.astype(jnp.bfloat16)
    query_rot = rotate(project(normed_first, query_weight), cosine_table, sine_table).astype(
        jnp.bfloat16
    )
    key_rot = rotate(project(normed_first, key_weight), cosine_table, sine_table).astype(
        jnp.bfloat16
    )
    value_rows = project(normed_first, value_weight).astype(jnp.bfloat16)
    query_heads = as_heads(query_rot)
    head_shape = (sequences, local_heads, block_rows)
    start_state = (
        jnp.full(head_shape, masked_score, jnp.float32),
        jnp.zeros(head_shape, jnp.float32),
        jnp.zeros(head_shape + (HEAD,), jnp.float32),
    )
    row_max, row_total, accum_heads = forward_fold(
        query_heads,
        positions,
        scale_factor,
        start_state,
        (
            lax.all_gather(key_rot, "ctx", axis=1, tiled=True),
            lax.all_gather(value_rows, "ctx", axis=1, tiled=True),
            lax.all_gather(positions, "ctx", axis=1, tiled=True),
        ),
    )
    log_total = row_max + jnp.log(row_total)
    mixed_heads = jnp.swapaxes(accum_heads / row_total[..., None], 1, 2)
    mixed_rows = mixed_heads.reshape(sequences, block_rows, -1).astype(jnp.bfloat16)
    hidden = token_rows + lax.psum(
        project(mixed_rows, output_weight).astype(jnp.bfloat16), "tensor"
    ).astype(jnp.float32)
    normed_second, inverse_second = normalize(hidden, gain_second)
    normed_second = normed_second.astype(jnp.bfloat16)
    gate_rows = project(normed_second, gate_weight)
    upward = project(normed_second, up_weight)
    sigmoid_gate = jax.nn.sigmoid(gate_rows)
    silu_gate = gate_rows * sigmoid_gate
    activated = (silu_gate * upward).astype(jnp.bfloat16)
    block_output = (
        hidden
        + lax.psum(project(activated, down_weight).astype(jnp.bfloat16), "tensor").astype(
            jnp.float32
        )
    ).astype(jnp.bfloat16)
    grad_down = outer_sum(activated, cotangent)
    grad_act = project_back(cotangent, down_weight)
    grad_gate_rows = (
        grad_act * upward * sigmoid_gate * (1.0 + gate_rows * (1.0 - sigmoid_gate))
    ).astype(jnp.bfloat16)
    grad_up_rows = (grad_act * silu_gate).astype(jnp.bfloat16)
    grad_gate = outer_sum(normed_second, grad_gate_rows)
    grad_up = outer_sum(normed_second, grad_up_rows)
    second_part = project_back(grad_gate_rows, gate_weight) + project_back(grad_up_rows, up_weight)
    grad_second = lax.psum(second_part.astype(jnp.bfloat16), "tensor").astype(jnp.float32)
    hidden_back, grad_middle = norm_back(hidden, inverse_second, gain_second, grad_second)
    grad_hidden = cotangent.astype(jnp.float32) + hidden_back
    hidden_low = grad_hidden.astype(jnp.bfloat16)
    grad_output = outer_sum(mixed_rows, hidden_low)
    grad_mixed = project_back(hidden_low, output_weight).astype(jnp.bfloat16)
    grad_heads = as_heads(grad_mixed)
    delta_rows = jnp.sum(grad_heads.astype(jnp.float32) * mixed_heads, axis=-1)
    delta_heads = jnp.swapaxes(delta_rows, 1, 2)
    query_start = jnp.zeros(head_shape + (HEAD,), jnp.float32)
    whole_rows = block_rows * lax.axis_size("ctx")
    key_start = jnp.zeros((sequences, whole_rows, local_heads, HEAD), jnp.float32)
    query_sum, key_total, value_total = gradient_fold(
        query_heads,
        positions,
        grad_heads,
        log_total,
        delta_heads,
        scale_factor,
        (query_start, key_start, key_start),
        (
            lax.all_gather(key_rot, "ctx", axis=1, tiled=True),
            lax.all_gather(value_rows, "ctx", axis=1, tiled=True),
            lax.all_gather(positions, "ctx", axis=1, tiled=True),
        ),
    )
    key_sum, value_sum = (
        lax.psum_scatter(
            key_total.astype(jnp.bfloat16), "ctx", scatter_dimension=1, tiled=True
        ).astype(jnp.float32),
        lax.psum_scatter(
            value_total.astype(jnp.bfloat16), "ctx", scatter_dimension=1, tiled=True
        ).astype(jnp.float32),
    )
    query_back = rotate(
        jnp.swapaxes(query_sum, 1, 2).reshape(sequences, block_rows, -1) * scale_factor,
        cosine_table,
        -sine_table,
    ).astype(jnp.bfloat16)
    key_back = rotate(
        key_sum.reshape(sequences, block_rows, -1) * scale_factor, cosine_table, -sine_table
    ).astype(jnp.bfloat16)
    value_back = value_sum.reshape(sequences, block_rows, -1).astype(jnp.bfloat16)
    grad_query = outer_sum(normed_first, query_back)
    grad_key = outer_sum(normed_first, key_back)
    grad_value = outer_sum(normed_first, value_back)
    first_part = (
        project_back(query_back, query_weight)
        + project_back(key_back, key_weight)
        + project_back(value_back, value_weight)
    )
    grad_first = lax.psum(first_part.astype(jnp.bfloat16), "tensor").astype(jnp.float32)
    rows_back, grad_before = norm_back(token_rows, inverse_first, gain_first, grad_first)
    grad_tokens = grad_hidden + rows_back
    results = lax.psum(
        (
            grad_before,
            grad_query,
            grad_key,
            grad_value,
            grad_output,
            grad_middle,
            grad_gate,
            grad_up,
            grad_down,
        ),
        ("dp", "ctx"),
    )
    return (
        block_output,
        grad_tokens,
        results[0],
        results[1],
        results[2],
        results[3],
        results[4],
        results[5],
        results[6],
        results[7],
        results[8],
    )


f32, bf16 = jnp.float32, jnp.bfloat16


def dot(left, right, left_dim, right_dim):
    return lax.dot_general(
        left, right, (((left_dim,), (right_dim,)), ((), ())), preferred_element_type=f32
    )


def attend_kernel(block, place_ref, slot_ref, *refs):
    pieces = refs[:4]
    out_ref, attended_ref, log_ref, all_ref, key_ref, value_ref = refs[4:]
    half = pieces[0].shape[1] // 2
    length = all_ref.shape[1]
    for index, piece in enumerate(pieces):
        for side in range(2):
            columns = pl.ds(pl.multiple_of(place_ref[2 * index + side] * half, half), half)
            part = piece[:, side * half : (side + 1) * half]
            all_ref[:, columns] = part
            key_ref[columns, :] = part[HEAD : 2 * HEAD, :].astype(f32).T.astype(bf16)
            value_ref[0:HEAD, columns] = part[2 * HEAD :, :]
    value_ref[HEAD:, :] = jnp.ones((value_ref.shape[0] - HEAD, length), bf16)

    def query_step(query_index, unused):
        columns = pl.ds(pl.multiple_of(query_index * block, block), block)
        queries = all_ref[0:HEAD, columns]

        def key_step(key_index, state, diagonal=False):
            old_max, accum = state
            rows = pl.ds(pl.multiple_of(key_index * block, block), block)
            scores = dot(key_ref[rows, :], queries, 1, 0)
            if diagonal:
                key_at = lax.broadcasted_iota(jnp.int32, (block, block), 0)
                query_at = lax.broadcasted_iota(jnp.int32, (block, block), 1)
                scores = jnp.where(key_at <= query_at, scores, masked_score)
            new_max = jnp.maximum(old_max, jnp.max(scores, axis=0, keepdims=True))
            weights = jnp.exp(scores - new_max).astype(bf16)
            accum = accum * jnp.exp(old_max - new_max) + dot(value_ref[:, rows], weights, 1, 0)
            return new_max, accum

        state = (
            jnp.full((1, block), masked_score, f32),
            jnp.zeros((value_ref.shape[0], block), f32),
        )
        state = lax.fori_loop(0, query_index, key_step, state)
        row_max, accum = key_step(query_index, state, True)
        total = accum[HEAD : HEAD + 1, :]
        mixed = accum[0:HEAD, :] / total
        attended_ref[:, columns] = mixed
        log_ref[:, columns] = jnp.broadcast_to(row_max + jnp.log(total), (8, block))
        for side in range(block // half):
            slot = slot_ref[query_index * (block // half) + side]
            out_ref[slot] = mixed[:, side * half : (side + 1) * half].astype(bf16)
        return 0

    lax.fori_loop(0, length // block, query_step, 0)


def gradient_kernel(block, first, last, place_ref, send_ref, side_ref, *refs):
    pieces_ref, all_ref, attended_ref, log_ref, *refs = refs
    half = pieces_ref.shape[2]
    length = all_ref.shape[1]
    ends = last == length // block
    if first:
        query_in_ref, key_in_ref, *refs = refs
    if ends:
        cosine_ref, sine_ref, out_ref, *refs = refs
        key_ref, value_ref, grad_ref, delta_ref, query_sum_ref, key_sum_ref = refs
    else:
        query_sum_ref, key_sum_ref, key_ref, value_ref, grad_ref, delta_ref = refs
    if first:
        query_sum_ref[...] = query_in_ref[...]
        done = pl.ds(0, first * block)
        key_sum_ref[:, done] = key_in_ref[:, done]
    else:
        query_sum_ref[...] = jnp.zeros_like(query_sum_ref)
    for index in range(pieces_ref.shape[0]):
        columns = pl.ds(pl.multiple_of(place_ref[index] * half, half), half)
        grad = pieces_ref[index]
        grad_ref[:, columns] = grad
        delta = jnp.sum(grad.astype(f32) * attended_ref[:, columns], axis=0, keepdims=True)
        delta_ref[:, columns] = jnp.broadcast_to(delta, (8, half))
    for index in range(first, last):
        columns = pl.ds(index * block, block)
        key_ref[columns, :] = all_ref[HEAD : 2 * HEAD, columns].astype(f32).T.astype(bf16)
        value_ref[columns, :] = all_ref[2 * HEAD :, columns].astype(f32).T.astype(bf16)

    def key_step(key_index, unused):
        rows = pl.ds(pl.multiple_of(key_index * block, block), block)
        keys = key_ref[rows, :]
        values = value_ref[rows, :]
        keys_turned = all_ref[HEAD : 2 * HEAD, rows]

        def query_step(query_index, state, diagonal=False):
            key_sum, value_sum = state
            columns = pl.ds(pl.multiple_of(query_index * block, block), block)
            queries = all_ref[0:HEAD, columns]
            grads = grad_ref[:, columns]
            scores = dot(keys, queries, 1, 0) - log_ref[0:1, columns]
            if diagonal:
                key_at = lax.broadcasted_iota(jnp.int32, (block, block), 0)
                query_at = lax.broadcasted_iota(jnp.int32, (block, block), 1)
                scores = jnp.where(key_at <= query_at, scores, masked_score)
            weights = jnp.exp(scores)
            grad_weights = dot(values, grads, 1, 0) - delta_ref[0:1, columns]
            grad_scores = (weights * grad_weights).astype(bf16)
            value_sum = value_sum + dot(grads, weights.astype(bf16), 1, 1)
            key_sum = key_sum + dot(queries, grad_scores, 1, 1)
            query_sum_ref[:, columns] += dot(keys_turned, grad_scores, 1, 0)
            return key_sum, value_sum

        state = (jnp.zeros((HEAD, block), f32), jnp.zeros((HEAD, block), f32))
        state = query_step(key_index, state, True)
        key_sum, value_sum = lax.fori_loop(key_index + 1, length // block, query_step, state)
        key_sum_ref[0:HEAD, rows] = key_sum
        key_sum_ref[HEAD:, rows] = value_sum
        return 0

    lax.fori_loop(first, last, key_step, 0)
    if not ends:
        return

    def turn_back(rows, cosine, sine):
        front, back = rows[: HEAD // 2, :], rows[HEAD // 2 :, :]
        return jnp.concatenate([front * cosine + back * sine, back * cosine - front * sine], axis=0)

    def write_step(index, unused):
        columns = pl.ds(pl.multiple_of(index * half, half), half)
        cosine, sine = cosine_ref[:, columns], sine_ref[:, columns]
        to = send_ref[index]
        at = pl.ds(pl.multiple_of(side_ref[index] * half, half), half)
        query_rows = query_sum_ref[:, columns] * (HEAD**-0.5)
        out_ref[to, 0:HEAD, at] = turn_back(query_rows, cosine, sine).astype(bf16)
        out_ref[to, HEAD : 2 * HEAD, at] = turn_back(
            key_sum_ref[0:HEAD, columns], cosine, sine
        ).astype(bf16)
        out_ref[to, 2 * HEAD :, at] = key_sum_ref[HEAD:, columns].astype(bf16)
        return 0

    lax.fori_loop(0, length // half, write_step, 0)


def attend(place, slot, pieces):
    rows, width = pieces[0].shape
    half, length = width // 2, width * len(pieces)
    smem, vmem = pl.BlockSpec(memory_space=pltpu.SMEM), pl.BlockSpec(memory_space=pltpu.VMEM)
    return pl.pallas_call(
        functools.partial(attend_kernel, width),
        out_shape=(
            jax.ShapeDtypeStruct((2 * len(pieces), HEAD, half), bf16),
            jax.ShapeDtypeStruct((HEAD, length), f32),
            jax.ShapeDtypeStruct((8, length), f32),
            jax.ShapeDtypeStruct((rows, length), bf16),
        ),
        in_specs=[smem] * 2 + [vmem] * 4,
        out_specs=[vmem] * 4,
        scratch_shapes=[pltpu.VMEM((length, HEAD), bf16), pltpu.VMEM((HEAD + 16, length), bf16)],
        compiler_params=pltpu.CompilerParams(vmem_limit_bytes=60 << 20),
        cost_estimate=pl.CostEstimate(flops=10**6, bytes_accessed=10**4, transcendentals=0),
        name="attend",
    )(place, slot, *pieces)


def attend_back(first, last, scalars, pieces, everything, attended, log_total, *sums):
    half = pieces.shape[2]
    rows, length = everything.shape
    smem, vmem = pl.BlockSpec(memory_space=pltpu.SMEM), pl.BlockSpec(memory_space=pltpu.VMEM)
    totals = [(HEAD, length), (2 * HEAD, length)]
    scratch = [
        pltpu.VMEM((length, HEAD), bf16),
        pltpu.VMEM((length, HEAD), bf16),
        pltpu.VMEM((HEAD, length), bf16),
        pltpu.VMEM((8, length), f32),
    ]
    ends = last == length // half
    if ends:
        out_shape = jax.ShapeDtypeStruct((length // (2 * half), rows, 2 * half), bf16)
        scratch = scratch + [pltpu.VMEM(shape, f32) for shape in totals]
    else:
        out_shape = tuple(jax.ShapeDtypeStruct(shape, f32) for shape in totals)
    return pl.pallas_call(
        functools.partial(gradient_kernel, half, first, last),
        out_shape=out_shape,
        in_specs=[smem] * 3 + [vmem] * (4 + len(sums)),
        out_specs=vmem if ends else (vmem, vmem),
        scratch_shapes=scratch,
        compiler_params=pltpu.CompilerParams(vmem_limit_bytes=30 << 20),
        cost_estimate=pl.CostEstimate(flops=10**6, bytes_accessed=10**4, transcendentals=0),
        name="attend_back",
    )(*scalars, pieces, everything, attended, log_total, *sums)


SMEM, VMEM = pl.BlockSpec(memory_space=pltpu.SMEM), pl.BlockSpec(memory_space=pltpu.VMEM)


def kernel_call(kernel, name, out_shape, scalars, *arrays, scratch=(), vmem=16, micros=0):
    return pl.pallas_call(
        kernel,
        out_shape=out_shape,
        in_specs=[SMEM] * len(scalars) + [VMEM] * len(arrays),
        out_specs=jax.tree.map(lambda unused: VMEM, out_shape),
        scratch_shapes=list(scratch),
        compiler_params=pltpu.CompilerParams(vmem_limit_bytes=vmem << 20),
        cost_estimate=pl.CostEstimate(
            flops=10**6 + micros * 10**9, bytes_accessed=10**4, transcendentals=0
        ),
        name=name,
    )(*scalars, *arrays)


def rows_at(index, count):
    return pl.ds(pl.multiple_of(index * count, count), count)


def token_kernel(side_ref, mine_ref, arrived_ref, tokens_ref, gain_ref, *refs):
    low_mine, low_arrived, grad_ref = refs
    side = side_ref[0]
    half = low_mine.shape[0]
    gain = gain_ref[...].astype(f32)
    for index, low in ((side, low_mine), (1 - side, low_arrived)):
        rows = rows_at(index, half)
        grad = mine_ref[rows, :].astype(f32) + arrived_ref[rows, :].astype(f32)
        token = tokens_ref[rows, :].astype(f32)
        inverse = lax.rsqrt(jnp.mean(token * token, axis=1, keepdims=True) + epsilon)
        weighted = grad * gain
        inner = jnp.mean(weighted * token, axis=1, keepdims=True)
        grad_ref[rows, :] = low[...].astype(f32) + (
            inverse * weighted - token * (inverse * inverse * inverse) * inner
        )


def head_grad_kernel(at_ref, back_ref, weight_ref, *refs):
    *normed, keep_ref, send_ref, sum_ref = refs
    side, core, spot, size = at_ref[0], at_ref[1], at_ref[2], back_ref.shape[0]
    half = back_ref.shape[2] // 2
    total = None
    for step in range(size):
        for place, rows in ((side, normed[2 * step]), (1 - side, normed[2 * step + 1])):
            at = lax.rem(spot - step + size, size)
            term = dot(back_ref[at, :, rows_at(place, half)], rows[...], 1, 0)
            total = term if total is None else total + term
    sum_ref[...] = total.astype(bf16)
    before = jnp.zeros((1, total.shape[1]), f32)
    for which in range(3):
        weight = weight_ref[rows_at(which * size + spot, HEAD), :].astype(f32)
        grad = total[which * HEAD : (which + 1) * HEAD, :]
        before = before + jnp.sum(weight * grad, axis=0, keepdims=True)
    rows = total.shape[0] // 2
    for out, at in ((keep_ref, core), (send_ref, 1 - core)):
        out[0:rows, :] = sum_ref[rows_at(at, rows), :]
        out[rows:, :] = jnp.broadcast_to(before, (16, total.shape[1])).astype(bf16)


def first_part_kernel(back_ref, weight_ref, out_ref, rows_ref):
    size = back_ref.shape[0]
    for head in range(size):
        for which in range(3):
            at = (which * size + head) * HEAD
            rows_ref[at : at + HEAD, :] = back_ref[head, which * HEAD : (which + 1) * HEAD, :]
    block = out_ref.shape[0] // 4
    for index in range(4):
        rows = slice(index * block, (index + 1) * block)
        out_ref[rows, :] = dot(rows_ref[:, rows], weight_ref[...], 0, 0).astype(bf16)


def prepare_kernel(at_ref, tokens_ref, gain_ref, cosine_ref, sine_ref, *refs):
    weights, refs = refs[:3], refs[3:]
    pieces, (normed_ref, mine_ref, other_ref, turned_ref, heads_ref) = refs[:-5], refs[-5:]
    spot, side, size = at_ref[0], at_ref[1], len(pieces)
    half = mine_ref.shape[0]
    token = tokens_ref[...].astype(f32)
    inverse = lax.rsqrt(jnp.mean(token * token, axis=1, keepdims=True) + epsilon)
    normed_ref[...] = (token * inverse * gain_ref[...].astype(f32)).astype(bf16)
    cosine, sine = cosine_ref[...], sine_ref[...]
    width = size * HEAD
    for which, weight in enumerate(weights):
        turned = weight[...].astype(f32).T.astype(bf16)
        turned_ref[which * width : (which + 1) * width, :] = turned
        product = dot(turned, normed_ref[...], 1, 1)
        for head in range(size):
            rows = product[head * HEAD : (head + 1) * HEAD, :]
            if which < 2:
                front, back = rows[: HEAD // 2, :], rows[HEAD // 2 :, :]
                rows = jnp.concatenate(
                    [front * cosine - back * sine, back * cosine + front * sine], axis=0
                )
            rows = rows.astype(bf16)
            if which == 0:
                rows = rows * bf16(HEAD**-0.5)
            heads_ref[head, which * HEAD : (which + 1) * HEAD, :] = rows
    for step, piece in enumerate(pieces):
        piece[...] = heads_ref[lax.rem(spot + step, size)]
    mine_ref[...] = normed_ref[rows_at(side, half), :]
    other_ref[...] = normed_ref[rows_at(1 - side, half), :]


def output_kernel(side_ref, mine_ref, arrived_ref, output_ref):
    half = mine_ref.shape[0]
    output_ref[rows_at(side_ref[0], half), :] = mine_ref[...]
    output_ref[rows_at(1 - side_ref[0], half), :] = arrived_ref[...]


def feed_kernel(side_ref, mixed_ref, tokens_ref, cotangent_ref, gain_ref, *refs):
    output_mine, gate_mine, up_mine, down_mine, other, *refs = refs
    grad_ref, low_ref, out_ref, normed_ref, middle_ref, *kept, output_ref = refs
    side = side_ref[0]
    half, features = normed_ref.shape
    block = 256
    size, units = output_mine.shape[0] // HEAD, gate_mine.shape[0]
    for index in range(size):
        at = index * HEAD
        output_ref[rows_at(2 * index + side, HEAD), :] = output_mine[at : at + HEAD, :]
        at = 3 * units + index * HEAD
        output_ref[rows_at(2 * index + 1 - side, HEAD), :] = other[at : at + HEAD, :]
    middle_ref[...] = jnp.zeros_like(middle_ref)
    parts = (
        (gate_mine, up_mine, down_mine, kept[:3]),
        tuple(other.at[at * units : (at + 1) * units, :] for at in range(3)) + (kept[3:],),
    )

    def step(index, unused):
        rows = rows_at(index, block)
        far = pl.ds(pl.multiple_of(side * half + index * block, block), block)
        token, cotangent = tokens_ref[far, :].astype(f32), cotangent_ref[far, :]
        hidden = token + dot(mixed_ref[:, rows], output_ref[...], 0, 0)
        inverse = lax.rsqrt(jnp.mean(hidden * hidden, axis=1, keepdims=True) + epsilon)
        gain = gain_ref[...].astype(f32)
        normed = (hidden * inverse * gain).astype(bf16)
        normed_ref[rows, :] = normed
        output_rows, grad_second = hidden, None
        for gate, up, down, (keep_gate, keep_up, keep_active) in parts:
            gate_rows = dot(normed, gate[...], 1, 1)
            upward = dot(normed, up[...], 1, 1)
            sigmoid_gate = jax.nn.sigmoid(gate_rows)
            silu_gate = gate_rows * sigmoid_gate
            activated = (silu_gate * upward).astype(bf16)
            keep_active[rows, :] = activated
            grad_act = dot(cotangent, down[...], 1, 1)
            grad_gate = (
                grad_act * upward * sigmoid_gate * (1.0 + gate_rows * (1.0 - sigmoid_gate))
            ).astype(bf16)
            keep_gate[rows, :] = grad_gate
            grad_up = (grad_act * silu_gate).astype(bf16)
            keep_up[rows, :] = grad_up
            output_rows = output_rows + dot(activated, down[...], 1, 0)
            term = dot(grad_gate, gate[...], 1, 0) + dot(grad_up, up[...], 1, 0)
            grad_second = term if grad_second is None else grad_second + term
        out_ref[rows, :] = output_rows.astype(bf16)
        weighted = grad_second * gain
        inner = jnp.mean(weighted * hidden, axis=1, keepdims=True)
        low = (
            cotangent.astype(f32)
            + (inverse * weighted - hidden * (inverse * inverse * inverse) * inner)
        ).astype(bf16)
        low_ref[rows, :] = low
        middle = jnp.sum(grad_second * hidden * inverse, axis=0, keepdims=True)
        middle_ref[...] += jnp.broadcast_to(middle, middle_ref.shape)
        grad_mixed = dot(output_ref[...], low, 1, 1).astype(bf16)
        for head in range(2 * size):
            grad_ref[head, :, rows] = grad_mixed[head * HEAD : (head + 1) * HEAD, :]
        return 0

    lax.fori_loop(0, half // block, step, 0)


def feed_grad_kernel(at_ref, mixed_ref, cotangent_ref, low_ref, normed_ref, middle_ref, *refs):
    kept, (keep_ref, send_ref, rows_ref, mixed_grad_ref) = refs[:6], refs[6:]
    core, side = at_ref[0], at_ref[1]
    half, units = kept[0].shape
    width = mixed_ref.shape[0] // 2
    size = width // HEAD
    mixed_grad_ref[...] = dot(mixed_ref[...], low_ref[...], 1, 0).astype(bf16)
    cotangent = cotangent_ref[rows_at(side, half), :]
    last = 3 * units + width
    rows_ref[last : last + 16, :] = jnp.broadcast_to(
        middle_ref[0:1, :], (16, middle_ref.shape[1])
    ).astype(bf16)
    rows_ref[last + 16 :, :] = jnp.zeros_like(rows_ref[last + 16 :, :])
    piece = keep_ref.shape[1]
    for which, of_side in ((0, side), (1, 1 - side)):
        grad_gate, grad_up, activated = kept[3 * which : 3 * which + 3]
        rows_ref[0:units, :] = dot(grad_gate[...], normed_ref[...], 0, 0).astype(bf16)
        rows_ref[units : 2 * units, :] = dot(grad_up[...], normed_ref[...], 0, 0).astype(bf16)
        rows_ref[2 * units : 3 * units, :] = dot(activated[...], cotangent, 0, 0).astype(bf16)
        for index in range(size):
            at = 3 * units + index * HEAD
            rows_ref[at : at + HEAD, :] = mixed_grad_ref[rows_at(2 * index + of_side, HEAD), :]
        keep_ref[which] = rows_ref[rows_at(core, piece), :]
        send_ref[which] = rows_ref[rows_at(1 - core, piece), :]


def add_low(left, right):
    return (left.astype(f32) + right.astype(f32)).astype(bf16)


def split_kernel(row_ref, keep_ref, arrived_ref, mine_ref, other_ref, keep_out, send_out):
    row, half, piece = row_ref[0], mine_ref.shape[0], keep_out.shape[1]
    mine_ref[...] = add_low(keep_ref[0, 0:half, :], arrived_ref[0, 0:half, :])
    other_ref[...] = add_low(keep_ref[1, 0:half, :], arrived_ref[1, 0:half, :])
    for out, at in ((keep_out, row), (send_out, 1 - row)):
        rows = pl.ds(pl.multiple_of(half + at * piece, piece), piece)
        for which in range(2):
            out[which] = add_low(keep_ref[which, rows, :], arrived_ref[which, rows, :])


def cross_kernel(row_ref, first_ref, first_in, second_ref, second_in, keep, send, mine, other):
    row, piece = row_ref[0], keep.shape[0]
    for out, at in ((keep, row), (send, 1 - row)):
        rows = rows_at(at, piece)
        out[...] = add_low(first_ref[rows, :], first_in[rows, :])
    mine[...] = add_low(second_ref[0], second_in[0])
    other[...] = add_low(second_ref[1], second_in[1])


def quarter_kernel(spot_ref, first_ref, first_in, second_ref, second_in, *outs):
    spot, size = spot_ref[0], len(outs)
    for step, out in enumerate(outs):
        rows = rows_at(lax.rem(spot + step, size), out.shape[1])
        out[0] = add_low(first_ref[rows, :], first_in[rows, :])
        out[1] = add_low(second_ref[rows, :], second_in[rows, :])


def total_kernel(*refs):
    *parts, head_ref, head_in, out_ref = refs
    total = parts[0][...].astype(f32)
    for part in parts[1:]:
        total = total + part[...].astype(f32)
    piece = total.shape[1]
    out_ref[0:piece, :] = total[0].astype(bf16)
    out_ref[piece : 2 * piece, :] = total[1].astype(bf16)
    out_ref[2 * piece :, :] = add_low(head_ref[...], head_in[...])


def head_split_kernel(row_ref, keep_ref, arrived_ref, keep_out, send_out):
    row, piece = row_ref[0], keep_out.shape[0] - 16
    for out, at in ((keep_out, row), (send_out, 1 - row)):
        rows = rows_at(at, piece)
        out[0:piece, :] = add_low(keep_ref[rows, :], arrived_ref[rows, :])
        out[piece:, :] = add_low(keep_ref[2 * piece :, :], arrived_ref[2 * piece :, :])


def finish_kernel(at_ref, *refs):
    parts, outs, (rows_ref, heads_ref) = refs[:16], refs[16:-2], refs[-2:]
    gate_ref, up_ref, down_ref, output_ref, middle_ref, *first_refs = outs
    spot, core, row = at_ref[0], at_ref[1], at_ref[2]
    size, quarter = heads_ref.shape[0], heads_ref.shape[1] // 4
    piece = (parts[0].shape[0] - quarter - 16) // 2
    for step in range(size):
        at = lax.rem(spot - step + size, size)
        for row_flip in range(2):
            for core_flip in range(2):
                part = parts[4 * step + 2 * row_flip + core_flip]
                row_at = 1 - row if row_flip else row
                core_at = 1 - core if core_flip else core
                for split in range(2):
                    place = (4 * core_at + 2 * split + row_at) * size + at
                    rows_ref[rows_at(place, piece), :] = part[split * piece : (split + 1) * piece, :]
                rows = rows_at(2 * core_at + row_at, quarter)
                heads_ref[at, rows, :] = part[2 * piece : 2 * piece + quarter, :]
    units, width = down_ref.shape[0], output_ref.shape[0]
    gate_ref[...] = rows_ref[0:units, :].astype(f32)
    up_ref[...] = rows_ref[units : 2 * units, :].astype(f32)
    down_ref[...] = rows_ref[2 * units : 3 * units, :].astype(f32)
    output_ref[...] = rows_ref[3 * units : 3 * units + width, :].astype(f32)
    last = 3 * units + width
    middle_ref[...] = rows_ref[last : last + 16, :].astype(f32)
    for which in range(3):
        rows = slice(which * HEAD, (which + 1) * HEAD)
        grad = jnp.concatenate([heads_ref[head, rows, :].astype(f32) for head in range(size)], axis=0)
        first_refs[which][...] = grad.T


def swap_tensor(array):
    return lax.ppermute(array, "tensor", [(0, 1), (1, 0)])


def swap_dp(array, bit):
    return lax.ppermute(array, "dp", [(index, index ^ bit) for index in range(4)])


def shift_ctx(array, step):
    size = lax.axis_size("ctx")
    return lax.ppermute(array, "ctx", [(index, (index + step) % size) for index in range(size)])


def hold(*arrays):
    return lax.optimization_barrier(arrays)


def head_shards(
    tokens,
    positions,
    norm_before,
    query_weight,
    key_weight,
    value_weight,
    output_weight,
    norm_middle,
    gate_weight,
    up_weight,
    down_weight,
    cotangent,
):
    tokens, positions, cotangent = tokens[0], positions[0], cotangent[0]
    size, spot, side = lax.axis_size("ctx"), lax.axis_index("ctx"), lax.axis_index("tensor")
    core, row = lax.axis_index("dp") % 2, lax.axis_index("dp") // 2
    count, features = tokens.shape
    half = count // 2
    length = count * size
    width = size * HEAD
    piece = 64 * size * (-(-(3 * gate_weight.shape[1] + width + 16) // (64 * size))) // (2 * size * 4)

    def array(*shape, dtype=bf16):
        return jax.ShapeDtypeStruct(shape, dtype)

    def scalars_of(*members):
        return (jnp.stack([member.astype(jnp.int32) for member in members]),)

    gate_turned, up_turned = gate_weight.T, up_weight.T
    straight = (positions[0] == spot * count) & (positions[half] == spot * count + half)

    def place_of(index, part):
        folded = jnp.where(part == 0, index, 2 * size - 1 - index)
        return jnp.where(straight, 2 * index + part, folded).astype(jnp.int32).reshape(-1)

    places = jnp.arange(2 * size)
    owner = jnp.where(straight, places // 2, jnp.minimum(places, 2 * size - 1 - places))
    owner_half = jnp.where(straight, places % 2, (places >= size).astype(jnp.int32))
    steps = jnp.arange(size)
    place_in = place_of(((spot - steps) % size)[:, None], jnp.arange(2)[None, :])
    place_grad = place_of(steps[:, None], jnp.arange(2)[None, :])
    slot = (2 * owner + owner_half).astype(jnp.int32)

    frequency = rope_base ** (-jnp.arange(HEAD // 2).astype(f32) * 2.0 / HEAD)
    angles = frequency[:, None] * positions.astype(f32)[None, :]
    cosine, sine = jnp.cos(angles), jnp.sin(angles)
    angles_all = frequency[:, None] * jnp.arange(length).astype(f32)[None, :]
    cosine_all, sine_all = jnp.cos(angles_all), jnp.sin(angles_all)

    gain_first, gain_second = norm_before[None], norm_middle[None]
    *pieces, normed_first, my_normed, other_normed, weights_turned = kernel_call(
        prepare_kernel,
        "prepare",
        tuple(array(3 * HEAD, count) for unused in range(size))
        + (
            array(count, features),
            array(half, features),
            array(half, features),
            array(3 * width, features),
        ),
        scalars_of(spot, side),
        tokens,
        gain_first,
        cosine,
        sine,
        query_weight,
        key_weight,
        value_weight,
        scratch=[pltpu.VMEM((size, 3 * HEAD, count), bf16)],
        vmem=60,
    )
    my_normed, down_late = hold(my_normed, down_weight)
    weights_other = swap_tensor(
        jnp.concatenate([gate_turned, up_turned, down_late, output_weight], axis=0)
    )
    pieces = [pieces[0]] + [shift_ctx(pieces[step], step) for step in range(1, size)]
    *pieces, my_normed, cosine_all, sine_all = hold(*pieces, my_normed, cosine_all, sine_all)
    mixed_out, attended, log_total, everything = attend(place_in, slot, pieces)
    mixed_out, normed_two, first_normed = hold(mixed_out, shift_ctx(my_normed, 2), my_normed)

    def exchange(parts):
        return lax.all_to_all(parts, ("ctx", "tensor"), 0, 0, tiled=True)

    mixed, normed_two, weights_other = hold(
        exchange(mixed_out).reshape(2 * width, half), normed_two, weights_other
    )
    units = gate_weight.shape[1]
    grad_mixed, hidden_low, output_half, normed_second, grad_middle, *kept = kernel_call(
        feed_kernel,
        "feed",
        (
            array(2 * size, HEAD, half),
            array(half, features),
            array(half, features),
            array(half, features),
            array(8, features, dtype=f32),
        )
        + tuple(array(half, units) for unused in range(6)),
        scalars_of(side),
        mixed,
        tokens,
        cotangent,
        gain_second,
        output_weight,
        gate_turned,
        up_turned,
        down_weight,
        weights_other,
        scratch=[pltpu.VMEM((2 * width, features), bf16)],
        vmem=36,
    )
    grad_pieces = exchange(grad_mixed)
    grad_middle, other_two = hold(grad_middle, swap_tensor(normed_two))
    rows_keep, rows_send = kernel_call(
        feed_grad_kernel,
        "feed_grad",
        (array(2, 4 * size * piece, features), array(2, 4 * size * piece, features)),
        scalars_of(core, side),
        mixed,
        cotangent,
        hidden_low,
        normed_second,
        grad_middle,
        *kept,
        scratch=[
            pltpu.VMEM((8 * size * piece, features), bf16),
            pltpu.VMEM((2 * width, features), bf16),
        ],
        vmem=34,
        micros=8,
    )
    scalars = (
        place_grad,
        owner.astype(jnp.int32),
        owner_half.astype(jnp.int32),
    )
    rows_arrived = swap_dp(rows_send, 1)
    strip = size * piece
    first_mine, first_other, second_keep, second_send = kernel_call(
        split_kernel,
        "split",
        (
            array(2 * strip, features),
            array(2 * strip, features),
            array(2, strip, features),
            array(2, strip, features),
        ),
        scalars_of(row),
        rows_keep,
        rows_arrived,
        micros=3,
    )
    grad_pieces, first_normed = hold(grad_pieces, first_normed)
    shared = (scalars, grad_pieces, everything, attended, log_total)
    query_sum, key_sum = attend_back(0, 2, *shared)
    query_sum, key_sum, first_in, second_in, normed_one, third_normed = hold(
        query_sum,
        key_sum,
        swap_tensor(first_other),
        swap_dp(second_send, 2),
        shift_ctx(first_normed, 1),
        first_normed,
    )
    first_keep, first_send, second_mine, second_other = kernel_call(
        cross_kernel,
        "cross",
        tuple(array(strip, features) for unused in range(4)),
        scalars_of(row),
        first_mine,
        first_in,
        second_keep,
        second_in,
    )
    query_sum, key_sum, first_send, second_other, normed_one = hold(
        query_sum, key_sum, first_send, second_other, normed_one
    )
    query_sum, key_sum = attend_back(2, 4, *shared, query_sum, key_sum)
    query_sum, key_sum, first_in, second_in, normed_three, normed_one = hold(
        query_sum,
        key_sum,
        swap_dp(first_send, 2),
        swap_tensor(second_other),
        shift_ctx(third_normed, size - 1),
        normed_one,
    )
    spot_now = scalars_of(spot)
    quarters = kernel_call(
        quarter_kernel,
        "quarter",
        tuple(array(2, piece, features) for unused in range(size)),
        spot_now,
        first_keep,
        first_in,
        second_mine,
        second_in,
    )
    query_sum, key_sum, normed_one, normed_three, *quarters = hold(
        query_sum, key_sum, normed_one, normed_three, *quarters
    )
    back_out = attend_back(4, 2 * size, *shared, query_sum, key_sum, cosine_all, sine_all)
    quarters = [quarters[0]] + [shift_ctx(quarters[step], step) for step in range(1, size)]
    back_out, other_one, normed_three, *quarters = hold(
        back_out, swap_tensor(normed_one), normed_three, *quarters
    )
    other_three = swap_tensor(normed_three)
    back = lax.all_to_all(back_out, "ctx", 0, 0, tiled=True)
    normed_halves = [my_normed, other_normed]
    normed_halves += [normed_one, other_one, normed_two, other_two, normed_three, other_three]
    head_keep, head_send = kernel_call(
        head_grad_kernel,
        "head_grad",
        (array(3 * HEAD // 2 + 16, features), array(3 * HEAD // 2 + 16, features)),
        scalars_of(side, core, spot),
        back_out,
        weights_turned,
        *normed_halves,
        scratch=[pltpu.VMEM((3 * HEAD, features), bf16)],
    )
    head_send, hidden_low, output_half = hold(head_send, hidden_low, output_half)
    head_keep, head_send = kernel_call(
        head_split_kernel,
        "head_split",
        (array(3 * HEAD // 4 + 16, features), array(3 * HEAD // 4 + 16, features)),
        scalars_of(row),
        head_keep,
        swap_dp(head_send, 1),
    )
    total = kernel_call(
        total_kernel,
        "total",
        array(2 * piece + 3 * HEAD // 4 + 16, features),
        (),
        *quarters,
        head_keep,
        swap_dp(head_send, 2),
    )
    back, total, low_arrived, output_arrived = hold(
        back, total, swap_tensor(hidden_low), swap_tensor(output_half)
    )
    first_part = kernel_call(
        first_part_kernel,
        "first_part",
        array(count, features),
        (),
        back,
        weights_turned,
        scratch=[pltpu.VMEM((3 * width, count), bf16)],
    )
    first_part, total = hold(first_part, total)
    arrivals = [total] + [shift_ctx(total, step) for step in range(1, size)]
    first_arrived, *across = hold(
        swap_tensor(first_part), *[swap_dp(arrived, 2) for arrived in arrivals]
    )
    grad_tokens = kernel_call(
        token_kernel,
        "grad_tokens",
        array(count, features, dtype=f32),
        scalars_of(side),
        first_part,
        first_arrived,
        tokens,
        gain_first,
        hidden_low,
        low_arrived,
    )
    block_output = kernel_call(
        output_kernel,
        "block_output",
        array(count, features),
        scalars_of(side),
        output_half,
        output_arrived,
    )

    parts = []
    for arrived, other_row in zip(arrivals, across):
        parts += [arrived, swap_dp(arrived, 1), other_row, swap_dp(other_row, 1)]
    last = 2 * piece + 3 * HEAD // 4
    before = sum(arrived[last : last + 8].astype(f32) for arrived in arrivals)
    grad_before = (before[0] + swap_tensor(before)[0]) / norm_before.astype(f32)
    (
        grad_gate,
        grad_up,
        grad_down,
        grad_output,
        grad_middle,
        grad_query,
        grad_key,
        grad_value,
    ) = kernel_call(
        finish_kernel,
        "finish",
        (
            array(units, features, dtype=f32),
            array(units, features, dtype=f32),
            array(units, features, dtype=f32),
            array(width, features, dtype=f32),
            array(16, features, dtype=f32),
        )
        + tuple(array(features, width, dtype=f32) for unused in range(3)),
        scalars_of(spot, core, row),
        *parts,
        scratch=[
            pltpu.VMEM((8 * strip, features), bf16),
            pltpu.VMEM((size, 3 * HEAD, features), bf16),
        ],
        vmem=30,
    )
    grad_middle = grad_middle[0]
    grad_gate, grad_up = grad_gate.T, grad_up.T
    return (
        block_output[None],
        grad_tokens[None],
        grad_before,
        grad_query,
        grad_key,
        grad_value,
        grad_output,
        grad_middle,
        grad_gate,
        grad_up,
        grad_down,
    )


def solution(mesh):
    sizes = dict(mesh.shape)

    def body(*arguments):
        local_heads = arguments[3].shape[1] // HEAD
        one_head = sizes["ctx"] == local_heads and sizes["tensor"] == 2 and sizes["dp"] == 4
        one_sequence = arguments[0].shape[0] == 1
        return (head_shards if one_head and one_sequence else shards)(*arguments)

    return jax.shard_map(
        body,
        mesh=mesh,
        in_specs=(
            P("dp", "ctx", None),
            P("dp", "ctx"),
            P(),
            P(None, "tensor"),
            P(None, "tensor"),
            P(None, "tensor"),
            P("tensor", None),
            P(),
            P(None, "tensor"),
            P(None, "tensor"),
            P("tensor", None),
            P("dp", "ctx", None),
        ),
        out_specs=(
            P("dp", "ctx", None),
            P("dp", "ctx", None),
            P(),
            P(None, "tensor"),
            P(None, "tensor"),
            P(None, "tensor"),
            P("tensor", None),
            P(),
            P(None, "tensor"),
            P(None, "tensor"),
            P("tensor", None),
        ),
        check_vma=False,
    )
```

```python
import functools
import math

import jax
import jax.numpy as jnp
from jax import lax
from jax.experimental import pallas as pl
from jax.experimental.pallas import tpu as pltpu
from jax.sharding import PartitionSpec as P

HEAD = 64


epsilon = 1e-05
rope_base = 10000.0
masked_score = -1e30


def rope_tables(positions):
    frequency = rope_base ** (-jnp.arange(HEAD // 2).astype(jnp.float32) * 2.0 / HEAD)
    angles = positions.astype(jnp.float32)[..., None] * frequency
    return (jnp.cos(angles), jnp.sin(angles))


def rotate(matrix, cosine_table, sine_table):
    shaped = matrix.reshape(matrix.shape[:-1] + (-1, HEAD))
    front_half = shaped[..., : HEAD // 2]
    back_half = shaped[..., HEAD // 2 :]
    cosine = cosine_table[..., None, :]
    sine_part = sine_table[..., None, :]
    turned = jnp.concatenate(
        [front_half * cosine - back_half * sine_part, back_half * cosine + front_half * sine_part],
        axis=-1,
    )
    return turned.reshape(matrix.shape)


def normalize(token_rows, gain_row):
    inverse_rms = lax.rsqrt(jnp.mean(token_rows * token_rows, axis=-1, keepdims=True) + epsilon)
    return (token_rows * inverse_rms * gain_row, inverse_rms)


def norm_back(token_rows, inverse_rms, gain_row, grad_normed):
    weighted = grad_normed * gain_row
    inner_sum = jnp.mean(weighted * token_rows, axis=-1, keepdims=True)
    grad_rows = (
        inverse_rms * weighted - token_rows * (inverse_rms * inverse_rms * inverse_rms) * inner_sum
    )
    grad_gain = jnp.sum(grad_normed * token_rows * inverse_rms, axis=(0, 1))
    return (grad_rows, grad_gain)


def project(left, weight):
    return jnp.einsum("sbd,dh->sbh", left, weight, preferred_element_type=jnp.float32)


def project_back(grad_rows, weight):
    return jnp.einsum("sbh,dh->sbd", grad_rows, weight, preferred_element_type=jnp.float32)


def outer_sum(left, right):
    return jnp.einsum("sbd,sbh->dh", left, right, preferred_element_type=jnp.float32)


def as_heads(matrix):
    return matrix.reshape(matrix.shape[:2] + (-1, HEAD))


def split_blocks(matrix, block_width):
    block_count = matrix.shape[1] // block_width
    shaped = matrix.reshape(matrix.shape[:1] + (block_count, block_width) + matrix.shape[2:])
    return jnp.moveaxis(shaped, 1, 0)


def join_blocks(stacked):
    joined = jnp.moveaxis(stacked, 0, 1)
    return joined.reshape((joined.shape[0], joined.shape[1] * joined.shape[2]) + joined.shape[3:])


def forward_fold(query_heads, query_pos, scale_factor, fold_state, incoming):
    key_part, value_part, key_pos = incoming
    block_width = math.gcd(key_part.shape[1], 512)
    blocks = (
        split_blocks(as_heads(key_part), block_width),
        split_blocks(as_heads(value_part), block_width),
        split_blocks(key_pos, block_width),
    )

    def forward_step_block(block_state, block_in):
        key_heads, value_heads, block_pos = block_in
        allowed = block_pos[:, None, None, :] <= query_pos[:, None, :, None]
        old_max, old_total, old_accum = block_state
        scores = (
            jnp.einsum(
                "sqhe,skhe->shqk", query_heads, key_heads, preferred_element_type=jnp.float32
            )
            * scale_factor
        )
        scores = jnp.where(allowed, scores, masked_score)
        new_max = jnp.maximum(old_max, jnp.max(scores, axis=-1))
        weights = jnp.where(allowed, jnp.exp(scores - new_max[..., None]), 0.0)
        factor = jnp.exp(old_max - new_max)
        new_total = old_total * factor + jnp.sum(weights, axis=-1)
        new_accum = old_accum * factor[..., None] + jnp.einsum(
            "shqk,skhe->shqe",
            weights.astype(jnp.bfloat16),
            value_heads,
            preferred_element_type=jnp.float32,
        )
        return ((new_max, new_total, new_accum), None)

    final_state, unused = lax.scan(forward_step_block, fold_state, blocks)
    return final_state


def gradient_fold(
    query_heads, query_pos, grad_heads, log_total, delta_heads, scale_factor, fold_state, incoming
):
    key_part, value_part, key_pos = incoming
    row_count = key_part.shape[1]
    block_width = math.gcd(row_count, 512)
    blocks = (
        split_blocks(as_heads(key_part), block_width),
        split_blocks(as_heads(value_part), block_width),
        split_blocks(key_pos, block_width),
    )

    def gradient_step_block(query_state, block_in):
        key_heads, value_heads, block_pos = block_in
        allowed = block_pos[:, None, None, :] <= query_pos[:, None, :, None]
        scores = (
            jnp.einsum(
                "sqhe,skhe->shqk", query_heads, key_heads, preferred_element_type=jnp.float32
            )
            * scale_factor
        )
        weights = jnp.where(allowed, jnp.exp(scores - log_total[..., None]), 0.0)
        grad_weights = jnp.einsum(
            "sqhe,skhe->shqk", grad_heads, value_heads, preferred_element_type=jnp.float32
        )
        grad_scores = (weights * (grad_weights - delta_heads[..., None])).astype(jnp.bfloat16)
        new_query = query_state + jnp.einsum(
            "shqk,skhe->shqe", grad_scores, key_heads, preferred_element_type=jnp.float32
        )
        key_grad = jnp.einsum(
            "shqk,sqhe->skhe", grad_scores, query_heads, preferred_element_type=jnp.float32
        )
        value_grad = jnp.einsum(
            "shqk,sqhe->skhe",
            weights.astype(jnp.bfloat16),
            grad_heads,
            preferred_element_type=jnp.float32,
        )
        return (new_query, (key_grad, value_grad))

    query_state, key_total, value_total = fold_state
    query_state, outputs = lax.scan(gradient_step_block, query_state, blocks)
    key_rows = join_blocks(outputs[0])
    value_rows = join_blocks(outputs[1])
    key_total = key_rows
    value_total = value_rows
    return (query_state, key_total, value_total)


def shards(
    tokens,
    positions,
    norm_before,
    query_weight,
    key_weight,
    value_weight,
    output_weight,
    norm_middle,
    gate_weight,
    up_weight,
    down_weight,
    cotangent,
):
    sequences = tokens.shape[0]
    block_rows = tokens.shape[1]
    local_heads = query_weight.shape[1] // HEAD
    scale_factor = HEAD ** (-0.5)
    cosine_table, sine_table = rope_tables(positions)
    token_rows = tokens.astype(jnp.float32)
    gain_first = norm_before.astype(jnp.float32)
    gain_second = norm_middle.astype(jnp.float32)
    normed_first, inverse_first = normalize(token_rows, gain_first)
    normed_first = normed_first.astype(jnp.bfloat16)
    query_rot = rotate(project(normed_first, query_weight), cosine_table, sine_table).astype(
        jnp.bfloat16
    )
    key_rot = rotate(project(normed_first, key_weight), cosine_table, sine_table).astype(
        jnp.bfloat16
    )
    value_rows = project(normed_first, value_weight).astype(jnp.bfloat16)
    query_heads = as_heads(query_rot)
    head_shape = (sequences, local_heads, block_rows)
    start_state = (
        jnp.full(head_shape, masked_score, jnp.float32),
        jnp.zeros(head_shape, jnp.float32),
        jnp.zeros(head_shape + (HEAD,), jnp.float32),
    )
    row_max, row_total, accum_heads = forward_fold(
        query_heads,
        positions,
        scale_factor,
        start_state,
        (
            lax.all_gather(key_rot, "ctx", axis=1, tiled=True),
            lax.all_gather(value_rows, "ctx", axis=1, tiled=True),
            lax.all_gather(positions, "ctx", axis=1, tiled=True),
        ),
    )
    log_total = row_max + jnp.log(row_total)
    mixed_heads = jnp.swapaxes(accum_heads / row_total[..., None], 1, 2)
    mixed_rows = mixed_heads.reshape(sequences, block_rows, -1).astype(jnp.bfloat16)
    hidden = token_rows + lax.psum(
        project(mixed_rows, output_weight).astype(jnp.bfloat16), "tensor"
    ).astype(jnp.float32)
    normed_second, inverse_second = normalize(hidden, gain_second)
    normed_second = normed_second.astype(jnp.bfloat16)
    gate_rows = project(normed_second, gate_weight)
    upward = project(normed_second, up_weight)
    sigmoid_gate = jax.nn.sigmoid(gate_rows)
    silu_gate = gate_rows * sigmoid_gate
    activated = (silu_gate * upward).astype(jnp.bfloat16)
    block_output = (
        hidden
        + lax.psum(project(activated, down_weight).astype(jnp.bfloat16), "tensor").astype(
            jnp.float32
        )
    ).astype(jnp.bfloat16)
    grad_down = outer_sum(activated, cotangent)
    grad_act = project_back(cotangent, down_weight)
    grad_gate_rows = (
        grad_act * upward * sigmoid_gate * (1.0 + gate_rows * (1.0 - sigmoid_gate))
    ).astype(jnp.bfloat16)
    grad_up_rows = (grad_act * silu_gate).astype(jnp.bfloat16)
    grad_gate = outer_sum(normed_second, grad_gate_rows)
    grad_up = outer_sum(normed_second, grad_up_rows)
    second_part = project_back(grad_gate_rows, gate_weight) + project_back(grad_up_rows, up_weight)
    grad_second = lax.psum(second_part.astype(jnp.bfloat16), "tensor").astype(jnp.float32)
    hidden_back, grad_middle = norm_back(hidden, inverse_second, gain_second, grad_second)
    grad_hidden = cotangent.astype(jnp.float32) + hidden_back
    hidden_low = grad_hidden.astype(jnp.bfloat16)
    grad_output = outer_sum(mixed_rows, hidden_low)
    grad_mixed = project_back(hidden_low, output_weight).astype(jnp.bfloat16)
    grad_heads = as_heads(grad_mixed)
    delta_rows = jnp.sum(grad_heads.astype(jnp.float32) * mixed_heads, axis=-1)
    delta_heads = jnp.swapaxes(delta_rows, 1, 2)
    query_start = jnp.zeros(head_shape + (HEAD,), jnp.float32)
    whole_rows = block_rows * lax.axis_size("ctx")
    key_start = jnp.zeros((sequences, whole_rows, local_heads, HEAD), jnp.float32)
    query_sum, key_total, value_total = gradient_fold(
        query_heads,
        positions,
        grad_heads,
        log_total,
        delta_heads,
        scale_factor,
        (query_start, key_start, key_start),
        (
            lax.all_gather(key_rot, "ctx", axis=1, tiled=True),
            lax.all_gather(value_rows, "ctx", axis=1, tiled=True),
            lax.all_gather(positions, "ctx", axis=1, tiled=True),
        ),
    )
    key_sum, value_sum = (
        lax.psum_scatter(
            key_total.astype(jnp.bfloat16), "ctx", scatter_dimension=1, tiled=True
        ).astype(jnp.float32),
        lax.psum_scatter(
            value_total.astype(jnp.bfloat16), "ctx", scatter_dimension=1, tiled=True
        ).astype(jnp.float32),
    )
    query_back = rotate(
        jnp.swapaxes(query_sum, 1, 2).reshape(sequences, block_rows, -1) * scale_factor,
        cosine_table,
        -sine_table,
    ).astype(jnp.bfloat16)
    key_back = rotate(
        key_sum.reshape(sequences, block_rows, -1) * scale_factor, cosine_table, -sine_table
    ).astype(jnp.bfloat16)
    value_back = value_sum.reshape(sequences, block_rows, -1).astype(jnp.bfloat16)
    grad_query = outer_sum(normed_first, query_back)
    grad_key = outer_sum(normed_first, key_back)
    grad_value = outer_sum(normed_first, value_back)
    first_part = (
        project_back(query_back, query_weight)
        + project_back(key_back, key_weight)
        + project_back(value_back, value_weight)
    )
    grad_first = lax.psum(first_part.astype(jnp.bfloat16), "tensor").astype(jnp.float32)
    rows_back, grad_before = norm_back(token_rows, inverse_first, gain_first, grad_first)
    grad_tokens = grad_hidden + rows_back
    results = lax.psum(
        (
            grad_before,
            grad_query,
            grad_key,
            grad_value,
            grad_output,
            grad_middle,
            grad_gate,
            grad_up,
            grad_down,
        ),
        ("dp", "ctx"),
    )
    return (
        block_output,
        grad_tokens,
        results[0],
        results[1],
        results[2],
        results[3],
        results[4],
        results[5],
        results[6],
        results[7],
        results[8],
    )


f32, bf16 = jnp.float32, jnp.bfloat16


def dot(left, right, left_dim, right_dim):
    return lax.dot_general(
        left, right, (((left_dim,), (right_dim,)), ((), ())), preferred_element_type=f32
    )


def attend_kernel(block, place_ref, slot_ref, *refs):
    pieces = refs[:4]
    out_ref, attended_ref, log_ref, all_ref, key_ref, value_ref = refs[4:]
    half = pieces[0].shape[1] // 2
    length = all_ref.shape[1]
    for index, piece in enumerate(pieces):
        for side in range(2):
            columns = pl.ds(pl.multiple_of(place_ref[2 * index + side] * half, half), half)
            part = piece[:, side * half : (side + 1) * half]
            all_ref[:, columns] = part
            key_ref[columns, :] = part[HEAD : 2 * HEAD, :].astype(f32).T.astype(bf16)
            value_ref[0:HEAD, columns] = part[2 * HEAD :, :]
    value_ref[HEAD:, :] = jnp.ones((value_ref.shape[0] - HEAD, length), bf16)

    def query_step(query_index, unused):
        columns = pl.ds(pl.multiple_of(query_index * block, block), block)
        queries = all_ref[0:HEAD, columns]

        def key_step(key_index, state, diagonal=False):
            old_max, accum = state
            rows = pl.ds(pl.multiple_of(key_index * block, block), block)
            scores = dot(key_ref[rows, :], queries, 1, 0)
            if diagonal:
                key_at = lax.broadcasted_iota(jnp.int32, (block, block), 0)
                query_at = lax.broadcasted_iota(jnp.int32, (block, block), 1)
                scores = jnp.where(key_at <= query_at, scores, masked_score)
            new_max = jnp.maximum(old_max, jnp.max(scores, axis=0, keepdims=True))
            weights = jnp.exp(scores - new_max).astype(bf16)
            accum = accum * jnp.exp(old_max - new_max) + dot(value_ref[:, rows], weights, 1, 0)
            return new_max, accum

        state = (
            jnp.full((1, block), masked_score, f32),
            jnp.zeros((value_ref.shape[0], block), f32),
        )
        state = lax.fori_loop(0, query_index, key_step, state)
        row_max, accum = key_step(query_index, state, True)
        total = accum[HEAD : HEAD + 1, :]
        mixed = accum[0:HEAD, :] / total
        attended_ref[:, columns] = mixed
        log_ref[:, columns] = jnp.broadcast_to(row_max + jnp.log(total), (8, block))
        for side in range(block // half):
            slot = slot_ref[query_index * (block // half) + side]
            out_ref[slot] = mixed[:, side * half : (side + 1) * half].astype(bf16)
        return 0

    lax.fori_loop(0, length // block, query_step, 0)


def gradient_kernel(block, first, last, place_ref, send_ref, side_ref, *refs):
    pieces_ref, all_ref, attended_ref, log_ref, *refs = refs
    half = pieces_ref.shape[2]
    length = all_ref.shape[1]
    ends = last == length // block
    if first:
        query_in_ref, key_in_ref, *refs = refs
    if ends:
        cosine_ref, sine_ref, out_ref, *refs = refs
        key_ref, value_ref, grad_ref, delta_ref, query_sum_ref, key_sum_ref = refs
    else:
        query_sum_ref, key_sum_ref, key_ref, value_ref, grad_ref, delta_ref = refs
    if first:
        query_sum_ref[...] = query_in_ref[...]
        done = pl.ds(0, first * block)
        key_sum_ref[:, done] = key_in_ref[:, done]
    else:
        query_sum_ref[...] = jnp.zeros_like(query_sum_ref)
    for index in range(pieces_ref.shape[0]):
        columns = pl.ds(pl.multiple_of(place_ref[index] * half, half), half)
        grad = pieces_ref[index]
        grad_ref[:, columns] = grad
        delta = jnp.sum(grad.astype(f32) * attended_ref[:, columns], axis=0, keepdims=True)
        delta_ref[:, columns] = jnp.broadcast_to(delta, (8, half))
    for index in range(first, last):
        columns = pl.ds(index * block, block)
        key_ref[columns, :] = all_ref[HEAD : 2 * HEAD, columns].astype(f32).T.astype(bf16)
        value_ref[columns, :] = all_ref[2 * HEAD :, columns].astype(f32).T.astype(bf16)

    def key_step(key_index, unused):
        rows = pl.ds(pl.multiple_of(key_index * block, block), block)
        keys = key_ref[rows, :]
        values = value_ref[rows, :]
        keys_turned = all_ref[HEAD : 2 * HEAD, rows]

        def query_step(query_index, state, diagonal=False):
            key_sum, value_sum = state
            columns = pl.ds(pl.multiple_of(query_index * block, block), block)
            queries = all_ref[0:HEAD, columns]
            grads = grad_ref[:, columns]
            scores = dot(keys, queries, 1, 0) - log_ref[0:1, columns]
            if diagonal:
                key_at = lax.broadcasted_iota(jnp.int32, (block, block), 0)
                query_at = lax.broadcasted_iota(jnp.int32, (block, block), 1)
                scores = jnp.where(key_at <= query_at, scores, masked_score)
            weights = jnp.exp(scores)
            grad_weights = dot(values, grads, 1, 0) - delta_ref[0:1, columns]
            grad_scores = (weights * grad_weights).astype(bf16)
            value_sum = value_sum + dot(grads, weights.astype(bf16), 1, 1)
            key_sum = key_sum + dot(queries, grad_scores, 1, 1)
            query_sum_ref[:, columns] += dot(keys_turned, grad_scores, 1, 0)
            return key_sum, value_sum

        state = (jnp.zeros((HEAD, block), f32), jnp.zeros((HEAD, block), f32))
        state = query_step(key_index, state, True)
        key_sum, value_sum = lax.fori_loop(key_index + 1, length // block, query_step, state)
        key_sum_ref[0:HEAD, rows] = key_sum
        key_sum_ref[HEAD:, rows] = value_sum
        return 0

    lax.fori_loop(first, last, key_step, 0)
    if not ends:
        return

    def turn_back(rows, cosine, sine):
        front, back = rows[: HEAD // 2, :], rows[HEAD // 2 :, :]
        return jnp.concatenate([front * cosine + back * sine, back * cosine - front * sine], axis=0)

    def write_step(index, unused):
        columns = pl.ds(pl.multiple_of(index * half, half), half)
        cosine, sine = cosine_ref[:, columns], sine_ref[:, columns]
        to = send_ref[index]
        at = pl.ds(pl.multiple_of(side_ref[index] * half, half), half)
        query_rows = query_sum_ref[:, columns] * (HEAD**-0.5)
        out_ref[to, 0:HEAD, at] = turn_back(query_rows, cosine, sine).astype(bf16)
        out_ref[to, HEAD : 2 * HEAD, at] = turn_back(
            key_sum_ref[0:HEAD, columns], cosine, sine
        ).astype(bf16)
        out_ref[to, 2 * HEAD :, at] = key_sum_ref[HEAD:, columns].astype(bf16)
        return 0

    lax.fori_loop(0, length // half, write_step, 0)


def attend(place, slot, pieces):
    rows, width = pieces[0].shape
    half, length = width // 2, width * len(pieces)
    smem, vmem = pl.BlockSpec(memory_space=pltpu.SMEM), pl.BlockSpec(memory_space=pltpu.VMEM)
    return pl.pallas_call(
        functools.partial(attend_kernel, width),
        out_shape=(
            jax.ShapeDtypeStruct((2 * len(pieces), HEAD, half), bf16),
            jax.ShapeDtypeStruct((HEAD, length), f32),
            jax.ShapeDtypeStruct((8, length), f32),
            jax.ShapeDtypeStruct((rows, length), bf16),
        ),
        in_specs=[smem] * 2 + [vmem] * 4,
        out_specs=[vmem] * 4,
        scratch_shapes=[pltpu.VMEM((length, HEAD), bf16), pltpu.VMEM((HEAD + 16, length), bf16)],
        compiler_params=pltpu.CompilerParams(vmem_limit_bytes=60 << 20),
        cost_estimate=pl.CostEstimate(flops=10**6, bytes_accessed=10**4, transcendentals=0),
        name="attend",
    )(place, slot, *pieces)


def attend_back(first, last, scalars, pieces, everything, attended, log_total, *sums):
    half = pieces.shape[2]
    rows, length = everything.shape
    smem, vmem = pl.BlockSpec(memory_space=pltpu.SMEM), pl.BlockSpec(memory_space=pltpu.VMEM)
    totals = [(HEAD, length), (2 * HEAD, length)]
    scratch = [
        pltpu.VMEM((length, HEAD), bf16),
        pltpu.VMEM((length, HEAD), bf16),
        pltpu.VMEM((HEAD, length), bf16),
        pltpu.VMEM((8, length), f32),
    ]
    ends = last == length // half
    if ends:
        out_shape = jax.ShapeDtypeStruct((length // (2 * half), rows, 2 * half), bf16)
        scratch = scratch + [pltpu.VMEM(shape, f32) for shape in totals]
    else:
        out_shape = tuple(jax.ShapeDtypeStruct(shape, f32) for shape in totals)
    return pl.pallas_call(
        functools.partial(gradient_kernel, half, first, last),
        out_shape=out_shape,
        in_specs=[smem] * 3 + [vmem] * (4 + len(sums)),
        out_specs=vmem if ends else (vmem, vmem),
        scratch_shapes=scratch,
        compiler_params=pltpu.CompilerParams(vmem_limit_bytes=30 << 20),
        cost_estimate=pl.CostEstimate(flops=10**6, bytes_accessed=10**4, transcendentals=0),
        name="attend_back",
    )(*scalars, pieces, everything, attended, log_total, *sums)


SMEM, VMEM = pl.BlockSpec(memory_space=pltpu.SMEM), pl.BlockSpec(memory_space=pltpu.VMEM)


def kernel_call(kernel, name, out_shape, scalars, *arrays, scratch=(), vmem=16, micros=0):
    return pl.pallas_call(
        kernel,
        out_shape=out_shape,
        in_specs=[SMEM] * len(scalars) + [VMEM] * len(arrays),
        out_specs=jax.tree.map(lambda unused: VMEM, out_shape),
        scratch_shapes=list(scratch),
        compiler_params=pltpu.CompilerParams(vmem_limit_bytes=vmem << 20),
        cost_estimate=pl.CostEstimate(
            flops=10**6 + micros * 10**9, bytes_accessed=10**4, transcendentals=0
        ),
        name=name,
    )(*scalars, *arrays)


def rows_at(index, count):
    return pl.ds(pl.multiple_of(index * count, count), count)


def token_kernel(side_ref, mine_ref, arrived_ref, tokens_ref, gain_ref, *refs):
    low_mine, low_arrived, grad_ref = refs
    side = side_ref[0]
    half = low_mine.shape[0]
    gain = gain_ref[...].astype(f32)
    for index, low in ((side, low_mine), (1 - side, low_arrived)):
        rows = rows_at(index, half)
        grad = mine_ref[rows, :].astype(f32) + arrived_ref[rows, :].astype(f32)
        token = tokens_ref[rows, :].astype(f32)
        inverse = lax.rsqrt(jnp.mean(token * token, axis=1, keepdims=True) + epsilon)
        weighted = grad * gain
        inner = jnp.mean(weighted * token, axis=1, keepdims=True)
        grad_ref[rows, :] = low[...].astype(f32) + (
            inverse * weighted - token * (inverse * inverse * inverse) * inner
        )


def head_grad_kernel(at_ref, back_ref, weight_ref, *refs):
    *normed, keep_ref, send_ref, sum_ref = refs
    side, core, spot, size = at_ref[0], at_ref[1], at_ref[2], back_ref.shape[0]
    half = back_ref.shape[2] // 2
    total = None
    for step in range(size):
        for place, rows in ((side, normed[2 * step]), (1 - side, normed[2 * step + 1])):
            at = lax.rem(spot - step + size, size)
            term = dot(back_ref[at, :, rows_at(place, half)], rows[...], 1, 0)
            total = term if total is None else total + term
    sum_ref[...] = total.astype(bf16)
    before = jnp.zeros((1, total.shape[1]), f32)
    for which in range(3):
        weight = weight_ref[rows_at(which * size + spot, HEAD), :].astype(f32)
        grad = total[which * HEAD : (which + 1) * HEAD, :]
        before = before + jnp.sum(weight * grad, axis=0, keepdims=True)
    rows = total.shape[0] // 2
    for out, at in ((keep_ref, core), (send_ref, 1 - core)):
        out[0:rows, :] = sum_ref[rows_at(at, rows), :]
        out[rows:, :] = jnp.broadcast_to(before, (16, total.shape[1])).astype(bf16)


def first_part_kernel(back_ref, weight_ref, out_ref, rows_ref):
    size = back_ref.shape[0]
    for head in range(size):
        for which in range(3):
            at = (which * size + head) * HEAD
            rows_ref[at : at + HEAD, :] = back_ref[head, which * HEAD : (which + 1) * HEAD, :]
    block = out_ref.shape[0] // 4
    for index in range(4):
        rows = slice(index * block, (index + 1) * block)
        out_ref[rows, :] = dot(rows_ref[:, rows], weight_ref[...], 0, 0).astype(bf16)


def prepare_kernel(at_ref, tokens_ref, gain_ref, cosine_ref, sine_ref, *refs):
    weights, refs = refs[:3], refs[3:]
    pieces, (normed_ref, mine_ref, other_ref, turned_ref, heads_ref) = refs[:-5], refs[-5:]
    spot, side, size = at_ref[0], at_ref[1], len(pieces)
    half = mine_ref.shape[0]
    token = tokens_ref[...].astype(f32)
    inverse = lax.rsqrt(jnp.mean(token * token, axis=1, keepdims=True) + epsilon)
    normed_ref[...] = (token * inverse * gain_ref[...].astype(f32)).astype(bf16)
    cosine, sine = cosine_ref[...], sine_ref[...]
    width = size * HEAD
    for which, weight in enumerate(weights):
        turned = weight[...].astype(f32).T.astype(bf16)
        turned_ref[which * width : (which + 1) * width, :] = turned
        product = dot(turned, normed_ref[...], 1, 1)
        for head in range(size):
            rows = product[head * HEAD : (head + 1) * HEAD, :]
            if which < 2:
                front, back = rows[: HEAD // 2, :], rows[HEAD // 2 :, :]
                rows = jnp.concatenate(
                    [front * cosine - back * sine, back * cosine + front * sine], axis=0
                )
            rows = rows.astype(bf16)
            if which == 0:
                rows = rows * bf16(HEAD**-0.5)
            heads_ref[head, which * HEAD : (which + 1) * HEAD, :] = rows
    for step, piece in enumerate(pieces):
        piece[...] = heads_ref[lax.rem(spot + step, size)]
    mine_ref[...] = normed_ref[rows_at(side, half), :]
    other_ref[...] = normed_ref[rows_at(1 - side, half), :]


def output_kernel(side_ref, mine_ref, arrived_ref, output_ref):
    half = mine_ref.shape[0]
    output_ref[rows_at(side_ref[0], half), :] = mine_ref[...]
    output_ref[rows_at(1 - side_ref[0], half), :] = arrived_ref[...]


def feed_kernel(side_ref, mixed_ref, tokens_ref, cotangent_ref, gain_ref, *refs):
    output_mine, gate_mine, up_mine, down_mine, other, *refs = refs
    grad_ref, low_ref, out_ref, normed_ref, middle_ref, *kept, output_ref = refs
    side = side_ref[0]
    half, features = normed_ref.shape
    block = 256
    size, units = output_mine.shape[0] // HEAD, gate_mine.shape[0]
    for index in range(size):
        at = index * HEAD
        output_ref[rows_at(2 * index + side, HEAD), :] = output_mine[at : at + HEAD, :]
        at = 3 * units + index * HEAD
        output_ref[rows_at(2 * index + 1 - side, HEAD), :] = other[at : at + HEAD, :]
    middle_ref[...] = jnp.zeros_like(middle_ref)
    parts = (
        (gate_mine, up_mine, down_mine, kept[:3]),
        tuple(other.at[at * units : (at + 1) * units, :] for at in range(3)) + (kept[3:],),
    )

    def step(index, unused):
        rows = rows_at(index, block)
        far = pl.ds(pl.multiple_of(side * half + index * block, block), block)
        token, cotangent = tokens_ref[far, :].astype(f32), cotangent_ref[far, :]
        hidden = token + dot(mixed_ref[:, rows], output_ref[...], 0, 0)
        inverse = lax.rsqrt(jnp.mean(hidden * hidden, axis=1, keepdims=True) + epsilon)
        gain = gain_ref[...].astype(f32)
        normed = (hidden * inverse * gain).astype(bf16)
        normed_ref[rows, :] = normed
        output_rows, grad_second = hidden, None
        for gate, up, down, (keep_gate, keep_up, keep_active) in parts:
            gate_rows = dot(normed, gate[...], 1, 1)
            upward = dot(normed, up[...], 1, 1)
            sigmoid_gate = jax.nn.sigmoid(gate_rows)
            silu_gate = gate_rows * sigmoid_gate
            activated = (silu_gate * upward).astype(bf16)
            keep_active[rows, :] = activated
            grad_act = dot(cotangent, down[...], 1, 1)
            grad_gate = (
                grad_act * upward * sigmoid_gate * (1.0 + gate_rows * (1.0 - sigmoid_gate))
            ).astype(bf16)
            keep_gate[rows, :] = grad_gate
            grad_up = (grad_act * silu_gate).astype(bf16)
            keep_up[rows, :] = grad_up
            output_rows = output_rows + dot(activated, down[...], 1, 0)
            term = dot(grad_gate, gate[...], 1, 0) + dot(grad_up, up[...], 1, 0)
            grad_second = term if grad_second is None else grad_second + term
        out_ref[rows, :] = output_rows.astype(bf16)
        weighted = grad_second * gain
        inner = jnp.mean(weighted * hidden, axis=1, keepdims=True)
        low = (
            cotangent.astype(f32)
            + (inverse * weighted - hidden * (inverse * inverse * inverse) * inner)
        ).astype(bf16)
        low_ref[rows, :] = low
        middle = jnp.sum(grad_second * hidden * inverse, axis=0, keepdims=True)
        middle_ref[...] += jnp.broadcast_to(middle, middle_ref.shape)
        grad_mixed = dot(output_ref[...], low, 1, 1).astype(bf16)
        for head in range(2 * size):
            grad_ref[head, :, rows] = grad_mixed[head * HEAD : (head + 1) * HEAD, :]
        return 0

    lax.fori_loop(0, half // block, step, 0)


def feed_grad_kernel(at_ref, mixed_ref, cotangent_ref, low_ref, normed_ref, middle_ref, *refs):
    kept, (keep_ref, send_ref, rows_ref, mixed_grad_ref) = refs[:6], refs[6:]
    core, side = at_ref[0], at_ref[1]
    half, units = kept[0].shape
    width = mixed_ref.shape[0] // 2
    size = width // HEAD
    mixed_grad_ref[...] = dot(mixed_ref[...], low_ref[...], 1, 0).astype(bf16)
    cotangent = cotangent_ref[rows_at(side, half), :]
    last = 3 * units + width
    rows_ref[last : last + 16, :] = jnp.broadcast_to(
        middle_ref[0:1, :], (16, middle_ref.shape[1])
    ).astype(bf16)
    rows_ref[last + 16 :, :] = jnp.zeros_like(rows_ref[last + 16 :, :])
    piece = keep_ref.shape[1]
    for which, of_side in ((0, side), (1, 1 - side)):
        grad_gate, grad_up, activated = kept[3 * which : 3 * which + 3]
        rows_ref[0:units, :] = dot(grad_gate[...], normed_ref[...], 0, 0).astype(bf16)
        rows_ref[units : 2 * units, :] = dot(grad_up[...], normed_ref[...], 0, 0).astype(bf16)
        rows_ref[2 * units : 3 * units, :] = dot(activated[...], cotangent, 0, 0).astype(bf16)
        for index in range(size):
            at = 3 * units + index * HEAD
            rows_ref[at : at + HEAD, :] = mixed_grad_ref[rows_at(2 * index + of_side, HEAD), :]
        keep_ref[which] = rows_ref[rows_at(core, piece), :]
        send_ref[which] = rows_ref[rows_at(1 - core, piece), :]


def add_low(left, right):
    return (left.astype(f32) + right.astype(f32)).astype(bf16)


def split_kernel(row_ref, keep_ref, arrived_ref, mine_ref, other_ref, keep_out, send_out):
    row, half, piece = row_ref[0], mine_ref.shape[0], keep_out.shape[1]
    mine_ref[...] = add_low(keep_ref[0, 0:half, :], arrived_ref[0, 0:half, :])
    other_ref[...] = add_low(keep_ref[1, 0:half, :], arrived_ref[1, 0:half, :])
    for out, at in ((keep_out, row), (send_out, 1 - row)):
        rows = pl.ds(pl.multiple_of(half + at * piece, piece), piece)
        for which in range(2):
            out[which] = add_low(keep_ref[which, rows, :], arrived_ref[which, rows, :])


def cross_kernel(row_ref, first_ref, first_in, second_ref, second_in, keep, send, mine, other):
    row, piece = row_ref[0], keep.shape[0]
    for out, at in ((keep, row), (send, 1 - row)):
        rows = rows_at(at, piece)
        out[...] = add_low(first_ref[rows, :], first_in[rows, :])
    mine[...] = add_low(second_ref[0], second_in[0])
    other[...] = add_low(second_ref[1], second_in[1])


def quarter_kernel(spot_ref, first_ref, first_in, second_ref, second_in, *outs):
    spot, size = spot_ref[0], len(outs)
    for step, out in enumerate(outs):
        rows = rows_at(lax.rem(spot + step, size), out.shape[1])
        out[0] = add_low(first_ref[rows, :], first_in[rows, :])
        out[1] = add_low(second_ref[rows, :], second_in[rows, :])


def total_kernel(*refs):
    *parts, head_ref, head_in, out_ref = refs
    total = parts[0][...].astype(f32)
    for part in parts[1:]:
        total = total + part[...].astype(f32)
    piece = total.shape[1]
    out_ref[0:piece, :] = total[0].astype(bf16)
    out_ref[piece : 2 * piece, :] = total[1].astype(bf16)
    out_ref[2 * piece :, :] = add_low(head_ref[...], head_in[...])


def head_split_kernel(row_ref, keep_ref, arrived_ref, keep_out, send_out):
    row, piece = row_ref[0], keep_out.shape[0] - 16
    for out, at in ((keep_out, row), (send_out, 1 - row)):
        rows = rows_at(at, piece)
        out[0:piece, :] = add_low(keep_ref[rows, :], arrived_ref[rows, :])
        out[piece:, :] = add_low(keep_ref[2 * piece :, :], arrived_ref[2 * piece :, :])


def finish_kernel(at_ref, *refs):
    parts, outs, (rows_ref, heads_ref) = refs[:16], refs[16:-2], refs[-2:]
    gate_ref, up_ref, down_ref, output_ref, middle_ref, *first_refs = outs
    spot, core, row = at_ref[0], at_ref[1], at_ref[2]
    size, quarter = heads_ref.shape[0], heads_ref.shape[1] // 4
    piece = (parts[0].shape[0] - quarter - 16) // 2
    for step in range(size):
        at = lax.rem(spot - step + size, size)
        for row_flip in range(2):
            for core_flip in range(2):
                part = parts[4 * step + 2 * row_flip + core_flip]
                row_at = 1 - row if row_flip else row
                core_at = 1 - core if core_flip else core
                for split in range(2):
                    place = (4 * core_at + 2 * split + row_at) * size + at
                    rows_ref[rows_at(place, piece), :] = part[split * piece : (split + 1) * piece, :]
                rows = rows_at(2 * core_at + row_at, quarter)
                heads_ref[at, rows, :] = part[2 * piece : 2 * piece + quarter, :]
    units, width = down_ref.shape[0], output_ref.shape[0]
    gate_ref[...] = rows_ref[0:units, :].astype(f32)
    up_ref[...] = rows_ref[units : 2 * units, :].astype(f32)
    down_ref[...] = rows_ref[2 * units : 3 * units, :].astype(f32)
    output_ref[...] = rows_ref[3 * units : 3 * units + width, :].astype(f32)
    last = 3 * units + width
    middle_ref[...] = rows_ref[last : last + 16, :].astype(f32)[0:1, :]
    for which in range(3):
        rows = slice(which * HEAD, (which + 1) * HEAD)
        grad = jnp.concatenate([heads_ref[head, rows, :].astype(f32) for head in range(size)], axis=0)
        first_refs[which][...] = grad.T


def swap_tensor(array):
    return lax.ppermute(array, "tensor", [(0, 1), (1, 0)])


def swap_dp(array, bit):
    return lax.ppermute(array, "dp", [(index, index ^ bit) for index in range(4)])


def shift_ctx(array, step):
    size = lax.axis_size("ctx")
    return lax.ppermute(array, "ctx", [(index, (index + step) % size) for index in range(size)])


def hold(*arrays):
    return lax.optimization_barrier(arrays)


def head_shards(
    tokens,
    positions,
    norm_before,
    query_weight,
    key_weight,
    value_weight,
    output_weight,
    norm_middle,
    gate_weight,
    up_weight,
    down_weight,
    cotangent,
):
    tokens, positions, cotangent = tokens[0], positions[0], cotangent[0]
    size, spot, side = lax.axis_size("ctx"), lax.axis_index("ctx"), lax.axis_index("tensor")
    core, row = lax.axis_index("dp") % 2, lax.axis_index("dp") // 2
    count, features = tokens.shape
    half = count // 2
    length = count * size
    width = size * HEAD
    piece = 64 * size * (-(-(3 * gate_weight.shape[1] + width + 16) // (64 * size))) // (2 * size * 4)

    def array(*shape, dtype=bf16):
        return jax.ShapeDtypeStruct(shape, dtype)

    def scalars_of(*members):
        return (jnp.stack([member.astype(jnp.int32) for member in members]),)

    gate_turned, up_turned = gate_weight.T, up_weight.T
    straight = (positions[0] == spot * count) & (positions[half] == spot * count + half)

    def place_of(index, part):
        folded = jnp.where(part == 0, index, 2 * size - 1 - index)
        return jnp.where(straight, 2 * index + part, folded).astype(jnp.int32).reshape(-1)

    places = jnp.arange(2 * size)
    owner = jnp.where(straight, places // 2, jnp.minimum(places, 2 * size - 1 - places))
    owner_half = jnp.where(straight, places % 2, (places >= size).astype(jnp.int32))
    steps = jnp.arange(size)
    place_in = place_of(((spot - steps) % size)[:, None], jnp.arange(2)[None, :])
    place_grad = place_of(steps[:, None], jnp.arange(2)[None, :])
    slot = (2 * owner + owner_half).astype(jnp.int32)

    frequency = rope_base ** (-jnp.arange(HEAD // 2).astype(f32) * 2.0 / HEAD)
    angles = frequency[:, None] * positions.astype(f32)[None, :]
    cosine, sine = jnp.cos(angles), jnp.sin(angles)
    angles_all = frequency[:, None] * jnp.arange(length).astype(f32)[None, :]
    cosine_all, sine_all = jnp.cos(angles_all), jnp.sin(angles_all)

    gain_first, gain_second = norm_before[None], norm_middle[None]
    *pieces, normed_first, my_normed, other_normed, weights_turned = kernel_call(
        prepare_kernel,
        "prepare",
        tuple(array(3 * HEAD, count) for unused in range(size))
        + (
            array(count, features),
            array(half, features),
            array(half, features),
            array(3 * width, features),
        ),
        scalars_of(spot, side),
        tokens,
        gain_first,
        cosine,
        sine,
        query_weight,
        key_weight,
        value_weight,
        scratch=[pltpu.VMEM((size, 3 * HEAD, count), bf16)],
        vmem=60,
    )
    my_normed, down_late = hold(my_normed, down_weight)
    weights_other = swap_tensor(
        jnp.concatenate([gate_turned, up_turned, down_late, output_weight], axis=0)
    )
    pieces = [pieces[0]] + [shift_ctx(pieces[step], step) for step in range(1, size)]
    send_places = (owner.astype(jnp.int32), owner_half.astype(jnp.int32))
    numbers = [
        scalars_of(*members)[0]
        for members in ((side,), (row,), (spot,), (core, side), (side, core, spot), (spot, core, row))
    ]
    *pieces, my_normed, cosine_all, sine_all, place_in, slot, place_grad, gain_second = hold(
        *pieces, my_normed, cosine_all, sine_all, place_in, slot, place_grad, gain_second
    )
    numbers, send_places, my_normed = hold(numbers, send_places, my_normed)
    side_now, row_now, spot_now, core_side, side_core_spot, spot_core_row = (
        (number,) for number in numbers
    )
    mixed_out, attended, log_total, everything = attend(place_in, slot, pieces)
    mixed_out, normed_two, first_normed = hold(mixed_out, shift_ctx(my_normed, 2), my_normed)

    def exchange(parts):
        return lax.all_to_all(parts, ("ctx", "tensor"), 0, 0, tiled=True)

    mixed, normed_two, weights_other = hold(
        exchange(mixed_out).reshape(2 * width, half), normed_two, weights_other
    )
    units = gate_weight.shape[1]
    grad_mixed, hidden_low, output_half, normed_second, grad_middle, *kept = kernel_call(
        feed_kernel,
        "feed",
        (
            array(2 * size, HEAD, half),
            array(half, features),
            array(half, features),
            array(half, features),
            array(8, features, dtype=f32),
        )
        + tuple(array(half, units) for unused in range(6)),
        side_now,
        mixed,
        tokens,
        cotangent,
        gain_second,
        output_weight,
        gate_turned,
        up_turned,
        down_weight,
        weights_other,
        scratch=[pltpu.VMEM((2 * width, features), bf16)],
        vmem=36,
    )
    grad_pieces = exchange(grad_mixed)
    grad_middle, other_two = hold(grad_middle, swap_tensor(normed_two))
    rows_keep, rows_send = kernel_call(
        feed_grad_kernel,
        "feed_grad",
        (array(2, 4 * size * piece, features), array(2, 4 * size * piece, features)),
        core_side,
        mixed,
        cotangent,
        hidden_low,
        normed_second,
        grad_middle,
        *kept,
        scratch=[
            pltpu.VMEM((8 * size * piece, features), bf16),
            pltpu.VMEM((2 * width, features), bf16),
        ],
        vmem=34,
        micros=8,
    )
    scalars = (
        place_grad,
        *send_places,
    )
    rows_arrived = swap_dp(rows_send, 1)
    strip = size * piece
    first_mine, first_other, second_keep, second_send = kernel_call(
        split_kernel,
        "split",
        (
            array(2 * strip, features),
            array(2 * strip, features),
            array(2, strip, features),
            array(2, strip, features),
        ),
        row_now,
        rows_keep,
        rows_arrived,
        micros=3,
    )
    grad_pieces, first_normed, output_half = hold(grad_pieces, first_normed, output_half)
    shared = (scalars, grad_pieces, everything, attended, log_total)
    query_sum, key_sum = attend_back(0, 2, *shared)
    query_sum, key_sum, first_in, second_in, normed_one, third_normed = hold(
        query_sum,
        key_sum,
        swap_tensor(first_other),
        swap_dp(second_send, 2),
        shift_ctx(first_normed, 1),
        first_normed,
    )
    first_keep, first_send, second_mine, second_other = kernel_call(
        cross_kernel,
        "cross",
        tuple(array(strip, features) for unused in range(4)),
        row_now,
        first_mine,
        first_in,
        second_keep,
        second_in,
    )
    query_sum, key_sum, first_send, second_other, normed_one = hold(
        query_sum, key_sum, first_send, second_other, normed_one
    )
    query_sum, key_sum = attend_back(2, 4, *shared, query_sum, key_sum)
    query_sum, key_sum, first_in, second_in, normed_three, normed_one = hold(
        query_sum,
        key_sum,
        swap_dp(first_send, 2),
        swap_tensor(second_other),
        shift_ctx(third_normed, size - 1),
        normed_one,
    )
    quarters = kernel_call(
        quarter_kernel,
        "quarter",
        tuple(array(2, piece, features) for unused in range(size)),
        spot_now,
        first_keep,
        first_in,
        second_mine,
        second_in,
    )
    query_sum, key_sum, normed_one, normed_three, *quarters = hold(
        query_sum, key_sum, normed_one, normed_three, *quarters
    )
    back_out = attend_back(4, 2 * size, *shared, query_sum, key_sum, cosine_all, sine_all)
    quarters = [quarters[0]] + [shift_ctx(quarters[step], step) for step in range(1, size)]
    back_out, other_one, normed_three, *quarters = hold(
        back_out, swap_tensor(normed_one), normed_three, *quarters
    )
    other_three, hidden_low, output_half = hold(swap_tensor(normed_three), hidden_low, output_half)
    back = lax.all_to_all(back_out, "ctx", 0, 0, tiled=True)
    normed_halves = [my_normed, other_normed]
    normed_halves += [normed_one, other_one, normed_two, other_two, normed_three, other_three]
    head_keep, head_send = kernel_call(
        head_grad_kernel,
        "head_grad",
        (array(3 * HEAD // 2 + 16, features), array(3 * HEAD // 2 + 16, features)),
        side_core_spot,
        back_out,
        weights_turned,
        *normed_halves,
        scratch=[pltpu.VMEM((3 * HEAD, features), bf16)],
        vmem=60,
    )
    head_keep, head_send = kernel_call(
        head_split_kernel,
        "head_split",
        (array(3 * HEAD // 4 + 16, features), array(3 * HEAD // 4 + 16, features)),
        row_now,
        head_keep,
        swap_dp(head_send, 1),
    )
    total = kernel_call(
        total_kernel,
        "total",
        array(2 * piece + 3 * HEAD // 4 + 16, features),
        (),
        *quarters,
        head_keep,
        swap_dp(head_send, 2),
    )
    back, total, low_arrived, output_arrived = hold(
        back, total, swap_tensor(hidden_low), swap_tensor(output_half)
    )
    first_part = kernel_call(
        first_part_kernel,
        "first_part",
        array(count, features),
        (),
        back,
        weights_turned,
        scratch=[pltpu.VMEM((3 * width, count), bf16)],
    )
    first_part, total = hold(first_part, total)
    arrivals = [total] + [shift_ctx(total, step) for step in range(1, size)]
    first_arrived = swap_tensor(first_part)
    across = [swap_dp(arrived, 2) for arrived in arrivals]
    grad_tokens = kernel_call(
        token_kernel,
        "grad_tokens",
        array(count, features, dtype=f32),
        side_now,
        first_part,
        first_arrived,
        tokens,
        gain_first,
        hidden_low,
        low_arrived,
    )
    block_output = kernel_call(
        output_kernel,
        "block_output",
        array(count, features),
        side_now,
        output_half,
        output_arrived,
    )

    grad_tokens, across[2] = hold(grad_tokens, across[2])
    parts = []
    for arrived, other_row in zip(arrivals, across):
        parts += [arrived, swap_dp(arrived, 1), other_row, swap_dp(other_row, 1)]
    last = 2 * piece + 3 * HEAD // 4
    before = sum(arrived[last : last + 8].astype(f32) for arrived in arrivals)
    grad_before = (before[0] + swap_tensor(before)[0]) / norm_before.astype(f32)
    (
        grad_gate,
        grad_up,
        grad_down,
        grad_output,
        grad_middle,
        grad_query,
        grad_key,
        grad_value,
    ) = kernel_call(
        finish_kernel,
        "finish",
        (
            array(units, features, dtype=f32),
            array(units, features, dtype=f32),
            array(units, features, dtype=f32),
            array(width, features, dtype=f32),
            array(1, features, dtype=f32),
        )
        + tuple(array(features, width, dtype=f32) for unused in range(3)),
        spot_core_row,
        *parts,
        scratch=[
            pltpu.VMEM((8 * strip, features), bf16),
            pltpu.VMEM((size, 3 * HEAD, features), bf16),
        ],
        vmem=30,
    )
    grad_middle = grad_middle.reshape(features)
    grad_gate, grad_up = grad_gate.T, grad_up.T
    return (
        block_output[None],
        grad_tokens[None],
        grad_before,
        grad_query,
        grad_key,
        grad_value,
        grad_output,
        grad_middle,
        grad_gate,
        grad_up,
        grad_down,
    )


def solution(mesh):
    sizes = dict(mesh.shape)

    def body(*arguments):
        local_heads = arguments[3].shape[1] // HEAD
        one_head = sizes["ctx"] == local_heads and sizes["tensor"] == 2 and sizes["dp"] == 4
        one_sequence = arguments[0].shape[0] == 1
        return (head_shards if one_head and one_sequence else shards)(*arguments)

    return jax.shard_map(
        body,
        mesh=mesh,
        in_specs=(
            P("dp", "ctx", None),
            P("dp", "ctx"),
            P(),
            P(None, "tensor"),
            P(None, "tensor"),
            P(None, "tensor"),
            P("tensor", None),
            P(),
            P(None, "tensor"),
            P(None, "tensor"),
            P("tensor", None),
            P("dp", "ctx", None),
        ),
        out_specs=(
            P("dp", "ctx", None),
            P("dp", "ctx", None),
            P(),
            P(None, "tensor"),
            P(None, "tensor"),
            P(None, "tensor"),
            P("tensor", None),
            P(),
            P(None, "tensor"),
            P(None, "tensor"),
            P("tensor", None),
        ),
        check_vma=False,
    )
```

```python
import functools
import math

import jax
import jax.numpy as jnp
from jax import lax
from jax.experimental import pallas as pl
from jax.experimental.pallas import tpu as pltpu
from jax.sharding import PartitionSpec as P

HEAD = 64


epsilon = 1e-05
rope_base = 10000.0
masked_score = -1e30


def rope_tables(positions):
    frequency = rope_base ** (-jnp.arange(HEAD // 2).astype(jnp.float32) * 2.0 / HEAD)
    angles = positions.astype(jnp.float32)[..., None] * frequency
    return (jnp.cos(angles), jnp.sin(angles))


def rotate(matrix, cosine_table, sine_table):
    shaped = matrix.reshape(matrix.shape[:-1] + (-1, HEAD))
    front_half = shaped[..., : HEAD // 2]
    back_half = shaped[..., HEAD // 2 :]
    cosine = cosine_table[..., None, :]
    sine_part = sine_table[..., None, :]
    turned = jnp.concatenate(
        [front_half * cosine - back_half * sine_part, back_half * cosine + front_half * sine_part],
        axis=-1,
    )
    return turned.reshape(matrix.shape)


def normalize(token_rows, gain_row):
    inverse_rms = lax.rsqrt(jnp.mean(token_rows * token_rows, axis=-1, keepdims=True) + epsilon)
    return (token_rows * inverse_rms * gain_row, inverse_rms)


def norm_back(token_rows, inverse_rms, gain_row, grad_normed):
    weighted = grad_normed * gain_row
    inner_sum = jnp.mean(weighted * token_rows, axis=-1, keepdims=True)
    grad_rows = (
        inverse_rms * weighted - token_rows * (inverse_rms * inverse_rms * inverse_rms) * inner_sum
    )
    grad_gain = jnp.sum(grad_normed * token_rows * inverse_rms, axis=(0, 1))
    return (grad_rows, grad_gain)


def project(left, weight):
    return jnp.einsum("sbd,dh->sbh", left, weight, preferred_element_type=jnp.float32)


def project_back(grad_rows, weight):
    return jnp.einsum("sbh,dh->sbd", grad_rows, weight, preferred_element_type=jnp.float32)


def outer_sum(left, right):
    return jnp.einsum("sbd,sbh->dh", left, right, preferred_element_type=jnp.float32)


def as_heads(matrix):
    return matrix.reshape(matrix.shape[:2] + (-1, HEAD))


def split_blocks(matrix, block_width):
    block_count = matrix.shape[1] // block_width
    shaped = matrix.reshape(matrix.shape[:1] + (block_count, block_width) + matrix.shape[2:])
    return jnp.moveaxis(shaped, 1, 0)


def join_blocks(stacked):
    joined = jnp.moveaxis(stacked, 0, 1)
    return joined.reshape((joined.shape[0], joined.shape[1] * joined.shape[2]) + joined.shape[3:])


def forward_fold(query_heads, query_pos, scale_factor, fold_state, incoming):
    key_part, value_part, key_pos = incoming
    block_width = math.gcd(key_part.shape[1], 512)
    blocks = (
        split_blocks(as_heads(key_part), block_width),
        split_blocks(as_heads(value_part), block_width),
        split_blocks(key_pos, block_width),
    )

    def forward_step_block(block_state, block_in):
        key_heads, value_heads, block_pos = block_in
        allowed = block_pos[:, None, None, :] <= query_pos[:, None, :, None]
        old_max, old_total, old_accum = block_state
        scores = (
            jnp.einsum(
                "sqhe,skhe->shqk", query_heads, key_heads, preferred_element_type=jnp.float32
            )
            * scale_factor
        )
        scores = jnp.where(allowed, scores, masked_score)
        new_max = jnp.maximum(old_max, jnp.max(scores, axis=-1))
        weights = jnp.where(allowed, jnp.exp(scores - new_max[..., None]), 0.0)
        factor = jnp.exp(old_max - new_max)
        new_total = old_total * factor + jnp.sum(weights, axis=-1)
        new_accum = old_accum * factor[..., None] + jnp.einsum(
            "shqk,skhe->shqe",
            weights.astype(jnp.bfloat16),
            value_heads,
            preferred_element_type=jnp.float32,
        )
        return ((new_max, new_total, new_accum), None)

    final_state, unused = lax.scan(forward_step_block, fold_state, blocks)
    return final_state


def gradient_fold(
    query_heads, query_pos, grad_heads, log_total, delta_heads, scale_factor, fold_state, incoming
):
    key_part, value_part, key_pos = incoming
    row_count = key_part.shape[1]
    block_width = math.gcd(row_count, 512)
    blocks = (
        split_blocks(as_heads(key_part), block_width),
        split_blocks(as_heads(value_part), block_width),
        split_blocks(key_pos, block_width),
    )

    def gradient_step_block(query_state, block_in):
        key_heads, value_heads, block_pos = block_in
        allowed = block_pos[:, None, None, :] <= query_pos[:, None, :, None]
        scores = (
            jnp.einsum(
                "sqhe,skhe->shqk", query_heads, key_heads, preferred_element_type=jnp.float32
            )
            * scale_factor
        )
        weights = jnp.where(allowed, jnp.exp(scores - log_total[..., None]), 0.0)
        grad_weights = jnp.einsum(
            "sqhe,skhe->shqk", grad_heads, value_heads, preferred_element_type=jnp.float32
        )
        grad_scores = (weights * (grad_weights - delta_heads[..., None])).astype(jnp.bfloat16)
        new_query = query_state + jnp.einsum(
            "shqk,skhe->shqe", grad_scores, key_heads, preferred_element_type=jnp.float32
        )
        key_grad = jnp.einsum(
            "shqk,sqhe->skhe", grad_scores, query_heads, preferred_element_type=jnp.float32
        )
        value_grad = jnp.einsum(
            "shqk,sqhe->skhe",
            weights.astype(jnp.bfloat16),
            grad_heads,
            preferred_element_type=jnp.float32,
        )
        return (new_query, (key_grad, value_grad))

    query_state, key_total, value_total = fold_state
    query_state, outputs = lax.scan(gradient_step_block, query_state, blocks)
    key_rows = join_blocks(outputs[0])
    value_rows = join_blocks(outputs[1])
    key_total = key_rows
    value_total = value_rows
    return (query_state, key_total, value_total)


def shards(
    tokens,
    positions,
    norm_before,
    query_weight,
    key_weight,
    value_weight,
    output_weight,
    norm_middle,
    gate_weight,
    up_weight,
    down_weight,
    cotangent,
):
    sequences = tokens.shape[0]
    block_rows = tokens.shape[1]
    local_heads = query_weight.shape[1] // HEAD
    scale_factor = HEAD ** (-0.5)
    cosine_table, sine_table = rope_tables(positions)
    token_rows = tokens.astype(jnp.float32)
    gain_first = norm_before.astype(jnp.float32)
    gain_second = norm_middle.astype(jnp.float32)
    normed_first, inverse_first = normalize(token_rows, gain_first)
    normed_first = normed_first.astype(jnp.bfloat16)
    query_rot = rotate(project(normed_first, query_weight), cosine_table, sine_table).astype(
        jnp.bfloat16
    )
    key_rot = rotate(project(normed_first, key_weight), cosine_table, sine_table).astype(
        jnp.bfloat16
    )
    value_rows = project(normed_first, value_weight).astype(jnp.bfloat16)
    query_heads = as_heads(query_rot)
    head_shape = (sequences, local_heads, block_rows)
    start_state = (
        jnp.full(head_shape, masked_score, jnp.float32),
        jnp.zeros(head_shape, jnp.float32),
        jnp.zeros(head_shape + (HEAD,), jnp.float32),
    )
    row_max, row_total, accum_heads = forward_fold(
        query_heads,
        positions,
        scale_factor,
        start_state,
        (
            lax.all_gather(key_rot, "ctx", axis=1, tiled=True),
            lax.all_gather(value_rows, "ctx", axis=1, tiled=True),
            lax.all_gather(positions, "ctx", axis=1, tiled=True),
        ),
    )
    log_total = row_max + jnp.log(row_total)
    mixed_heads = jnp.swapaxes(accum_heads / row_total[..., None], 1, 2)
    mixed_rows = mixed_heads.reshape(sequences, block_rows, -1).astype(jnp.bfloat16)
    hidden = token_rows + lax.psum(
        project(mixed_rows, output_weight).astype(jnp.bfloat16), "tensor"
    ).astype(jnp.float32)
    normed_second, inverse_second = normalize(hidden, gain_second)
    normed_second = normed_second.astype(jnp.bfloat16)
    gate_rows = project(normed_second, gate_weight)
    upward = project(normed_second, up_weight)
    sigmoid_gate = jax.nn.sigmoid(gate_rows)
    silu_gate = gate_rows * sigmoid_gate
    activated = (silu_gate * upward).astype(jnp.bfloat16)
    block_output = (
        hidden
        + lax.psum(project(activated, down_weight).astype(jnp.bfloat16), "tensor").astype(
            jnp.float32
        )
    ).astype(jnp.bfloat16)
    grad_down = outer_sum(activated, cotangent)
    grad_act = project_back(cotangent, down_weight)
    grad_gate_rows = (
        grad_act * upward * sigmoid_gate * (1.0 + gate_rows * (1.0 - sigmoid_gate))
    ).astype(jnp.bfloat16)
    grad_up_rows = (grad_act * silu_gate).astype(jnp.bfloat16)
    grad_gate = outer_sum(normed_second, grad_gate_rows)
    grad_up = outer_sum(normed_second, grad_up_rows)
    second_part = project_back(grad_gate_rows, gate_weight) + project_back(grad_up_rows, up_weight)
    grad_second = lax.psum(second_part.astype(jnp.bfloat16), "tensor").astype(jnp.float32)
    hidden_back, grad_middle = norm_back(hidden, inverse_second, gain_second, grad_second)
    grad_hidden = cotangent.astype(jnp.float32) + hidden_back
    hidden_low = grad_hidden.astype(jnp.bfloat16)
    grad_output = outer_sum(mixed_rows, hidden_low)
    grad_mixed = project_back(hidden_low, output_weight).astype(jnp.bfloat16)
    grad_heads = as_heads(grad_mixed)
    delta_rows = jnp.sum(grad_heads.astype(jnp.float32) * mixed_heads, axis=-1)
    delta_heads = jnp.swapaxes(delta_rows, 1, 2)
    query_start = jnp.zeros(head_shape + (HEAD,), jnp.float32)
    whole_rows = block_rows * lax.axis_size("ctx")
    key_start = jnp.zeros((sequences, whole_rows, local_heads, HEAD), jnp.float32)
    query_sum, key_total, value_total = gradient_fold(
        query_heads,
        positions,
        grad_heads,
        log_total,
        delta_heads,
        scale_factor,
        (query_start, key_start, key_start),
        (
            lax.all_gather(key_rot, "ctx", axis=1, tiled=True),
            lax.all_gather(value_rows, "ctx", axis=1, tiled=True),
            lax.all_gather(positions, "ctx", axis=1, tiled=True),
        ),
    )
    key_sum, value_sum = (
        lax.psum_scatter(
            key_total.astype(jnp.bfloat16), "ctx", scatter_dimension=1, tiled=True
        ).astype(jnp.float32),
        lax.psum_scatter(
            value_total.astype(jnp.bfloat16), "ctx", scatter_dimension=1, tiled=True
        ).astype(jnp.float32),
    )
    query_back = rotate(
        jnp.swapaxes(query_sum, 1, 2).reshape(sequences, block_rows, -1) * scale_factor,
        cosine_table,
        -sine_table,
    ).astype(jnp.bfloat16)
    key_back = rotate(
        key_sum.reshape(sequences, block_rows, -1) * scale_factor, cosine_table, -sine_table
    ).astype(jnp.bfloat16)
    value_back = value_sum.reshape(sequences, block_rows, -1).astype(jnp.bfloat16)
    grad_query = outer_sum(normed_first, query_back)
    grad_key = outer_sum(normed_first, key_back)
    grad_value = outer_sum(normed_first, value_back)
    first_part = (
        project_back(query_back, query_weight)
        + project_back(key_back, key_weight)
        + project_back(value_back, value_weight)
    )
    grad_first = lax.psum(first_part.astype(jnp.bfloat16), "tensor").astype(jnp.float32)
    rows_back, grad_before = norm_back(token_rows, inverse_first, gain_first, grad_first)
    grad_tokens = grad_hidden + rows_back
    results = lax.psum(
        (
            grad_before,
            grad_query,
            grad_key,
            grad_value,
            grad_output,
            grad_middle,
            grad_gate,
            grad_up,
            grad_down,
        ),
        ("dp", "ctx"),
    )
    return (
        block_output,
        grad_tokens,
        results[0],
        results[1],
        results[2],
        results[3],
        results[4],
        results[5],
        results[6],
        results[7],
        results[8],
    )


f32, bf16 = jnp.float32, jnp.bfloat16


def dot(left, right, left_dim, right_dim):
    return lax.dot_general(
        left, right, (((left_dim,), (right_dim,)), ((), ())), preferred_element_type=f32
    )


def attend_kernel(block, place_ref, slot_ref, *refs):
    pieces = refs[:4]
    out_ref, attended_ref, log_ref, all_ref, key_ref, value_ref = refs[4:]
    half = pieces[0].shape[1] // 2
    length = all_ref.shape[1]
    for index, piece in enumerate(pieces):
        for side in range(2):
            columns = pl.ds(pl.multiple_of(place_ref[2 * index + side] * half, half), half)
            part = piece[:, side * half : (side + 1) * half]
            all_ref[:, columns] = part
            key_ref[columns, :] = part[HEAD : 2 * HEAD, :].astype(f32).T.astype(bf16)
            value_ref[0:HEAD, columns] = part[2 * HEAD :, :]
    value_ref[HEAD:, :] = jnp.ones((value_ref.shape[0] - HEAD, length), bf16)

    def query_step(query_index, unused):
        columns = pl.ds(pl.multiple_of(query_index * block, block), block)
        queries = all_ref[0:HEAD, columns]

        def key_step(key_index, state, diagonal=False):
            old_max, accum = state
            rows = pl.ds(pl.multiple_of(key_index * block, block), block)
            scores = dot(key_ref[rows, :], queries, 1, 0)
            if diagonal:
                key_at = lax.broadcasted_iota(jnp.int32, (block, block), 0)
                query_at = lax.broadcasted_iota(jnp.int32, (block, block), 1)
                scores = jnp.where(key_at <= query_at, scores, masked_score)
            new_max = jnp.maximum(old_max, jnp.max(scores, axis=0, keepdims=True))
            weights = jnp.exp(scores - new_max).astype(bf16)
            accum = accum * jnp.exp(old_max - new_max) + dot(value_ref[:, rows], weights, 1, 0)
            return new_max, accum

        state = (
            jnp.full((1, block), masked_score, f32),
            jnp.zeros((value_ref.shape[0], block), f32),
        )
        state = lax.fori_loop(0, query_index, key_step, state)
        row_max, accum = key_step(query_index, state, True)
        total = accum[HEAD : HEAD + 1, :]
        mixed = accum[0:HEAD, :] / total
        attended_ref[:, columns] = mixed
        log_ref[:, columns] = jnp.broadcast_to(row_max + jnp.log(total), (8, block))
        for side in range(block // half):
            slot = slot_ref[query_index * (block // half) + side]
            out_ref[slot] = mixed[:, side * half : (side + 1) * half].astype(bf16)
        return 0

    lax.fori_loop(0, length // block, query_step, 0)


def gradient_kernel(block, first, last, place_ref, send_ref, side_ref, *refs):
    pieces_ref, all_ref, attended_ref, log_ref, *refs = refs
    half = pieces_ref.shape[2]
    length = all_ref.shape[1]
    ends = last == length // block
    if first:
        query_in_ref, key_in_ref, *refs = refs
    if ends:
        cosine_ref, sine_ref, out_ref, *refs = refs
        key_ref, value_ref, grad_ref, delta_ref, query_sum_ref, key_sum_ref = refs
    else:
        query_sum_ref, key_sum_ref, key_ref, value_ref, grad_ref, delta_ref = refs
    if first:
        query_sum_ref[...] = query_in_ref[...]
        done = pl.ds(0, first * block)
        key_sum_ref[:, done] = key_in_ref[:, done]
    else:
        query_sum_ref[...] = jnp.zeros_like(query_sum_ref)
    for index in range(pieces_ref.shape[0]):
        columns = pl.ds(pl.multiple_of(place_ref[index] * half, half), half)
        grad = pieces_ref[index]
        grad_ref[:, columns] = grad
        delta = jnp.sum(grad.astype(f32) * attended_ref[:, columns], axis=0, keepdims=True)
        delta_ref[:, columns] = jnp.broadcast_to(delta, (8, half))
    for index in range(first, last):
        columns = pl.ds(index * block, block)
        key_ref[columns, :] = all_ref[HEAD : 2 * HEAD, columns].astype(f32).T.astype(bf16)
        value_ref[columns, :] = all_ref[2 * HEAD :, columns].astype(f32).T.astype(bf16)

    def key_step(key_index, unused):
        rows = pl.ds(pl.multiple_of(key_index * block, block), block)
        keys = key_ref[rows, :]
        values = value_ref[rows, :]
        keys_turned = all_ref[HEAD : 2 * HEAD, rows]

        def query_step(query_index, state, diagonal=False):
            key_sum, value_sum = state
            columns = pl.ds(pl.multiple_of(query_index * block, block), block)
            queries = all_ref[0:HEAD, columns]
            grads = grad_ref[:, columns]
            scores = dot(keys, queries, 1, 0) - log_ref[0:1, columns]
            if diagonal:
                key_at = lax.broadcasted_iota(jnp.int32, (block, block), 0)
                query_at = lax.broadcasted_iota(jnp.int32, (block, block), 1)
                scores = jnp.where(key_at <= query_at, scores, masked_score)
            weights = jnp.exp(scores)
            grad_weights = dot(values, grads, 1, 0) - delta_ref[0:1, columns]
            grad_scores = (weights * grad_weights).astype(bf16)
            value_sum = value_sum + dot(grads, weights.astype(bf16), 1, 1)
            key_sum = key_sum + dot(queries, grad_scores, 1, 1)
            query_sum_ref[:, columns] += dot(keys_turned, grad_scores, 1, 0)
            return key_sum, value_sum

        state = (jnp.zeros((HEAD, block), f32), jnp.zeros((HEAD, block), f32))
        state = query_step(key_index, state, True)
        key_sum, value_sum = lax.fori_loop(key_index + 1, length // block, query_step, state)
        key_sum_ref[0:HEAD, rows] = key_sum
        key_sum_ref[HEAD:, rows] = value_sum
        return 0

    lax.fori_loop(first, last, key_step, 0)
    if not ends:
        return

    def turn_back(rows, cosine, sine):
        front, back = rows[: HEAD // 2, :], rows[HEAD // 2 :, :]
        return jnp.concatenate([front * cosine + back * sine, back * cosine - front * sine], axis=0)

    def write_step(index, unused):
        columns = pl.ds(pl.multiple_of(index * half, half), half)
        cosine, sine = cosine_ref[:, columns], sine_ref[:, columns]
        to = send_ref[index]
        at = pl.ds(pl.multiple_of(side_ref[index] * half, half), half)
        query_rows = query_sum_ref[:, columns] * (HEAD**-0.5)
        out_ref[to, 0:HEAD, at] = turn_back(query_rows, cosine, sine).astype(bf16)
        out_ref[to, HEAD : 2 * HEAD, at] = turn_back(
            key_sum_ref[0:HEAD, columns], cosine, sine
        ).astype(bf16)
        out_ref[to, 2 * HEAD :, at] = key_sum_ref[HEAD:, columns].astype(bf16)
        return 0

    lax.fori_loop(0, length // half, write_step, 0)


def attend(place, slot, pieces):
    rows, width = pieces[0].shape
    half, length = width // 2, width * len(pieces)
    smem, vmem = pl.BlockSpec(memory_space=pltpu.SMEM), pl.BlockSpec(memory_space=pltpu.VMEM)
    return pl.pallas_call(
        functools.partial(attend_kernel, width),
        out_shape=(
            jax.ShapeDtypeStruct((2 * len(pieces), HEAD, half), bf16),
            jax.ShapeDtypeStruct((HEAD, length), f32),
            jax.ShapeDtypeStruct((8, length), f32),
            jax.ShapeDtypeStruct((rows, length), bf16),
        ),
        in_specs=[smem] * 2 + [vmem] * 4,
        out_specs=[vmem] * 4,
        scratch_shapes=[pltpu.VMEM((length, HEAD), bf16), pltpu.VMEM((HEAD + 16, length), bf16)],
        compiler_params=pltpu.CompilerParams(vmem_limit_bytes=60 << 20),
        cost_estimate=pl.CostEstimate(flops=10**6, bytes_accessed=10**4, transcendentals=0),
        name="attend",
    )(place, slot, *pieces)


def attend_back(first, last, scalars, pieces, everything, attended, log_total, *sums):
    half = pieces.shape[2]
    rows, length = everything.shape
    smem, vmem = pl.BlockSpec(memory_space=pltpu.SMEM), pl.BlockSpec(memory_space=pltpu.VMEM)
    totals = [(HEAD, length), (2 * HEAD, length)]
    scratch = [
        pltpu.VMEM((length, HEAD), bf16),
        pltpu.VMEM((length, HEAD), bf16),
        pltpu.VMEM((HEAD, length), bf16),
        pltpu.VMEM((8, length), f32),
    ]
    ends = last == length // half
    if ends:
        out_shape = jax.ShapeDtypeStruct((length // (2 * half), rows, 2 * half), bf16)
        scratch = scratch + [pltpu.VMEM(shape, f32) for shape in totals]
    else:
        out_shape = tuple(jax.ShapeDtypeStruct(shape, f32) for shape in totals)
    return pl.pallas_call(
        functools.partial(gradient_kernel, half, first, last),
        out_shape=out_shape,
        in_specs=[smem] * 3 + [vmem] * (4 + len(sums)),
        out_specs=vmem if ends else (vmem, vmem),
        scratch_shapes=scratch,
        compiler_params=pltpu.CompilerParams(vmem_limit_bytes=30 << 20),
        cost_estimate=pl.CostEstimate(flops=10**6, bytes_accessed=10**4, transcendentals=0),
        name="attend_back",
    )(*scalars, pieces, everything, attended, log_total, *sums)


SMEM, VMEM = pl.BlockSpec(memory_space=pltpu.SMEM), pl.BlockSpec(memory_space=pltpu.VMEM)


def kernel_call(kernel, name, out_shape, scalars, *arrays, scratch=(), vmem=16, micros=0):
    return pl.pallas_call(
        kernel,
        out_shape=out_shape,
        in_specs=[SMEM] * len(scalars) + [VMEM] * len(arrays),
        out_specs=jax.tree.map(lambda unused: VMEM, out_shape),
        scratch_shapes=list(scratch),
        compiler_params=pltpu.CompilerParams(vmem_limit_bytes=vmem << 20),
        cost_estimate=pl.CostEstimate(
            flops=10**6 + micros * 10**9, bytes_accessed=10**4, transcendentals=0
        ),
        name=name,
    )(*scalars, *arrays)


def rows_at(index, count):
    return pl.ds(pl.multiple_of(index * count, count), count)


def token_kernel(side_ref, mine_ref, arrived_ref, tokens_ref, gain_ref, *refs):
    low_mine, low_arrived, grad_ref = refs
    side = side_ref[0]
    half = low_mine.shape[0]
    gain = gain_ref[...].astype(f32)
    for index, low in ((side, low_mine), (1 - side, low_arrived)):
        rows = rows_at(index, half)
        grad = mine_ref[rows, :].astype(f32) + arrived_ref[rows, :].astype(f32)
        token = tokens_ref[rows, :].astype(f32)
        inverse = lax.rsqrt(jnp.mean(token * token, axis=1, keepdims=True) + epsilon)
        weighted = grad * gain
        inner = jnp.mean(weighted * token, axis=1, keepdims=True)
        grad_ref[rows, :] = low[...].astype(f32) + (
            inverse * weighted - token * (inverse * inverse * inverse) * inner
        )


def head_grad_kernel(at_ref, back_ref, weight_ref, *refs):
    *normed, keep_ref, send_ref, sum_ref = refs
    side, core, spot, size = at_ref[0], at_ref[1], at_ref[2], back_ref.shape[0]
    half = back_ref.shape[2] // 2
    total = None
    for step in range(size):
        for place, rows in ((side, normed[2 * step]), (1 - side, normed[2 * step + 1])):
            at = lax.rem(spot - step + size, size)
            term = dot(back_ref[at, :, rows_at(place, half)], rows[...], 1, 0)
            total = term if total is None else total + term
    sum_ref[...] = total.astype(bf16)
    before = jnp.zeros((1, total.shape[1]), f32)
    for which in range(3):
        weight = weight_ref[rows_at(which * size + spot, HEAD), :].astype(f32)
        grad = total[which * HEAD : (which + 1) * HEAD, :]
        before = before + jnp.sum(weight * grad, axis=0, keepdims=True)
    rows = total.shape[0] // 2
    for out, at in ((keep_ref, core), (send_ref, 1 - core)):
        out[0:rows, :] = sum_ref[rows_at(at, rows), :]
        out[rows:, :] = jnp.broadcast_to(before, (16, total.shape[1])).astype(bf16)


def first_part_kernel(back_ref, weight_ref, out_ref, rows_ref):
    size = back_ref.shape[0]
    for head in range(size):
        for which in range(3):
            at = (which * size + head) * HEAD
            rows_ref[at : at + HEAD, :] = back_ref[head, which * HEAD : (which + 1) * HEAD, :]
    block = out_ref.shape[0] // 4
    for index in range(4):
        rows = slice(index * block, (index + 1) * block)
        out_ref[rows, :] = dot(rows_ref[:, rows], weight_ref[...], 0, 0).astype(bf16)


def prepare_kernel(tokens_ref, gain_ref, cosine_ref, sine_ref, *refs):
    weights, refs = refs[:3], refs[3:]
    pieces, (normed_ref, mine_ref, other_ref, turned_ref, heads_ref) = refs[:-5], refs[-5:]
    spot, side, size = lax.axis_index("ctx"), lax.axis_index("tensor"), len(pieces)
    half = mine_ref.shape[0]
    token = tokens_ref[...].astype(f32)
    inverse = lax.rsqrt(jnp.mean(token * token, axis=1, keepdims=True) + epsilon)
    normed_ref[...] = (token * inverse * gain_ref[...].astype(f32)).astype(bf16)
    cosine, sine = cosine_ref[...], sine_ref[...]
    width = size * HEAD
    for which, weight in enumerate(weights):
        turned = weight[...].astype(f32).T.astype(bf16)
        turned_ref[which * width : (which + 1) * width, :] = turned
        product = dot(turned, normed_ref[...], 1, 1)
        for head in range(size):
            rows = product[head * HEAD : (head + 1) * HEAD, :]
            if which < 2:
                front, back = rows[: HEAD // 2, :], rows[HEAD // 2 :, :]
                rows = jnp.concatenate(
                    [front * cosine - back * sine, back * cosine + front * sine], axis=0
                )
            rows = rows.astype(bf16)
            if which == 0:
                rows = rows * bf16(HEAD**-0.5)
            heads_ref[head, which * HEAD : (which + 1) * HEAD, :] = rows
    for step, piece in enumerate(pieces):
        piece[...] = heads_ref[lax.rem(spot + step, size)]
    mine_ref[...] = normed_ref[rows_at(side, half), :]
    other_ref[...] = normed_ref[rows_at(1 - side, half), :]


def output_kernel(side_ref, mine_ref, arrived_ref, output_ref):
    half = mine_ref.shape[0]
    output_ref[rows_at(side_ref[0], half), :] = mine_ref[...]
    output_ref[rows_at(1 - side_ref[0], half), :] = arrived_ref[...]


def feed_kernel(side_ref, mixed_ref, tokens_ref, cotangent_ref, gain_ref, *refs):
    output_mine, gate_mine, up_mine, down_mine, other, *refs = refs
    grad_ref, low_ref, out_ref, normed_ref, middle_ref, *kept, output_ref = refs
    side = side_ref[0]
    half, features = normed_ref.shape
    block = 256
    size, units = output_mine.shape[0] // HEAD, gate_mine.shape[0]
    for index in range(size):
        at = index * HEAD
        output_ref[rows_at(2 * index + side, HEAD), :] = output_mine[at : at + HEAD, :]
        at = 3 * units + index * HEAD
        output_ref[rows_at(2 * index + 1 - side, HEAD), :] = other[at : at + HEAD, :]
    middle_ref[...] = jnp.zeros_like(middle_ref)
    parts = (
        (gate_mine, up_mine, down_mine, kept[:3]),
        tuple(other.at[at * units : (at + 1) * units, :] for at in range(3)) + (kept[3:],),
    )

    def step(index, unused):
        rows = rows_at(index, block)
        far = pl.ds(pl.multiple_of(side * half + index * block, block), block)
        token, cotangent = tokens_ref[far, :].astype(f32), cotangent_ref[far, :]
        hidden = token + dot(mixed_ref[:, rows], output_ref[...], 0, 0)
        inverse = lax.rsqrt(jnp.mean(hidden * hidden, axis=1, keepdims=True) + epsilon)
        gain = gain_ref[...].astype(f32)
        normed = (hidden * inverse * gain).astype(bf16)
        normed_ref[rows, :] = normed
        output_rows, grad_second = hidden, None
        for gate, up, down, (keep_gate, keep_up, keep_active) in parts:
            gate_rows = dot(normed, gate[...], 1, 1)
            upward = dot(normed, up[...], 1, 1)
            sigmoid_gate = jax.nn.sigmoid(gate_rows)
            silu_gate = gate_rows * sigmoid_gate
            activated = (silu_gate * upward).astype(bf16)
            keep_active[rows, :] = activated
            grad_act = dot(cotangent, down[...], 1, 1)
            grad_gate = (
                grad_act * upward * sigmoid_gate * (1.0 + gate_rows * (1.0 - sigmoid_gate))
            ).astype(bf16)
            keep_gate[rows, :] = grad_gate
            grad_up = (grad_act * silu_gate).astype(bf16)
            keep_up[rows, :] = grad_up
            output_rows = output_rows + dot(activated, down[...], 1, 0)
            term = dot(grad_gate, gate[...], 1, 0) + dot(grad_up, up[...], 1, 0)
            grad_second = term if grad_second is None else grad_second + term
        out_ref[rows, :] = output_rows.astype(bf16)
        weighted = grad_second * gain
        inner = jnp.mean(weighted * hidden, axis=1, keepdims=True)
        low = (
            cotangent.astype(f32)
            + (inverse * weighted - hidden * (inverse * inverse * inverse) * inner)
        ).astype(bf16)
        low_ref[rows, :] = low
        middle = jnp.sum(grad_second * hidden * inverse, axis=0, keepdims=True)
        middle_ref[...] += jnp.broadcast_to(middle, middle_ref.shape)
        grad_mixed = dot(output_ref[...], low, 1, 1).astype(bf16)
        for head in range(2 * size):
            grad_ref[head, :, rows] = grad_mixed[head * HEAD : (head + 1) * HEAD, :]
        return 0

    lax.fori_loop(0, half // block, step, 0)


def feed_grad_kernel(at_ref, mixed_ref, cotangent_ref, low_ref, normed_ref, middle_ref, *refs):
    kept, (keep_ref, send_ref, rows_ref, mixed_grad_ref) = refs[:6], refs[6:]
    core, side = at_ref[0], at_ref[1]
    half, units = kept[0].shape
    width = mixed_ref.shape[0] // 2
    size = width // HEAD
    mixed_grad_ref[...] = dot(mixed_ref[...], low_ref[...], 1, 0).astype(bf16)
    cotangent = cotangent_ref[rows_at(side, half), :]
    last = 3 * units + width
    rows_ref[last : last + 16, :] = jnp.broadcast_to(
        middle_ref[0:1, :], (16, middle_ref.shape[1])
    ).astype(bf16)
    rows_ref[last + 16 :, :] = jnp.zeros_like(rows_ref[last + 16 :, :])
    piece = keep_ref.shape[1]
    for which, of_side in ((0, side), (1, 1 - side)):
        grad_gate, grad_up, activated = kept[3 * which : 3 * which + 3]
        rows_ref[0:units, :] = dot(grad_gate[...], normed_ref[...], 0, 0).astype(bf16)
        rows_ref[units : 2 * units, :] = dot(grad_up[...], normed_ref[...], 0, 0).astype(bf16)
        rows_ref[2 * units : 3 * units, :] = dot(activated[...], cotangent, 0, 0).astype(bf16)
        for index in range(size):
            at = 3 * units + index * HEAD
            rows_ref[at : at + HEAD, :] = mixed_grad_ref[rows_at(2 * index + of_side, HEAD), :]
        keep_ref[which] = rows_ref[rows_at(core, piece), :]
        send_ref[which] = rows_ref[rows_at(1 - core, piece), :]


def add_low(left, right):
    return (left.astype(f32) + right.astype(f32)).astype(bf16)


def split_kernel(row_ref, keep_ref, arrived_ref, mine_ref, other_ref, keep_out, send_out):
    row, half, piece = row_ref[0], mine_ref.shape[0], keep_out.shape[1]
    mine_ref[...] = add_low(keep_ref[0, 0:half, :], arrived_ref[0, 0:half, :])
    other_ref[...] = add_low(keep_ref[1, 0:half, :], arrived_ref[1, 0:half, :])
    for out, at in ((keep_out, row), (send_out, 1 - row)):
        rows = pl.ds(pl.multiple_of(half + at * piece, piece), piece)
        for which in range(2):
            out[which] = add_low(keep_ref[which, rows, :], arrived_ref[which, rows, :])


def cross_kernel(row_ref, first_ref, first_in, second_ref, second_in, keep, send, mine, other):
    row, piece = row_ref[0], keep.shape[0]
    for out, at in ((keep, row), (send, 1 - row)):
        rows = rows_at(at, piece)
        out[...] = add_low(first_ref[rows, :], first_in[rows, :])
    mine[...] = add_low(second_ref[0], second_in[0])
    other[...] = add_low(second_ref[1], second_in[1])


def quarter_kernel(spot_ref, first_ref, first_in, second_ref, second_in, *outs):
    spot, size = spot_ref[0], len(outs)
    for step, out in enumerate(outs):
        rows = rows_at(lax.rem(spot + step, size), out.shape[1])
        out[0] = add_low(first_ref[rows, :], first_in[rows, :])
        out[1] = add_low(second_ref[rows, :], second_in[rows, :])


def total_kernel(*refs):
    *parts, head_ref, head_in, out_ref = refs
    total = parts[0][...].astype(f32)
    for part in parts[1:]:
        total = total + part[...].astype(f32)
    piece = total.shape[1]
    out_ref[0:piece, :] = total[0].astype(bf16)
    out_ref[piece : 2 * piece, :] = total[1].astype(bf16)
    out_ref[2 * piece :, :] = add_low(head_ref[...], head_in[...])


def head_split_kernel(row_ref, keep_ref, arrived_ref, keep_out, send_out):
    row, piece = row_ref[0], keep_out.shape[0] - 16
    for out, at in ((keep_out, row), (send_out, 1 - row)):
        rows = rows_at(at, piece)
        out[0:piece, :] = add_low(keep_ref[rows, :], arrived_ref[rows, :])
        out[piece:, :] = add_low(keep_ref[2 * piece :, :], arrived_ref[2 * piece :, :])


def finish_kernel(at_ref, *refs):
    parts, outs, (rows_ref, heads_ref) = refs[:16], refs[16:-2], refs[-2:]
    gate_ref, up_ref, down_ref, output_ref, middle_ref, *first_refs = outs
    spot, core, row = at_ref[0], at_ref[1], at_ref[2]
    size, quarter = heads_ref.shape[0], heads_ref.shape[1] // 4
    piece = (parts[0].shape[0] - quarter - 16) // 2
    for step in range(size):
        at = lax.rem(spot - step + size, size)
        for row_flip in range(2):
            for core_flip in range(2):
                part = parts[4 * step + 2 * row_flip + core_flip]
                row_at = 1 - row if row_flip else row
                core_at = 1 - core if core_flip else core
                for split in range(2):
                    place = (4 * core_at + 2 * split + row_at) * size + at
                    rows_ref[rows_at(place, piece), :] = part[split * piece : (split + 1) * piece, :]
                rows = rows_at(2 * core_at + row_at, quarter)
                heads_ref[at, rows, :] = part[2 * piece : 2 * piece + quarter, :]
    units, width = down_ref.shape[0], output_ref.shape[0]
    gate_ref[...] = rows_ref[0:units, :].astype(f32)
    up_ref[...] = rows_ref[units : 2 * units, :].astype(f32)
    down_ref[...] = rows_ref[2 * units : 3 * units, :].astype(f32)
    output_ref[...] = rows_ref[3 * units : 3 * units + width, :].astype(f32)
    last = 3 * units + width
    middle_ref[...] = rows_ref[last : last + 16, :].astype(f32)[0:1, :]
    for which in range(3):
        rows = slice(which * HEAD, (which + 1) * HEAD)
        grad = jnp.concatenate([heads_ref[head, rows, :].astype(f32) for head in range(size)], axis=0)
        first_refs[which][...] = grad.T


def swap_tensor(array):
    return lax.ppermute(array, "tensor", [(0, 1), (1, 0)])


def swap_dp(array, bit):
    return lax.ppermute(array, "dp", [(index, index ^ bit) for index in range(4)])


def shift_ctx(array, step):
    size = lax.axis_size("ctx")
    return lax.ppermute(array, "ctx", [(index, (index + step) % size) for index in range(size)])


def hold(*arrays):
    return lax.optimization_barrier(arrays)


def head_shards(
    tokens,
    positions,
    norm_before,
    query_weight,
    key_weight,
    value_weight,
    output_weight,
    norm_middle,
    gate_weight,
    up_weight,
    down_weight,
    cotangent,
):
    tokens, positions, cotangent = tokens[0], positions[0], cotangent[0]
    size, spot, side = lax.axis_size("ctx"), lax.axis_index("ctx"), lax.axis_index("tensor")
    core, row = lax.axis_index("dp") % 2, lax.axis_index("dp") // 2
    count, features = tokens.shape
    half = count // 2
    length = count * size
    width = size * HEAD
    piece = 64 * size * (-(-(3 * gate_weight.shape[1] + width + 16) // (64 * size))) // (2 * size * 4)

    def array(*shape, dtype=bf16):
        return jax.ShapeDtypeStruct(shape, dtype)

    def scalars_of(*members):
        return (jnp.stack([member.astype(jnp.int32) for member in members]),)

    gate_turned, up_turned = gate_weight.T, up_weight.T
    straight = (positions[0] == spot * count) & (positions[half] == spot * count + half)

    def place_of(index, part):
        folded = jnp.where(part == 0, index, 2 * size - 1 - index)
        return jnp.where(straight, 2 * index + part, folded).astype(jnp.int32).reshape(-1)

    places = jnp.arange(2 * size)
    owner = jnp.where(straight, places // 2, jnp.minimum(places, 2 * size - 1 - places))
    owner_half = jnp.where(straight, places % 2, (places >= size).astype(jnp.int32))
    steps = jnp.arange(size)
    place_in = place_of(((spot - steps) % size)[:, None], jnp.arange(2)[None, :])
    place_grad = place_of(steps[:, None], jnp.arange(2)[None, :])
    slot = (2 * owner + owner_half).astype(jnp.int32)

    frequency = rope_base ** (-jnp.arange(HEAD // 2).astype(f32) * 2.0 / HEAD)
    angles = frequency[:, None] * positions.astype(f32)[None, :]
    cosine, sine = jnp.cos(angles), jnp.sin(angles)
    angles_all = frequency[:, None] * jnp.arange(length).astype(f32)[None, :]
    cosine_all, sine_all = jnp.cos(angles_all), jnp.sin(angles_all)

    gain_first, gain_second = norm_before[None], norm_middle[None]
    *pieces, normed_first, my_normed, other_normed, weights_turned = kernel_call(
        prepare_kernel,
        "prepare",
        tuple(array(3 * HEAD, count) for unused in range(size))
        + (
            array(count, features),
            array(half, features),
            array(half, features),
            array(3 * width, features),
        ),
        (),
        tokens,
        gain_first,
        cosine,
        sine,
        query_weight,
        key_weight,
        value_weight,
        scratch=[pltpu.VMEM((size, 3 * HEAD, count), bf16)],
        vmem=60,
    )
    my_normed, down_late = hold(my_normed, down_weight)
    weights_other = swap_tensor(
        jnp.concatenate([gate_turned, up_turned, down_late, output_weight], axis=0)
    )
    pieces = [pieces[0]] + [shift_ctx(pieces[step], step) for step in range(1, size)]
    send_places = (owner.astype(jnp.int32), owner_half.astype(jnp.int32))
    numbers = [
        scalars_of(*members)[0]
        for members in ((side,), (row,), (spot,), (core, side), (side, core, spot), (spot, core, row))
    ]
    *pieces, my_normed, cosine_all, sine_all, place_in, slot, place_grad, gain_second = hold(
        *pieces, my_normed, cosine_all, sine_all, place_in, slot, place_grad, gain_second
    )
    numbers, send_places, my_normed = hold(numbers, send_places, my_normed)
    side_now, row_now, spot_now, core_side, side_core_spot, spot_core_row = (
        (number,) for number in numbers
    )
    mixed_out, attended, log_total, everything = attend(place_in, slot, pieces)
    mixed_out, normed_two, first_normed = hold(mixed_out, shift_ctx(my_normed, 2), my_normed)

    def exchange(parts):
        return lax.all_to_all(parts, ("ctx", "tensor"), 0, 0, tiled=True)

    mixed, normed_two, weights_other = hold(
        exchange(mixed_out).reshape(2 * width, half), normed_two, weights_other
    )
    units = gate_weight.shape[1]
    grad_mixed, hidden_low, output_half, normed_second, grad_middle, *kept = kernel_call(
        feed_kernel,
        "feed",
        (
            array(2 * size, HEAD, half),
            array(half, features),
            array(half, features),
            array(half, features),
            array(8, features, dtype=f32),
        )
        + tuple(array(half, units) for unused in range(6)),
        side_now,
        mixed,
        tokens,
        cotangent,
        gain_second,
        output_weight,
        gate_turned,
        up_turned,
        down_weight,
        weights_other,
        scratch=[pltpu.VMEM((2 * width, features), bf16)],
        vmem=36,
    )
    grad_pieces = exchange(grad_mixed)
    grad_middle, other_two = hold(grad_middle, swap_tensor(normed_two))
    rows_keep, rows_send = kernel_call(
        feed_grad_kernel,
        "feed_grad",
        (array(2, 4 * size * piece, features), array(2, 4 * size * piece, features)),
        core_side,
        mixed,
        cotangent,
        hidden_low,
        normed_second,
        grad_middle,
        *kept,
        scratch=[
            pltpu.VMEM((8 * size * piece, features), bf16),
            pltpu.VMEM((2 * width, features), bf16),
        ],
        vmem=34,
        micros=8,
    )
    scalars = (
        place_grad,
        *send_places,
    )
    rows_arrived = swap_dp(rows_send, 1)
    strip = size * piece
    first_mine, first_other, second_keep, second_send = kernel_call(
        split_kernel,
        "split",
        (
            array(2 * strip, features),
            array(2 * strip, features),
            array(2, strip, features),
            array(2, strip, features),
        ),
        row_now,
        rows_keep,
        rows_arrived,
        micros=3,
    )
    grad_pieces, first_normed, output_half = hold(grad_pieces, first_normed, output_half)
    shared = (scalars, grad_pieces, everything, attended, log_total)
    query_sum, key_sum = attend_back(0, 2, *shared)
    query_sum, key_sum, first_in, second_in, normed_one, third_normed = hold(
        query_sum,
        key_sum,
        swap_tensor(first_other),
        swap_dp(second_send, 2),
        shift_ctx(first_normed, 1),
        first_normed,
    )
    first_keep, first_send, second_mine, second_other = kernel_call(
        cross_kernel,
        "cross",
        tuple(array(strip, features) for unused in range(4)),
        row_now,
        first_mine,
        first_in,
        second_keep,
        second_in,
    )
    query_sum, key_sum, first_send, second_other, normed_one = hold(
        query_sum, key_sum, first_send, second_other, normed_one
    )
    query_sum, key_sum = attend_back(2, 4, *shared, query_sum, key_sum)
    query_sum, key_sum, first_in, second_in, normed_three, normed_one = hold(
        query_sum,
        key_sum,
        swap_dp(first_send, 2),
        swap_tensor(second_other),
        shift_ctx(third_normed, size - 1),
        normed_one,
    )
    quarters = kernel_call(
        quarter_kernel,
        "quarter",
        tuple(array(2, piece, features) for unused in range(size)),
        spot_now,
        first_keep,
        first_in,
        second_mine,
        second_in,
    )
    query_sum, key_sum, normed_one, normed_three, *quarters = hold(
        query_sum, key_sum, normed_one, normed_three, *quarters
    )
    back_out = attend_back(4, 2 * size, *shared, query_sum, key_sum, cosine_all, sine_all)
    quarters = [quarters[0]] + [shift_ctx(quarters[step], step) for step in range(1, size)]
    back_out, other_one, normed_three, *quarters = hold(
        back_out, swap_tensor(normed_one), normed_three, *quarters
    )
    other_three, hidden_low, output_half = hold(swap_tensor(normed_three), hidden_low, output_half)
    back = lax.all_to_all(back_out, "ctx", 0, 0, tiled=True)
    normed_halves = [my_normed, other_normed]
    normed_halves += [normed_one, other_one, normed_two, other_two, normed_three, other_three]
    head_keep, head_send = kernel_call(
        head_grad_kernel,
        "head_grad",
        (array(3 * HEAD // 2 + 16, features), array(3 * HEAD // 2 + 16, features)),
        side_core_spot,
        back_out,
        weights_turned,
        *normed_halves,
        scratch=[pltpu.VMEM((3 * HEAD, features), bf16)],
        vmem=60,
    )
    head_keep, head_send = kernel_call(
        head_split_kernel,
        "head_split",
        (array(3 * HEAD // 4 + 16, features), array(3 * HEAD // 4 + 16, features)),
        row_now,
        head_keep,
        swap_dp(head_send, 1),
    )
    total = kernel_call(
        total_kernel,
        "total",
        array(2 * piece + 3 * HEAD // 4 + 16, features),
        (),
        *quarters,
        head_keep,
        swap_dp(head_send, 2),
    )
    block_output = kernel_call(
        output_kernel,
        "block_output",
        array(count, features),
        side_now,
        output_half,
        swap_tensor(output_half),
    )
    back, total, low_arrived, block_output = hold(
        back, total, swap_tensor(hidden_low), block_output
    )
    first_part = kernel_call(
        first_part_kernel,
        "first_part",
        array(count, features),
        (),
        back,
        weights_turned,
        scratch=[pltpu.VMEM((3 * width, count), bf16)],
    )
    first_part, total = hold(first_part, total)
    arrivals = [total] + [shift_ctx(total, step) for step in range(1, size)]
    across = [swap_dp(arrived, 2) for arrived in arrivals]
    first_arrived, across[1] = hold(swap_tensor(first_part), across[1])
    grad_tokens = kernel_call(
        token_kernel,
        "grad_tokens",
        array(count, features, dtype=f32),
        side_now,
        first_part,
        first_arrived,
        tokens,
        gain_first,
        hidden_low,
        low_arrived,
    )

    parts = []
    for arrived, other_row in zip(arrivals, across):
        parts += [arrived, swap_dp(arrived, 1), other_row, swap_dp(other_row, 1)]
    last = 2 * piece + 3 * HEAD // 4
    before = sum(arrived[last : last + 8].astype(f32) for arrived in arrivals)
    grad_tokens, before = hold(grad_tokens, before)
    grad_before = (before[0] + swap_tensor(before)[0]) / norm_before.astype(f32)
    (
        grad_gate,
        grad_up,
        grad_down,
        grad_output,
        grad_middle,
        grad_query,
        grad_key,
        grad_value,
    ) = kernel_call(
        finish_kernel,
        "finish",
        (
            array(units, features, dtype=f32),
            array(units, features, dtype=f32),
            array(units, features, dtype=f32),
            array(width, features, dtype=f32),
            array(1, features, dtype=f32),
        )
        + tuple(array(features, width, dtype=f32) for unused in range(3)),
        spot_core_row,
        *parts,
        scratch=[
            pltpu.VMEM((8 * strip, features), bf16),
            pltpu.VMEM((size, 3 * HEAD, features), bf16),
        ],
        vmem=30,
    )
    grad_middle = grad_middle.reshape(features)
    grad_gate, grad_up = grad_gate.T, grad_up.T
    return (
        block_output[None],
        grad_tokens[None],
        grad_before,
        grad_query,
        grad_key,
        grad_value,
        grad_output,
        grad_middle,
        grad_gate,
        grad_up,
        grad_down,
    )


def solution(mesh):
    sizes = dict(mesh.shape)

    def body(*arguments):
        local_heads = arguments[3].shape[1] // HEAD
        one_head = sizes["ctx"] == local_heads and sizes["tensor"] == 2 and sizes["dp"] == 4
        one_sequence = arguments[0].shape[0] == 1
        return (head_shards if one_head and one_sequence else shards)(*arguments)

    return jax.shard_map(
        body,
        mesh=mesh,
        in_specs=(
            P("dp", "ctx", None),
            P("dp", "ctx"),
            P(),
            P(None, "tensor"),
            P(None, "tensor"),
            P(None, "tensor"),
            P("tensor", None),
            P(),
            P(None, "tensor"),
            P(None, "tensor"),
            P("tensor", None),
            P("dp", "ctx", None),
        ),
        out_specs=(
            P("dp", "ctx", None),
            P("dp", "ctx", None),
            P(),
            P(None, "tensor"),
            P(None, "tensor"),
            P(None, "tensor"),
            P("tensor", None),
            P(),
            P(None, "tensor"),
            P(None, "tensor"),
            P("tensor", None),
        ),
        check_vma=False,
    )
```
